512 devices in a mesh: ctx: 32 (over y, z_hi), head: 16 (over x, z_lo, core).
Axes of the slice: x: 4, y: 8, z: 8 (z_hi: 4, z_lo: 2; z = z_hi * 2 + z_lo), core: 2. Of those that a mesh axis runs over, the one named last changes fastest.
Arguments:
- x_in: bfloat16 [8192, 4096], P(('ctx', 'head')), may hold values from -6 to 6
- b_in: bfloat16 [8192, 1024], P(('ctx', 'head')), may hold values from -6 to 6
- c_in: bfloat16 [8192, 1024], P(('ctx', 'head')), may hold values from -6 to 6
- dt_in: bfloat16 [8192, 64], P(('ctx', 'head')), may hold values from -2.5 to 2.5
- gate_in: bfloat16 [8192, 4096], P(('ctx', 'head')), may hold values from -6 to 6
- out_grad: bfloat16 [8192, 4096], P(('ctx', 'head')), may hold values from -6 to 6
- conv_x: float32 [4, 4096], P(None, 'head'), may hold values from -3 to 3
- conv_b: float32 [4, 1024], replicated, may hold values from -3 to 3
- conv_c: float32 [4, 1024], replicated, may hold values from -3 to 3
- a_log: float32 [64], P('head'), may hold values from -12 to -3
- dt_bias: float32 [64], P('head'), may hold values from -0.5 to 0.5
- d_skip: float32 [64], P('head'), may hold values from 0.5 to 1.5
- norm_gain: float32 [4096], replicated, may hold values from 0.5 to 1.5
Outputs:
- x_grad: bfloat16 [8192, 4096], P(('ctx', 'head'))
- b_grad: bfloat16 [8192, 1024], P(('ctx', 'head'))
- c_grad: bfloat16 [8192, 1024], P(('ctx', 'head'))
- dt_grad: bfloat16 [8192, 64], P(('ctx', 'head'))
- gate_grad: bfloat16 [8192, 4096], P(('ctx', 'head'))
- conv_x_grad: float32 [4, 4096], P(None, 'head')
- conv_b_grad: float32 [4, 1024], replicated
- conv_c_grad: float32 [4, 1024], replicated
- a_log_grad: float32 [64], P('head')
- dt_bias_grad: float32 [64], P('head')
- d_skip_grad: float32 [64], P('head')
- gain_grad: float32 [4096], replicated
The draws below stay inside these ranges and needn't reach their ends.
All inputs are finite; a program needn't handle non-finite values.
Results may differ from the reference program's by a relative error of at most 0.015.
The reference program's roundings to bfloat16 on the way count: a program that leaves them out, or rounds other values in their place, can miss the bound.
Values may be sent and summed in bfloat16 or wider, within the bound.
No kernel may reach another device: no remote copies, remote signals or barrier semaphores. Data moves between devices by JAX's collectives and lax.ppermute only.
A program may use at most 64 MiB of HBM per device.

```python
import jax
import jax.numpy as jnp
import numpy as np
from jax import lax

H = 64
P_SIZE = 64
N = 128
G = 8
K = 4
CH = 256
SPANS_DEV = 1
D = 4096
TOKENS = 8192
N_HEAD = 16


def draw_dt_in(key, part):
    key = jax.random.fold_in(key, 11)
    key_offset, key_noise = jax.random.split(key)
    block_count = TOKENS // (SPANS_DEV * CH)
    offsets = jax.random.uniform(key_offset, (block_count, 1, H), jnp.float32, -1.0, 1.0)
    noise = jnp.clip(0.8 * jax.random.normal(key_noise, (block_count, SPANS_DEV * CH, H), jnp.float32), -1.5, 1.5)
    return (offsets + noise).reshape(TOKENS, H).astype(jnp.bfloat16)


def draw_a_log(key, part):
    key = jax.random.fold_in(key, 5)
    key_pick, key_fast, key_slow = jax.random.split(key, 3)
    fast_share = 0.5
    chosen = jax.random.uniform(key_pick, (H,), jnp.float32) < fast_share
    fast_rate = jax.random.uniform(key_fast, (H,), jnp.float32, jnp.log(1.0 / 50.0), jnp.log(1.0 / 25.0))
    slow_rate = jax.random.uniform(key_slow, (H,), jnp.float32, jnp.log(0.1), jnp.log(0.7)) - jnp.log(1.0 * TOKENS)
    slow_rate = jnp.maximum(slow_rate, -12.0)
    return jnp.where(chosen, fast_rate, slow_rate).astype(jnp.float32)


def steps_of(own_key, dims, cuts, low, high):
    level, own = 1.0, jax.random.fold_in(own_key, 6)
    for axis_at, shards_of in cuts:
        steps = jnp.exp(jax.random.uniform(jax.random.fold_in(own, axis_at), (shards_of,), jnp.float32, low / len(cuts), high / len(cuts)))
        level = level * jnp.repeat(steps, dims[axis_at] // shards_of).reshape([-1 if axis == axis_at else 1 for axis in range(len(dims))])
    return level


def centred(stream_key, extent, spread, reach, cuts=(), held_as=jnp.bfloat16):
    level = steps_of(stream_key, extent, cuts, -0.22, 0.18) if cuts else 1.0
    result = jax.random.normal(stream_key, extent, jnp.float32) * spread * level
    return jnp.minimum(jnp.maximum(result, -reach), reach).astype(held_as)


def setup_inputs(seed: int = 0) -> dict:
    streams_of = jax.random.split(jax.random.key(seed), 14)
    return {
        "x_in": centred(streams_of[0], (TOKENS, D), 1.0, 6.0, ((0, 512),)),
        "b_in": centred(streams_of[1], (TOKENS, G * N), 1.0, 6.0, ((0, 512),)),
        "c_in": centred(streams_of[2], (TOKENS, G * N), 1.0, 6.0, ((0, 512),)),
        "dt_in": draw_dt_in(jax.random.fold_in(streams_of[13], 71), 0),
        "gate_in": centred(streams_of[4], (TOKENS, D), 1.0, 6.0, ((0, 512),)),
        "out_grad": centred(streams_of[5], (TOKENS, D), 1.0, 6.0, ((0, 512),)),
        "conv_x": centred(streams_of[6], (K, D), 0.5, 3.0, ((1, 16),), jnp.float32),
        "conv_b": centred(streams_of[7], (K, G * N), 0.5, 3.0, (), jnp.float32),
        "conv_c": centred(streams_of[8], (K, G * N), 0.5, 3.0, (), jnp.float32),
        "a_log": draw_a_log(jax.random.fold_in(streams_of[13], 71), 0),
        "dt_bias": jnp.clip(jax.random.uniform(streams_of[10], (H,), jnp.float32, -0.5, 0.5) * steps_of(streams_of[10], (H,), ((0, 16),), -0.4, 0.0), -0.5, 0.5),
        "d_skip": jnp.clip(0.5 + 1.0 * jax.random.uniform(streams_of[11], (H,), jnp.float32) ** steps_of(streams_of[11], (H,), ((0, 16),), -0.2, 0.2), 0.5, 1.5),
        "norm_gain": jnp.clip(1.0 + 0.1 * jax.random.normal(streams_of[12], (D,), jnp.float32), 0.5, 1.5),
    }


PRECISE = lax.Precision.HIGHEST

def causal_taps(padded, weight):
    row_count = padded.shape[0] - weight.shape[0] + 1
    summed = weight[0] * padded[0:row_count]
    for tap_index in range(1, weight.shape[0]):
        summed = summed + weight[tap_index] * padded[tap_index:tap_index + row_count]
    return summed

def conv_silu(source, weight):
    padded = jnp.concatenate([jnp.zeros((weight.shape[0] - 1, source.shape[1]), jnp.float32), source], axis=0)
    return jax.nn.silu(causal_taps(padded, weight))

def stored(array_in):
    return lax.optimization_barrier(array_in.astype(jnp.bfloat16)).astype(jnp.float32)

def rates_of(dt_raw, dt_bias, a_log):
    stepsize = jax.nn.softplus(dt_raw + dt_bias)
    return (stepsize, -jnp.exp(a_log) * stepsize)

def span_math(carried, pieces):
    x_rows, b_rows, c_rows, log_rows, step_rows = pieces
    cumlog = jnp.cumsum(log_rows, axis=0)
    block_len = log_rows.shape[0]
    causal = (jnp.arange(block_len)[:, None] >= jnp.arange(block_len)[None, :])[None]
    log_gap = cumlog.T[:, :, None] - cumlog.T[:, None, :]
    decays = jnp.where(causal, jnp.exp(jnp.where(causal, log_gap, 0.0)), 0.0)
    scores = jnp.einsum('ten,sen->ets', c_rows, b_rows, precision=PRECISE)
    weights = scores * decays * step_rows.T[:, None, :]
    inside = jnp.einsum('ets,sep->tep', weights, x_rows, precision=PRECISE)
    from_state = jnp.einsum('ten,epn->tep', c_rows, carried, precision=PRECISE) * jnp.exp(cumlog)[:, :, None]
    final_log = cumlog[-1]
    to_end = jnp.exp(final_log[None, :] - cumlog) * step_rows
    fresh_state = jnp.einsum('sep,sen->epn', x_rows * to_end[:, :, None], b_rows, precision=PRECISE)
    carried = jnp.exp(final_log)[:, None, None] * carried + fresh_state
    return (carried, inside + from_state)

def gated_norm(mixed_in, gate_vec, gain_vec):
    gated = mixed_in * jax.nn.silu(gate_vec)
    grouped = gated.reshape(gated.shape[0], G, -1)
    inv_rms = lax.rsqrt(lax.optimization_barrier(jnp.mean(grouped * grouped, axis=-1, keepdims=True)) + 1e-05)
    return (grouped * inv_rms).reshape(gated.shape) * gain_vec

def reference(x_in, b_in, c_in, dt_in, gate_in, out_grad, conv_x, conv_b, conv_c, a_log, dt_bias, d_skip, norm_gain):
    heads_dev = H // N_HEAD
    per_group = H // G
    groups_dev = max(1, heads_dev * G // H)
    n_blocks = N_HEAD * groups_dev
    group_pick = np.array([block_at * heads_dev // per_group + inner_at for block_at in range(N_HEAD) for inner_at in range(groups_dev)], dtype=np.int32)
    head_pick = np.array([head_id // heads_dev * groups_dev + head_id % heads_dev // per_group for head_id in range(H)], dtype=np.int32)

    def copies(source):
        return source.astype(jnp.float32).reshape(TOKENS, G, N)[:, group_pick, :].reshape(TOKENS, n_blocks * N)

    def conv_part(x_rows, b_rows, c_rows, w_x, w_b, w_c):
        pick_b = w_b.reshape(K, G, N)[:, group_pick, :].reshape(K, n_blocks * N)
        pick_c = w_c.reshape(K, G, N)[:, group_pick, :].reshape(K, n_blocks * N)
        return (conv_silu(x_rows, w_x), conv_silu(b_rows, pick_b), conv_silu(c_rows, pick_c))
    (x_conv, b_conv, c_conv), conv_back = jax.vjp(conv_part, x_in.astype(jnp.float32), copies(b_in), copies(c_in), conv_x, conv_b, conv_c)
    x_heads = stored(x_conv).reshape(TOKENS, H, P_SIZE)
    b_blocks = stored(b_conv).reshape(TOKENS, n_blocks, N)
    c_blocks = stored(c_conv).reshape(TOKENS, n_blocks, N)

    def ssd_part(x_heads, b_blocks, c_blocks, dt_raw, dt_bias, a_log, d_skip):
        stepsize, logdecay = rates_of(dt_raw, dt_bias, a_log)
        n_spans = TOKENS // CH

        def advance(carried, pieces):
            x_rows, b_blk, c_blk, log_rows, step_rows = pieces
            return span_math(carried, (x_rows, b_blk[:, head_pick, :], c_blk[:, head_pick, :], log_rows, step_rows))

        def split_rows(array_in):
            return array_in.reshape((n_spans, CH) + array_in.shape[1:])
        zero_state = jnp.zeros((H, P_SIZE, N), jnp.float32)
        _, outputs = lax.scan(jax.checkpoint(advance), zero_state, (split_rows(x_heads), split_rows(b_blocks), split_rows(c_blocks), split_rows(logdecay), split_rows(stepsize)))
        return outputs.reshape(x_heads.shape) + d_skip[:, None] * x_heads
    mixed_out, ssd_back = jax.vjp(ssd_part, x_heads, b_blocks, c_blocks, dt_in.astype(jnp.float32), dt_bias, a_log, d_skip)
    mixed_out = mixed_out.reshape(TOKENS, D).astype(jnp.bfloat16)
    _, norm_back = jax.vjp(gated_norm, mixed_out.astype(jnp.float32), gate_in.astype(jnp.float32), norm_gain)
    y_grad, gate_grad, gain_grad = norm_back(out_grad.astype(jnp.float32))
    dx_heads, db_blocks, dc_blocks, dt_grad, dt_bias_grad, a_log_grad, d_skip_grad = ssd_back(stored(y_grad).reshape(TOKENS, H, P_SIZE))
    dx_rows, db_rows, dc_rows, conv_x_grad, conv_b_grad, conv_c_grad = conv_back((dx_heads.reshape(TOKENS, D), db_blocks.reshape(TOKENS, n_blocks * N), dc_blocks.reshape(TOKENS, n_blocks * N)))

    def regroup(partial_value):
        rounded = stored(partial_value).reshape(TOKENS, n_blocks, N)
        summed = jnp.zeros((TOKENS, G, N), jnp.float32).at[:, group_pick, :].add(rounded)
        return summed.reshape(TOKENS, G * N).astype(jnp.bfloat16)
    return (dx_rows.astype(jnp.bfloat16), regroup(db_rows), regroup(dc_rows), dt_grad.astype(jnp.bfloat16), gate_grad.astype(jnp.bfloat16), conv_x_grad, conv_b_grad, conv_c_grad, a_log_grad, dt_bias_grad, d_skip_grad, gain_grad)
```

```python
import functools

import jax
import jax.numpy as jnp
from jax import lax
from jax.experimental import pallas as pl
from jax.experimental.pallas import tpu as pltpu
from jax.sharding import PartitionSpec as P

BF, F32 = jnp.bfloat16, jnp.float32
GROUPS = 8
N = 128
PS = 64
HD = 4
CW = 256
T = 256
KT = 4
ROWS = 16
IN_W = 1152
OUT_W = 896
VMEM_LIMIT = 48 * 1024 * 1024


def dot(a, b, ca, cb):
    return lax.dot_general(
        a, b, (((ca,), (cb,)), ((), ())), preferred_element_type=F32
    )


def pieces(a, count):
    out = []
    for _ in range(count - 1):
        head = a.astype(BF)
        out.append(head)
        a = a - head.astype(F32)
    return out + [a.astype(BF)]


def dot_parts(a, b, ca, cb, count):
    total = None
    for piece in pieces(a, count):
        term = dot(piece, b, ca, cb)
        total = term if total is None else total + term
    return total


def dot_right(a, b, ca, cb):
    high, low = pieces(b, 2)
    return dot(a, high, ca, cb) + dot(a, low, ca, cb)


def dot_both(a, b, ca, cb):
    a_high, a_low = pieces(a, 2)
    b_high, b_low = pieces(b, 2)
    return dot(a_high, b_high, ca, cb) + (dot(a_high, b_low, ca, cb) + dot(a_low, b_high, ca, cb))


def iota(shape, axis):
    return lax.broadcasted_iota(jnp.int32, shape, axis)


def spread(cols):
    low = iota((cols.shape[0], 128), 1) < PS
    halves = []
    for pair in range(HD // 2):
        first = jnp.broadcast_to(cols[:, 2 * pair : 2 * pair + 1], (cols.shape[0], 128))
        second = jnp.broadcast_to(cols[:, 2 * pair + 1 : 2 * pair + 2], (cols.shape[0], 128))
        halves.append(jnp.where(low, first, second))
    return jnp.concatenate(halves, axis=1)


def head_sums(wide):
    pick = (iota((CW, 128), 0) // PS == iota((CW, 128), 1)).astype(BF)
    return dot_parts(wide, pick, 1, 0, 3)


def scalar_row(ref, width, per):
    lane = iota((1, width), 1) // per
    row = jnp.zeros((1, width), F32)
    for e in range(HD):
        row = jnp.where(lane == e, ref[e], row)
    return row


def softplus(v):
    return jnp.maximum(v, 0.0) + jnp.log1p(jnp.exp(-jnp.abs(v)))


def rates(dt_cols, bias_row, alog_row):
    live = iota((T, 128), 1) < HD
    shifted = dt_cols + bias_row
    step = jnp.where(live, softplus(shifted), 0.0)
    logd = -jnp.exp(alog_row) * step
    tril = (iota((T, T), 0) >= iota((T, T), 1)).astype(BF)
    cum = sum(dot(tril, piece, 1, 0) for piece in pieces(logd, 3))
    return shifted, step, logd, cum


def taps(ext_ref, weight, lo, hi):
    total = None
    for k in range(KT):
        term = weight[k : k + 1, :] * ext_ref[ROWS - KT + 1 + k : ROWS - KT + 1 + k + T, lo:hi]
        total = term if total is None else total + term
    return total


def gap_decay(cum, cum_t, e):
    causal = iota((T, T), 0) >= iota((T, T), 1)
    gap = jnp.where(causal, cum[:, e : e + 1] - cum_t[e : e + 1, :], 0.0)
    return jnp.where(causal, jnp.exp(gap), 0.0)


def silu_slope(pre):
    gate = jax.nn.sigmoid(pre)
    return pre * gate, gate * (1.0 + pre * (1.0 - gate))


def three_rows(row, count):
    at = iota((count, row.shape[1]), 0)
    high, middle, low = pieces(row, 3)
    return jnp.where(
        at == 0,
        high.astype(F32),
        jnp.where(at == 1, middle.astype(F32), jnp.where(at == 2, low.astype(F32), 0.0)),
    ).astype(BF)


def enter_math(ext, dt_cols, wx, wb, wc, bias_row, alog_row):
    def act(weight, lo, hi):
        pre = taps(ext, weight, lo, hi)
        return (pre * jax.nn.sigmoid(pre)).astype(BF)

    x_act, b_act, c_act = act(wx, 0, 256), act(wb, 256, 384), act(wc, 384, 512)
    shifted, step, logd, cum = rates(dt_cols, bias_row, alog_row)
    final = cum[T - 1 : T, :]
    to_end = jnp.exp(final - cum) * step
    weighted = x_act.astype(F32) * spread(to_end)
    fresh = dot_parts(weighted, b_act, 0, 0, 2)
    return x_act, b_act, c_act, step, cum, fresh, final


def within_math(x_act, b_act, c_act, step, cum, cum_t):
    scores = dot(c_act, b_act, 1, 1)
    stepped = x_act.astype(F32) * spread(step)
    outs, kept = [], []
    for e in range(HD):
        mix = (scores * gap_decay(cum, cum_t, e)).astype(BF)
        kept.append(mix)
        part = stepped[:, e * PS : (e + 1) * PS]
        high, low = pieces(part, 2)
        both = dot(mix, jnp.concatenate([high, low], axis=1), 1, 0)
        outs.append(both[:, :PS] + both[:, PS:])
    return jnp.concatenate(outs, axis=1), kept


def mix_math(x_act, c_act, inside, carried, cum, skip_row, gate, out_grad, gain):
    grown = spread(jnp.exp(cum))
    y = inside + grown * dot_right(c_act, carried, 1, 1)
    mixed = (y + skip_row * x_act.astype(F32)).astype(BF)
    gate_act = gate * jax.nn.sigmoid(gate)
    v = mixed.astype(F32) * gate_act
    squares = jnp.sum(v * v, axis=1, keepdims=True)
    along = jnp.sum(out_grad * gain * v, axis=1, keepdims=True)
    return y, mixed, squares, along


def norm_math(mixed, gate, out_grad, gain, squares, along, c_act, cum):
    gate_act, gate_slope = silu_slope(gate)
    mixed = mixed.astype(F32)
    v = mixed * gate_act
    inv = lax.rsqrt(squares * (1.0 / (2 * CW)) + 1e-05)
    normed = v * inv
    v_grad = inv * (out_grad * gain - normed * (along * inv * (1.0 / (2 * CW))))
    y_grad = (v_grad * gate_act).astype(BF)
    gate_grad = (v_grad * mixed * gate_slope).astype(BF)
    gain_grad = jnp.sum(out_grad * normed, axis=0, keepdims=True)
    grown = spread(jnp.exp(cum))
    lifted = y_grad.astype(F32) * grown
    start_grad = dot_parts(lifted, c_act, 0, 0, 2)
    return y_grad, gate_grad, gain_grad, lifted, start_grad


def within_back_math(x_act, b_act, c_act, step, cum, cum_t, kept, y, y_grad, lifted, carried):
    score_grad = jnp.zeros((T, T), F32)
    x_parts = []
    step_t = step.T
    for e in range(HD):
        cut = slice(e * PS, (e + 1) * PS)
        x_parts.append(dot(kept[e], y_grad[:, cut], 0, 0))
        mix_grad = dot(y_grad[:, cut], x_act[:, cut], 1, 1)
        score_grad = score_grad + mix_grad * (gap_decay(cum, cum_t, e) * step_t[e : e + 1, :])
    x_in = jnp.concatenate(x_parts, axis=1)
    score_grad = score_grad.astype(BF)
    c_grad = dot(score_grad, b_act, 1, 0) + dot_both(lifted, carried, 1, 0)
    b_in = dot(score_grad, c_act, 0, 0)
    dy = y_grad.astype(F32)
    x32 = x_act.astype(F32)
    out_dots = head_sums(dy * y)
    in_dots = head_sums(x32 * x_in)
    skip_grad = jnp.sum(dy * x32, axis=0, keepdims=True)
    return x_in, b_in, c_grad, out_dots, in_dots, skip_grad


def leave_math(x_act, b_act, step, cum, shifted, logd, alog_row, skip_row, y_grad, x_in, b_in, out_dots, in_dots, carried, end_grad):
    final = cum[T - 1 : T, :]
    tail = jnp.exp(final - cum)
    x32 = x_act.astype(F32)
    end_b = end_grad.astype(BF)
    x_state = spread(tail) * dot(b_act, end_b, 1, 1)
    state_dots = head_sums(x32 * x_state)
    wide_step = spread(step)
    x_grad = wide_step * (x_in + x_state) + skip_row * y_grad.astype(F32)
    weighted = (x32 * spread(tail * step)).astype(BF)
    b_grad = b_in + dot(weighted, end_b, 1, 0)
    pull = step * state_dots
    cum_grad = out_dots - step * in_dots - pull
    kept_dots = jnp.sum(carried * end_grad, axis=1, keepdims=True)
    lane = iota((1, 128), 1)
    over = jnp.zeros((1, 128), F32)
    for e in range(HD):
        over = jnp.where(lane == e, jnp.sum(kept_dots[e * PS : (e + 1) * PS, :], axis=0, keepdims=True), over)
    final_grad = jnp.sum(pull, axis=0, keepdims=True) + jnp.exp(final) * over
    triu = (iota((T, T), 0) <= iota((T, T), 1)).astype(BF)
    log_grad = sum(dot(triu, piece, 1, 0) for piece in pieces(cum_grad, 3)) + final_grad
    step_grad = in_dots + state_dots - jnp.exp(alog_row) * log_grad
    alog_grad = jnp.sum(log_grad * logd, axis=0, keepdims=True)
    live = iota((T, 128), 1) < HD
    dt_grad = jnp.where(live, step_grad * jax.nn.sigmoid(shifted), 0.0)
    bias_grad = jnp.sum(dt_grad, axis=0, keepdims=True)
    return x_grad, b_grad, dt_grad, alog_grad, bias_grad


def conv_slopes(ext, wx, wb, wc):
    def slope(weight, lo, hi):
        return silu_slope(taps(ext, weight, lo, hi))[1]

    return jnp.concatenate([slope(wx, 0, 256), slope(wb, 256, 384), slope(wc, 384, 512)], axis=1)


def weight_grads(ext, pre_grad):
    return [
        jnp.sum(pre_grad * ext[ROWS - KT + 1 + k : ROWS - KT + 1 + k + T], axis=0, keepdims=True)
        for k in range(KT)
    ]


def conv_back(pre_ext, weight, lo, hi):
    total = None
    for k in range(KT):
        term = weight[k : k + 1, :] * pre_ext[KT - 1 - k : KT - 1 - k + T, lo:hi]
        total = term if total is None else total + term
    return total


ZW = 4
PACK = T + 8


def call(kernel, out_shape, in_specs, out_specs=None, scratch=(), flops=0, bytes_accessed=0):
    vmem = pl.BlockSpec(memory_space=pltpu.VMEM)
    smem = pl.BlockSpec(memory_space=pltpu.SMEM)
    place = {"v": vmem, "s": smem}
    return pl.pallas_call(
        kernel,
        out_shape=out_shape,
        in_specs=[place[c] for c in in_specs],
        out_specs=[place[c] for c in (out_specs or "v" * len(out_shape))],
        scratch_shapes=list(scratch),
        compiler_params=pltpu.CompilerParams(vmem_limit_bytes=VMEM_LIMIT),
        cost_estimate=pl.CostEstimate(
            flops=flops, bytes_accessed=bytes_accessed, transcendentals=0
        ),
    )


def sds(shape, dtype):
    return jax.ShapeDtypeStruct(shape, dtype)


def pack_kernel(x, b, c, dt, gate, out_grad, out):
    ways = out.shape[0]
    per = GROUPS * N // ways
    wide_dt = jnp.concatenate(
        [dt[...].astype(F32), jnp.zeros((ROWS, 128 - dt.shape[1]), F32)], axis=1
    )
    lane = iota((ROWS, 128), 1)
    for j in range(ways):
        g = (j * per) // N
        own = slice(j * CW, (j + 1) * CW)
        shared = slice(g * N, (g + 1) * N)
        out[j, :, 0:256] = x[:, own]
        out[j, :, 256:384] = b[:, shared]
        out[j, :, 384:512] = c[:, shared]
        out[j, :, 512:768] = gate[:, own]
        out[j, :, 768:1024] = out_grad[:, own]
        turned = pltpu.roll(wide_dt, (128 - HD * j) % 128, 1)
        out[j, :, 1024:1152] = jnp.where(lane < HD, turned, 0.0).astype(BF)


def group_lanes(ref, where):
    return ref[:, pl.ds(pl.multiple_of(where[1] * N, N), N)]


def final_rows(final):
    return jnp.broadcast_to(final, (8, 128))


def enter_kernel(rows, halo, wx, wb, wc, alog, bias, where, xbc, step_out, cum_out, send, ext):
    ext[0:ROWS] = halo[...].astype(F32)
    ext[ROWS : ROWS + T] = rows[:, 0:512].astype(F32)
    x_act, b_act, c_act, step, cum, fresh, final = enter_math(
        ext,
        rows[:, 1024:1152].astype(F32),
        wx[...],
        group_lanes(wb, where),
        group_lanes(wc, where),
        scalar_row(bias, 128, 1),
        scalar_row(alog, 128, 1),
    )
    xbc[:, 0:256] = x_act
    xbc[:, 256:384] = b_act
    xbc[:, 384:512] = c_act
    step_out[...] = step
    cum_out[...] = cum
    tail = final_rows(final)
    for i in range(send.shape[0]):
        send[i, 0:T] = fresh
        send[i, T:PACK] = tail


def within_kernel(xbc, step, cum, inside, kept):
    step, cum = step[...], cum[...]
    out, mixes = within_math(xbc[:, 0:256], xbc[:, 256:384], xbc[:, 384:512], step, cum, cum.T)
    inside[...] = out
    for e in range(HD):
        kept[e] = mixes[e]


def head_column(row):
    return jnp.concatenate(
        [jnp.broadcast_to(row[:, e : e + 1], (PS, 1)) for e in range(HD)], axis=0
    )


def chain(received, count, backward, mine):
    state = jnp.zeros((T, 128), F32)
    total = jnp.zeros((1, 128), F32)
    kept_state, kept_total = state, total
    for i in range(count):
        at = count - 1 - i if backward else i
        here = mine == at
        kept_state = jnp.where(here, state, kept_state)
        kept_total = jnp.where(here, total, kept_total)
        log = received[at, T : T + 1, :]
        state = head_column(jnp.exp(log)) * state + received[at, 0:T, :]
        total = total + log
    return kept_state, kept_total, state, total


def near_kernel(backward, received, where, send, near):
    kept_state, kept_total, state, total = chain(received, received.shape[0], backward, where[2])
    near[0:T] = kept_state
    near[T:PACK] = final_rows(kept_total)
    tail = final_rows(total)
    for i in range(send.shape[0]):
        send[i, 0:T] = state
        send[i, T:PACK] = tail


def far_state(backward, received, near, mine):
    count = received.shape[0]
    state = jnp.zeros((T, 128), F32)
    for i in range(count):
        at = count - 1 - i if backward else i
        log = received[at, T : T + 1, :]
        longer = head_column(jnp.exp(log)) * state + received[at, 0:T, :]
        use = (at > mine) if backward else (at < mine)
        state = jnp.where(use, longer, state)
    return head_column(jnp.exp(near[T : T + 1, :])) * state + near[0:T, :]


def pair_rows(squares, along):
    lane = iota((T, 128), 1)
    both = jnp.where(lane == 0, squares, jnp.where(lane == 1, along, 0.0))
    return both.T[0:8, :]


def gain_lanes(ref, where):
    return ref[:, pl.ds(pl.multiple_of(where[0] * CW, CW), CW)]


def mix_kernel(received, near, xbc, inside, cum, rows, gain, skip, where, y_out, mixed_out, carried_out, message):
    carried = far_state(False, received, near, where[3])
    y, mixed, squares, along = mix_math(
        xbc[:, 0:256],
        xbc[:, 384:512],
        inside[...],
        carried,
        cum[...],
        scalar_row(skip, CW, PS),
        rows[:, 512:768].astype(F32),
        rows[:, 768:1024].astype(F32),
        gain_lanes(gain, where),
    )
    y_out[...] = y
    mixed_out[...] = mixed
    carried_out[...] = carried
    message[...] = pair_rows(squares, along)


def norm_kernel(message, mixed, rows, gain, xbc, cum, where, y_grad_out, gate_out, gain_out, lifted_out, send):
    cum = cum[...]
    sums = jnp.concatenate([message[...], jnp.zeros((120, T), F32)], axis=0).T
    y_grad, gate_grad, gain_grad, lifted, start_grad = norm_math(
        mixed[...],
        rows[:, 512:768].astype(F32),
        rows[:, 768:1024].astype(F32),
        gain_lanes(gain, where),
        sums[:, 0:1],
        sums[:, 1:2],
        xbc[:, 384:512],
        cum,
    )
    y_grad_out[...] = y_grad
    gate_out[...] = gate_grad
    gain_out[...] = jnp.broadcast_to(gain_grad, (8, CW))
    lifted_out[...] = lifted
    tail = final_rows(cum[T - 1 : T, :])
    for i in range(send.shape[0]):
        send[i, 0:T] = start_grad
        send[i, T:PACK] = tail


def back_kernel(
    rows, halo, wx, wb, wc, where, xbc, step, cum, kept, y, y_grad, lifted, carried,
    x_in_out, b_in_out, c_grad_out, out_dots_out, in_dots_out, skip_out, slopes_out, ext,
):
    ext[0:ROWS] = halo[...].astype(F32)
    ext[ROWS : ROWS + T] = rows[:, 0:512].astype(F32)
    slopes_out[...] = conv_slopes(
        ext, wx[...], group_lanes(wb, where), group_lanes(wc, where)
    )
    cum = cum[...]
    x_in, b_in, c_grad, out_dots, in_dots, skip_grad = within_back_math(
        xbc[:, 0:256],
        xbc[:, 256:384],
        xbc[:, 384:512],
        step[...],
        cum,
        cum.T,
        [kept[e] for e in range(HD)],
        y[...],
        y_grad[...],
        lifted[...],
        carried[...],
    )
    x_in_out[...] = x_in
    b_in_out[...] = b_in
    c_grad_out[...] = c_grad
    out_dots_out[...] = out_dots
    in_dots_out[...] = in_dots
    skip_out[...] = jnp.broadcast_to(skip_grad, (8, CW))


def leave_kernel(
    received, near, rows, halo, where, alog, bias, skip, xbc, step, cum, y_grad, x_in, b_in,
    c_grad, out_dots, in_dots, carried, gain_grad, skip_grad, slopes,
    pre_out, dt_out, send, ext,
):
    ext[0:ROWS] = halo[...].astype(F32)
    ext[ROWS : ROWS + T] = rows[:, 0:512].astype(F32)
    end_grad = far_state(True, received, near, where[3])
    alog_row = scalar_row(alog, 128, 1)
    step = step[...]
    x_grad, b_grad, dt_grad, alog_grad, bias_grad = leave_math(
        xbc[:, 0:256],
        xbc[:, 256:384],
        step,
        cum[...],
        rows[:, 1024:1152].astype(F32) + scalar_row(bias, 128, 1),
        -jnp.exp(alog_row) * step,
        alog_row,
        scalar_row(skip, CW, PS),
        y_grad[...],
        x_in[...],
        b_in[...],
        out_dots[...],
        in_dots[...],
        carried[...],
        end_grad,
    )
    dt_out[...] = dt_grad
    pre = jnp.concatenate([x_grad, b_grad, c_grad[...]], axis=1) * slopes[...]
    pre_out[...] = pre
    weights = weight_grads(ext, pre)
    block = jnp.concatenate(
        weights
        + [
            jnp.concatenate([gain_grad[0:1, :], skip_grad[0:1, :]], axis=1),
            jnp.concatenate([alog_grad, bias_grad, jnp.zeros((1, 256), F32)], axis=1),
            jnp.zeros((2, 512), F32),
            pre[0:8, :],
        ],
        axis=0,
    )
    for i in range(send.shape[0]):
        send[i] = block


def near_sum_kernel(received, where, send, halo):
    ways = received.shape[0]
    mine = where[2]
    total = received[0, 0:8, :]
    for i in range(1, ways):
        total = total + received[i, 0:8, :]
    following = jnp.zeros((8, 512), F32)
    for i in range(1, ways):
        following = jnp.where(mine == i - 1, received[i, 8:16, :], following)
    halo[...] = following
    first = received[0, 8:16, :]
    for i in range(send.shape[0]):
        send[i, 0:8] = total
        send[i, 8:16] = first


def finish_kernel(received, near_halo, where, wx, wb, wc, pre, dt_grad, gate_grad, send, conv_x_out, alog_out, bias_out, skip_out, ext):
    ways = received.shape[0]
    total = received[0, 0:8, :]
    for i in range(1, ways):
        total = total + received[i, 0:8, :]
    following = jnp.zeros((8, 512), F32)
    for i in range(1, ways):
        following = jnp.where(where[3] == i - 1, received[i, 8:16, :], following)
    following = jnp.where(where[2] == ZW - 1, following, near_halo[...])
    ext[0:T] = pre[...]
    ext[T : T + 8] = following
    x_grad = conv_back(ext, wx[...], 0, 256).astype(BF)
    b_grad = conv_back(ext, group_lanes(wb, where), 256, 384).astype(BF)
    c_grad = conv_back(ext, group_lanes(wc, where), 384, 512).astype(BF)
    conv_x_out[...] = total[0:KT, 0:CW]
    for e in range(HD):
        alog_out[e] = jnp.sum(total[5:6, e : e + 1])
        bias_out[e] = jnp.sum(total[5:6, 128 + e : 129 + e])
        skip_out[e] = jnp.sum(total[4:5, CW + e * PS : CW + (e + 1) * PS])
    shared = jnp.concatenate([total[0:5, 256:512], jnp.zeros((11, 256), F32)], axis=0)
    shared = jnp.where(iota((16, 256), 0) == 4, jnp.broadcast_to(total[4:5, 0:256], (16, 256)), shared)
    high, middle, low = pieces(shared, 3)
    dt_low = dt_grad[...].astype(BF)
    for j in range(send.shape[0]):
        cut = slice(j * ROWS, (j + 1) * ROWS)
        send[j, :, 0:256] = x_grad[cut]
        send[j, :, 256:384] = b_grad[cut]
        send[j, :, 384:512] = c_grad[cut]
        send[j, :, 512:768] = gate_grad[cut, :]
        send[j, :, 768:896] = dt_low[cut]
        send[j, :, 896:1152] = high
        send[j, :, 1152:1408] = middle
        send[j, :, 1408:1664] = low


def unpack_kernel(received, x_out, b_out, c_out, dt_out, gate_out, conv_b_out, conv_c_out, gain_out):
    ways = received.shape[0]
    lane = iota((ROWS, 128), 1)
    dt = jnp.zeros((ROWS, 128), F32)
    shared = []
    for j in range(ways):
        own = slice(j * CW, (j + 1) * CW)
        x_out[:, own] = received[j, :, 0:256]
        gate_out[:, own] = received[j, :, 512:768]
        turned = pltpu.roll(received[j, :, 768:896].astype(F32), HD * j, 1)
        dt = jnp.where(lane // HD == j, turned, dt)
        shared.append(
            received[j, :, 896:1152].astype(F32)
            + received[j, :, 1152:1408].astype(F32)
            + received[j, :, 1408:1664].astype(F32)
        )
        gain_out[:, own] = shared[j][4:5, :]
    dt_out[...] = dt[:, 0 : dt_out.shape[1]].astype(BF)
    per = ways // GROUPS
    for g in range(GROUPS):
        cut = slice(g * N, (g + 1) * N)
        b_sum, c_sum, w_sum = 0.0, 0.0, 0.0
        for j in range(g * per, (g + 1) * per):
            b_sum = b_sum + received[j, :, 256:384].astype(F32)
            c_sum = c_sum + received[j, :, 384:512].astype(F32)
            w_sum = w_sum + shared[j]
        b_out[:, cut] = b_sum.astype(BF)
        c_out[:, cut] = c_sum.astype(BF)
        conv_b_out[:, cut] = w_sum[0:KT, 0:128]
        conv_c_out[:, cut] = w_sum[0:KT, 128:256]


def per_device(
    x_in, b_in, c_in, dt_in, gate_in, out_grad, conv_x, conv_b, conv_c, a_log, dt_bias, d_skip, norm_gain
):
    ways = lax.axis_size("head")
    blocks = lax.axis_size("ctx")
    far = blocks // ZW
    near_groups = [[y * ZW + z for z in range(ZW)] for y in range(far)]
    far_groups = [[y * ZW + z for y in range(far)] for z in range(ZW)]
    head_at, ctx_at = lax.axis_index("head"), lax.axis_index("ctx")
    where = jnp.stack(
        [head_at, head_at * GROUPS // ways, ctx_at % ZW, ctx_at // ZW]
    ).astype(jnp.int32)
    gain = norm_gain.reshape(1, -1)

    def near_swap(value):
        return lax.all_to_all(value, "ctx", 0, 0, axis_index_groups=near_groups)

    def far_swap(value):
        return lax.all_to_all(value, "ctx", 0, 0, axis_index_groups=far_groups)

    def head_swap(value):
        return lax.all_to_all(value, "head", 0, 0, tiled=True)

    sent = call(pack_kernel, [sds((ways, ROWS, IN_W), BF)], "vvvvvv")(
        x_in, b_in, c_in, dt_in, gate_in, out_grad
    )[0]
    arrived = head_swap(sent)
    rows = arrived.reshape(T, IN_W)
    halo = lax.ppermute(
        arrived[ways - 1, :, 0:512], "ctx", [(i, i + 1) for i in range(blocks - 1)]
    )
    wide = sds((T, CW), F32)
    slim = sds((T, 128), F32)
    message = sds((ZW, PACK, 128), F32)
    far_message = sds((far, PACK, 128), F32)
    near_part = sds((PACK, 128), F32)
    ext = pltpu.VMEM((ROWS + T, 512), F32)

    xbc, step, cum, send = call(
        enter_kernel, [sds((T, 512), BF), slim, slim, message], "vvvvvsss", scratch=[ext]
    )(rows, halo, conv_x, conv_b, conv_c, a_log, dt_bias, where)
    received = near_swap(send)
    inside, kept = call(
        within_kernel, [wide, sds((HD, T, T), BF)], "vvv", flops=10**8, bytes_accessed=2 * 10**6
    )(xbc, step, cum)
    send, near = call(functools.partial(near_kernel, False), [far_message, near_part], "vs")(
        received, where
    )
    received = far_swap(send)
    y, mixed, carried, sums = call(
        mix_kernel,
        [wide, sds((T, CW), BF), slim, sds((8, T), F32)],
        "vvvvvvvss",
    )(received, near, xbc, inside, cum, rows, gain, d_skip, where)
    per = ways // GROUPS
    sums = lax.psum(
        sums, "head", axis_index_groups=[[g * per + i for i in range(per)] for g in range(GROUPS)]
    )
    y_grad, gate_grad, gain_grad, lifted, send = call(
        norm_kernel,
        [sds((T, CW), BF), sds((T, CW), BF), sds((8, CW), F32), wide, message],
        "vvvvvvs",
    )(sums, mixed, rows, gain, xbc, cum, where)
    received = near_swap(send)
    x_part, b_part, c_grad, out_dots, in_dots, skip_grad, slopes = call(
        back_kernel,
        [wide, slim, slim, slim, slim, sds((8, CW), F32), sds((T, 512), F32)],
        "vvvvvsvvvvvvvv",
        scratch=[ext],
        flops=3 * 10**8,
        bytes_accessed=4 * 10**6,
    )(rows, halo, conv_x, conv_b, conv_c, where, xbc, step, cum, kept, y, y_grad, lifted, carried)
    send, near = call(functools.partial(near_kernel, True), [far_message, near_part], "vs")(
        received, where
    )
    received = far_swap(send)
    pre, dt_grad, send = call(
        leave_kernel,
        [sds((T, 512), F32), slim, sds((ZW, 16, 512), F32)],
        "vvvvssss" + "v" * 13,
        scratch=[ext],
    )(
        received, near, rows, halo, where, a_log, dt_bias, d_skip, xbc, step, cum, y_grad, x_part,
        b_part, c_grad, out_dots, in_dots, carried, gain_grad, skip_grad, slopes,
    )
    received = near_swap(send)
    send, near_halo = call(
        near_sum_kernel, [sds((far, 16, 512), F32), sds((8, 512), F32)], "vs"
    )(received, where)
    received = far_swap(send)
    four = sds((HD,), F32)
    send, conv_x_grad, alog_grad, bias_grad, skip_sum = call(
        finish_kernel,
        [sds((ways, ROWS, 1664), BF), sds((KT, CW), F32), four, four, four],
        "vvsvvvvvv",
        "vvsss",
        scratch=[pltpu.VMEM((T + 8, 512), F32)],
    )(received, near_halo, where, conv_x, conv_b, conv_c, pre, dt_grad, gate_grad)
    received = head_swap(send)
    heads = dt_in.shape[1]
    x_grad, b_grad, c_grad, dt_out, gate_out, conv_b_grad, conv_c_grad, gain_sum = call(
        unpack_kernel,
        [
            sds(x_in.shape, BF),
            sds(b_in.shape, BF),
            sds(c_in.shape, BF),
            sds((ROWS, heads), BF),
            sds(gate_in.shape, BF),
            sds(conv_b.shape, F32),
            sds(conv_c.shape, F32),
            sds((1, norm_gain.shape[0]), F32),
        ],
        "v",
    )(received)
    return (
        x_grad,
        b_grad,
        c_grad,
        dt_out,
        gate_out,
        conv_x_grad,
        conv_b_grad,
        conv_c_grad,
        alog_grad,
        bias_grad,
        skip_sum,
        gain_sum.reshape(-1),
    )


def solution(mesh):
    tokens = P(("ctx", "head"), None)
    return jax.shard_map(
        per_device,
        mesh=mesh,
        in_specs=(tokens,) * 6 + (P(None, "head"), P(), P(), P("head"), P("head"), P("head"), P()),
        out_specs=(tokens,) * 5
        + (P(None, "head"), P(), P(), P("head"), P("head"), P("head"), P()),
        check_vma=False,
    )
```

```python
import functools

import jax
import jax.numpy as jnp
from jax import lax
from jax.experimental import pallas as pl
from jax.experimental.pallas import tpu as pltpu
from jax.sharding import PartitionSpec as P

BF, F32 = jnp.bfloat16, jnp.float32
GROUPS = 8
N = 128
PS = 64
HD = 4
CW = 256
T = 256
KT = 4
ROWS = 16
IN_W = 1152
OUT_W = 1152
VMEM_LIMIT = 16 * 1024 * 1024


def dot(a, b, ca, cb):
    return lax.dot_general(
        a, b, (((ca,), (cb,)), ((), ())), preferred_element_type=F32
    )


def pieces(a, count):
    out = []
    for _ in range(count - 1):
        head = a.astype(BF)
        out.append(head)
        a = a - head.astype(F32)
    return out + [a.astype(BF)]


def dot_parts(a, b, ca, cb, count):
    total = None
    for piece in pieces(a, count):
        term = dot(piece, b, ca, cb)
        total = term if total is None else total + term
    return total


def dot_right(a, b, ca, cb):
    high, low = pieces(b, 2)
    return dot(a, high, ca, cb) + dot(a, low, ca, cb)


def dot_both(a, b, ca, cb):
    a_high, a_low = pieces(a, 2)
    b_high, b_low = pieces(b, 2)
    return dot(a_high, b_high, ca, cb) + (dot(a_high, b_low, ca, cb) + dot(a_low, b_high, ca, cb))


def iota(shape, axis):
    return lax.broadcasted_iota(jnp.int32, shape, axis)


def spread(cols):
    low = iota((cols.shape[0], 128), 1) < PS
    halves = []
    for pair in range(HD // 2):
        first = jnp.broadcast_to(cols[:, 2 * pair : 2 * pair + 1], (cols.shape[0], 128))
        second = jnp.broadcast_to(cols[:, 2 * pair + 1 : 2 * pair + 2], (cols.shape[0], 128))
        halves.append(jnp.where(low, first, second))
    return jnp.concatenate(halves, axis=1)


def head_sums(wide):
    pick = (iota((CW, 128), 0) // PS == iota((CW, 128), 1)).astype(BF)
    return dot_parts(wide, pick, 1, 0, 3)


def scalar_row(ref, first, width, per):
    lane = iota((1, width), 1) // per
    row = jnp.zeros((1, width), F32)
    for e in range(HD):
        row = jnp.where(lane == e, ref[first + e], row)
    return row


def softplus(v):
    return jnp.maximum(v, 0.0) + jnp.log1p(jnp.exp(-jnp.abs(v)))


def rates(dt_cols, bias_row, alog_row):
    live = iota((T, 128), 1) < HD
    shifted = dt_cols + bias_row
    step = jnp.where(live, softplus(shifted), 0.0)
    logd = -jnp.exp(alog_row) * step
    tril = (iota((T, T), 0) >= iota((T, T), 1)).astype(BF)
    cum = sum(dot(tril, piece, 1, 0) for piece in pieces(logd, 3))
    return shifted, step, logd, cum


def taps(ext_ref, weight, lo, hi):
    total = None
    for k in range(KT):
        term = weight[k : k + 1, :] * ext_ref[ROWS - KT + 1 + k : ROWS - KT + 1 + k + T, lo:hi]
        total = term if total is None else total + term
    return total


def gap_decay(cum, cum_t, e):
    causal = iota((T, T), 0) >= iota((T, T), 1)
    gap = jnp.where(causal, cum[:, e : e + 1] - cum_t[e : e + 1, :], 0.0)
    return jnp.where(causal, jnp.exp(gap), 0.0)


def silu_slope(pre):
    gate = jax.nn.sigmoid(pre)
    return pre * gate, gate * (1.0 + pre * (1.0 - gate))


def three_rows(row, count):
    at = iota((count, row.shape[1]), 0)
    high, middle, low = pieces(row, 3)
    return jnp.where(
        at == 0,
        high.astype(F32),
        jnp.where(at == 1, middle.astype(F32), jnp.where(at == 2, low.astype(F32), 0.0)),
    ).astype(BF)


def enter_math(ext, dt_cols, wx, wb, wc, bias_row, alog_row):
    def act(weight, lo, hi):
        pre = taps(ext, weight, lo, hi)
        return (pre * jax.nn.sigmoid(pre)).astype(BF)

    x_act, b_act, c_act = act(wx, 0, 256), act(wb, 256, 384), act(wc, 384, 512)
    shifted, step, logd, cum = rates(dt_cols, bias_row, alog_row)
    final = cum[T - 1 : T, :]
    to_end = jnp.exp(final - cum) * step
    weighted = x_act.astype(F32) * spread(to_end)
    fresh = dot_parts(weighted, b_act, 0, 0, 2)
    return x_act, b_act, c_act, step, cum, fresh, final


def within_math(x_act, b_act, c_act, step, cum, cum_t):
    scores = dot(c_act, b_act, 1, 1)
    stepped = x_act.astype(F32) * spread(step)
    outs, kept = [], []
    for e in range(HD):
        mix = (scores * gap_decay(cum, cum_t, e)).astype(BF)
        kept.append(mix)
        part = stepped[:, e * PS : (e + 1) * PS]
        high, low = pieces(part, 2)
        both = dot(mix, jnp.concatenate([high, low], axis=1), 1, 0)
        outs.append(both[:, :PS] + both[:, PS:])
    return jnp.concatenate(outs, axis=1), kept


def mix_math(x_act, c_act, inside, carried, cum, skip_row, gate, out_grad, gain):
    grown = spread(jnp.exp(cum))
    y = inside + grown * dot_right(c_act, carried, 1, 1)
    mixed = (y + skip_row * x_act.astype(F32)).astype(BF)
    gate_act = gate * jax.nn.sigmoid(gate)
    v = mixed.astype(F32) * gate_act
    squares = jnp.sum(v * v, axis=1, keepdims=True)
    along = jnp.sum(out_grad * gain * v, axis=1, keepdims=True)
    return y, mixed, squares, along


def norm_math(mixed, gate, out_grad, gain, squares, along, c_act, cum):
    gate_act, gate_slope = silu_slope(gate)
    mixed = mixed.astype(F32)
    v = mixed * gate_act
    inv = lax.rsqrt(squares * (1.0 / (2 * CW)) + 1e-05)
    normed = v * inv
    v_grad = inv * (out_grad * gain - normed * (along * inv * (1.0 / (2 * CW))))
    y_grad = (v_grad * gate_act).astype(BF)
    gate_grad = (v_grad * mixed * gate_slope).astype(BF)
    gain_grad = jnp.sum(out_grad * normed, axis=0, keepdims=True)
    grown = spread(jnp.exp(cum))
    lifted = y_grad.astype(F32) * grown
    start_grad = dot_parts(lifted, c_act, 0, 0, 2)
    return y_grad, gate_grad, gain_grad, lifted, start_grad


def within_back_math(x_act, b_act, c_act, step, cum, cum_t, kept, y, y_grad, lifted, carried):
    score_grad = jnp.zeros((T, T), F32)
    x_parts = []
    step_t = step.T
    for e in range(HD):
        cut = slice(e * PS, (e + 1) * PS)
        x_parts.append(dot(kept[e], y_grad[:, cut], 0, 0))
        mix_grad = dot(y_grad[:, cut], x_act[:, cut], 1, 1)
        score_grad = score_grad + mix_grad * (gap_decay(cum, cum_t, e) * step_t[e : e + 1, :])
    x_in = jnp.concatenate(x_parts, axis=1)
    score_grad = score_grad.astype(BF)
    c_grad = dot(score_grad, b_act, 1, 0) + dot_both(lifted, carried, 1, 0)
    b_in = dot(score_grad, c_act, 0, 0)
    dy = y_grad.astype(F32)
    x32 = x_act.astype(F32)
    out_dots = head_sums(dy * y)
    in_dots = head_sums(x32 * x_in)
    skip_grad = jnp.sum(dy * x32, axis=0, keepdims=True)
    return x_in, b_in, c_grad, out_dots, in_dots, skip_grad


def leave_math(x_act, b_act, step, cum, shifted, logd, alog_row, skip_row, y_grad, x_in, b_in, out_dots, in_dots, carried, end_grad):
    final = cum[T - 1 : T, :]
    tail = jnp.exp(final - cum)
    x32 = x_act.astype(F32)
    end_b = end_grad.astype(BF)
    x_state = spread(tail) * dot(b_act, end_b, 1, 1)
    state_dots = head_sums(x32 * x_state)
    wide_step = spread(step)
    x_grad = wide_step * (x_in + x_state) + skip_row * y_grad.astype(F32)
    weighted = (x32 * spread(tail * step)).astype(BF)
    b_grad = b_in + dot(weighted, end_b, 1, 0)
    pull = step * state_dots
    cum_grad = out_dots - step * in_dots - pull
    kept_dots = jnp.sum(carried * end_grad, axis=1, keepdims=True)
    lane = iota((1, 128), 1)
    over = jnp.zeros((1, 128), F32)
    for e in range(HD):
        over = jnp.where(lane == e, jnp.sum(kept_dots[e * PS : (e + 1) * PS, :], axis=0, keepdims=True), over)
    final_grad = jnp.sum(pull, axis=0, keepdims=True) + jnp.exp(final) * over
    triu = (iota((T, T), 0) <= iota((T, T), 1)).astype(BF)
    log_grad = sum(dot(triu, piece, 1, 0) for piece in pieces(cum_grad, 3)) + final_grad
    step_grad = in_dots + state_dots - jnp.exp(alog_row) * log_grad
    alog_grad = jnp.sum(log_grad * logd, axis=0, keepdims=True)
    live = iota((T, 128), 1) < HD
    dt_grad = jnp.where(live, step_grad * jax.nn.sigmoid(shifted), 0.0)
    bias_grad = jnp.sum(dt_grad, axis=0, keepdims=True)
    return x_grad, b_grad, dt_grad, alog_grad, bias_grad


def conv_slopes(ext, wx, wb, wc):
    def slope(weight, lo, hi):
        return silu_slope(taps(ext, weight, lo, hi))[1]

    return jnp.concatenate([slope(wx, 0, 256), slope(wb, 256, 384), slope(wc, 384, 512)], axis=1)


def weight_grads(ext, pre_grad):
    return [
        jnp.sum(pre_grad * ext[ROWS - KT + 1 + k : ROWS - KT + 1 + k + T], axis=0, keepdims=True)
        for k in range(KT)
    ]


def conv_back(pre_ext, weight, lo, hi):
    total = None
    for k in range(KT):
        term = weight[k : k + 1, :] * pre_ext[KT - 1 - k : KT - 1 - k + T, lo:hi]
        total = term if total is None else total + term
    return total


def call(kernel, out_shape, in_specs, out_specs=None, scratch=(), flops=0, bytes_accessed=0):
    place = {
        "v": pl.BlockSpec(memory_space=pltpu.VMEM),
        "s": pl.BlockSpec(memory_space=pltpu.SMEM),
        "h": pl.BlockSpec(memory_space=pltpu.HBM),
    }
    return pl.pallas_call(
        kernel,
        out_shape=out_shape,
        in_specs=[place[c] for c in in_specs],
        out_specs=[place[c] for c in (out_specs or "v" * len(out_shape))],
        scratch_shapes=list(scratch),
        compiler_params=pltpu.CompilerParams(vmem_limit_bytes=VMEM_LIMIT),
        cost_estimate=pl.CostEstimate(
            flops=flops, bytes_accessed=bytes_accessed, transcendentals=0
        ),
    )


def sds(shape, dtype):
    return jax.ShapeDtypeStruct(shape, dtype)


def pack_kernel(x_at, b_at, c_at, dt_at, gate_at, grad_at, out, x, b, c, dt, gate, out_grad, sems):
    moves = [
        pltpu.make_async_copy(source, target, sems.at[i])
        for i, (source, target) in enumerate(
            [(x_at, x), (b_at, b), (c_at, c), (dt_at, dt), (gate_at, gate), (grad_at, out_grad)]
        )
    ]
    for move in moves:
        move.start()
    for move in moves:
        move.wait()
    ways = out.shape[0]
    per = GROUPS * N // ways
    wide_dt = jnp.concatenate(
        [dt[...].astype(F32), jnp.zeros((ROWS, 128 - dt.shape[1]), F32)], axis=1
    )
    lane = iota((ROWS, 128), 1)
    for j in range(ways):
        g = (j * per) // N
        own = slice(j * CW, (j + 1) * CW)
        shared = slice(g * N, (g + 1) * N)
        out[j, :, 0:256] = x[:, own]
        out[j, :, 256:384] = b[:, shared]
        out[j, :, 384:512] = c[:, shared]
        out[j, :, 512:768] = gate[:, own]
        out[j, :, 768:1024] = out_grad[:, own]
        turned = pltpu.roll(wide_dt, (128 - HD * j) % 128, 1)
        out[j, :, 1024:1152] = jnp.where(lane < HD, turned, 0.0).astype(BF)


def group_lanes(ref, where):
    return ref[:, pl.ds(pl.multiple_of(where[1] * N, N), N)]


def gain_lanes(ref, where):
    return ref[:, pl.ds(pl.multiple_of(where[0] * CW, CW), CW)]


def head_column(row):
    return jnp.concatenate(
        [jnp.broadcast_to(row[:, e : e + 1], (PS, 128)) for e in range(HD)], axis=0
    )


def enter_kernel(rows, halo, wx, wb, wc, head, where, xbc, step_out, cum_out, send, ext):
    ext[0:ROWS] = halo[...].astype(F32)
    ext[ROWS : ROWS + T] = rows[:, 0:512].astype(F32)
    x_act, b_act, c_act, step, cum, fresh, final = enter_math(
        ext,
        rows[:, 1024:1152].astype(F32),
        wx[...],
        group_lanes(wb, where),
        group_lanes(wc, where),
        scalar_row(head, HD, 128, 1),
        scalar_row(head, 0, 128, 1),
    )
    xbc[:, 0:256] = x_act
    xbc[:, 256:384] = b_act
    xbc[:, 384:512] = c_act
    step_out[...] = step
    cum_out[...] = cum
    pieces_of = send.shape[0]
    send[:, 0:8] = fresh.reshape(pieces_of, 8, 128)
    send[:, 8:16] = head_column(final).reshape(pieces_of, 8, 128)


def within_kernel(xbc, step, cum, inside, kept):
    step, cum = step[...], cum[...]
    out, mixes = within_math(xbc[:, 0:256], xbc[:, 256:384], xbc[:, 384:512], step, cum, cum.T)
    inside[...] = out
    for e in range(HD):
        kept[e] = mixes[e]


def scan_kernel(received, send, decays):
    state = jnp.zeros((8, 128), F32)
    for i in range(received.shape[0]):
        send[i] = state
        decay = jnp.exp(received[i, 8:16])
        decays[i] = decay
        state = decay * state + received[i, 0:8]


def scan_back_kernel(received, decays, send):
    state = jnp.zeros((8, 128), F32)
    for i in reversed(range(received.shape[0])):
        send[i] = state
        state = decays[i] * state + received[i]


def pair_rows(squares, along):
    lane = iota((T, 128), 1)
    both = jnp.where(lane == 0, squares, jnp.where(lane == 1, along, 0.0))
    return both.T[0:8, :]


def mix_kernel(carried, xbc, inside, cum, rows, gain, head, where, y_out, mixed_out, message):
    y, mixed, squares, along = mix_math(
        xbc[:, 0:256],
        xbc[:, 384:512],
        inside[...],
        carried[...],
        cum[...],
        scalar_row(head, 2 * HD, CW, PS),
        rows[:, 512:768].astype(F32),
        rows[:, 768:1024].astype(F32),
        gain_lanes(gain, where),
    )
    y_out[...] = y
    mixed_out[...] = mixed
    message[...] = pair_rows(squares, along)


def norm_kernel(message, mixed, rows, gain, xbc, cum, where, y_grad_out, gate_out, gain_out, lifted_out, send):
    sums = jnp.concatenate([message[...], jnp.zeros((120, T), F32)], axis=0).T
    y_grad, gate_grad, gain_grad, lifted, start_grad = norm_math(
        mixed[...],
        rows[:, 512:768].astype(F32),
        rows[:, 768:1024].astype(F32),
        gain_lanes(gain, where),
        sums[:, 0:1],
        sums[:, 1:2],
        xbc[:, 384:512],
        cum[...],
    )
    y_grad_out[...] = y_grad
    gate_out[...] = gate_grad
    gain_out[...] = jnp.broadcast_to(gain_grad, (8, CW))
    lifted_out[...] = lifted
    send[...] = start_grad.reshape(send.shape)


def back_kernel(
    rows, halo, wx, wb, wc, where, xbc, step, cum, kept, y, y_grad, lifted, carried,
    x_in_out, b_in_out, c_grad_out, out_dots_out, in_dots_out, skip_out, slopes_out, ext,
):
    ext[0:ROWS] = halo[...].astype(F32)
    ext[ROWS : ROWS + T] = rows[:, 0:512].astype(F32)
    slopes_out[...] = conv_slopes(
        ext, wx[...], group_lanes(wb, where), group_lanes(wc, where)
    )
    cum = cum[...]
    x_in, b_in, c_grad, out_dots, in_dots, skip_grad = within_back_math(
        xbc[:, 0:256],
        xbc[:, 256:384],
        xbc[:, 384:512],
        step[...],
        cum,
        cum.T,
        [kept[e] for e in range(HD)],
        y[...],
        y_grad[...],
        lifted[...],
        carried[...],
    )
    x_in_out[...] = x_in
    b_in_out[...] = b_in
    c_grad_out[...] = c_grad
    out_dots_out[...] = out_dots
    in_dots_out[...] = in_dots
    skip_out[...] = jnp.broadcast_to(skip_grad, (8, CW))


def leave_kernel(
    end_grad, rows, halo, head, xbc, step, cum, y_grad, x_in, b_in, c_grad, out_dots, in_dots,
    carried, gain_grad, skip_grad, slopes, pre_out, dt_out, rim, send, ext,
):
    ext[0:ROWS] = halo[...].astype(F32)
    ext[ROWS : ROWS + T] = rows[:, 0:512].astype(F32)
    alog_row = scalar_row(head, 0, 128, 1)
    step = step[...]
    x_grad, b_grad, dt_grad, alog_grad, bias_grad = leave_math(
        xbc[:, 0:256],
        xbc[:, 256:384],
        step,
        cum[...],
        rows[:, 1024:1152].astype(F32) + scalar_row(head, HD, 128, 1),
        -jnp.exp(alog_row) * step,
        alog_row,
        scalar_row(head, 2 * HD, CW, PS),
        y_grad[...],
        x_in[...],
        b_in[...],
        out_dots[...],
        in_dots[...],
        carried[...],
        end_grad[...],
    )
    dt_out[...] = dt_grad
    pre = jnp.concatenate([x_grad, b_grad, c_grad[...]], axis=1) * slopes[...]
    pre_out[...] = pre
    rim[...] = pre[0:8]
    weights = jnp.concatenate(weight_grads(ext, pre), axis=0)
    block = jnp.concatenate(
        [weights[:, i * 128 : (i + 1) * 128] for i in range(4)]
        + [gain_grad[0:1, 0:128], gain_grad[0:1, 128:256]]
        + [skip_grad[0:1, 0:128], skip_grad[0:1, 128:256]]
        + [alog_grad, bias_grad, jnp.zeros((2, 128), F32)],
        axis=0,
    )
    for i in range(send.shape[0]):
        send[i] = block


def finish_kernel(received, following, where, wx, wb, wc, pre, dt_grad, gate_grad, send, conv_x_out, alog_out, bias_out, skip_out, ext):
    total = received[0]
    for i in range(1, received.shape[0]):
        total = total + received[i]
    ext[0:T] = pre[...]
    ext[T : T + 8] = following[...]
    x_grad = conv_back(ext, wx[...], 0, 256).astype(BF)
    b_grad = conv_back(ext, group_lanes(wb, where), 256, 384).astype(BF)
    c_grad = conv_back(ext, group_lanes(wc, where), 384, 512).astype(BF)
    conv_x_out[...] = jnp.concatenate([total[0:4], total[4:8]], axis=1)
    for e in range(HD):
        at = 18 + e // 2
        cut = slice((e % 2) * PS, (e % 2 + 1) * PS)
        alog_out[e] = jnp.sum(total[20:21, e : e + 1])
        bias_out[e] = jnp.sum(total[21:22, e : e + 1])
        skip_out[e] = jnp.sum(total[at : at + 1, cut])
    shared = jnp.concatenate(
        [
            jnp.concatenate([total[8:12], total[12:16]], axis=1),
            jnp.concatenate([total[16:17], total[17:18]], axis=1),
        ],
        axis=0,
    )
    high = shared.astype(BF).astype(F32)
    middle = (shared - high).astype(BF).astype(F32)
    low = shared - high - middle
    shared = jnp.concatenate([high, middle, low, jnp.zeros((1, 256), F32)], axis=0).astype(BF)
    dt_low = dt_grad[...].astype(BF)
    for j in range(send.shape[0]):
        cut = slice(j * ROWS, (j + 1) * ROWS)
        send[j, :, 0:256] = x_grad[cut]
        send[j, :, 256:384] = b_grad[cut]
        send[j, :, 384:512] = c_grad[cut]
        send[j, :, 512:768] = gate_grad[cut, :]
        send[j, :, 768:896] = dt_low[cut]
        send[j, :, 896:1152] = shared


def unpack_kernel(received, x_out, b_out, c_out, dt_out, gate_out, conv_b_out, conv_c_out, gain_out):
    ways = received.shape[0]
    lane = iota((ROWS, 128), 1)
    dt = jnp.zeros((ROWS, 128), F32)
    shared = []
    for j in range(ways):
        own = slice(j * CW, (j + 1) * CW)
        x_out[:, own] = received[j, :, 0:256]
        gate_out[:, own] = received[j, :, 512:768]
        turned = pltpu.roll(received[j, :, 768:896].astype(F32), HD * j, 1)
        dt = jnp.where(lane // HD == j, turned, dt)
        three = received[j, :, 896:1152].astype(F32)
        shared.append(three[0:5] + three[5:10] + three[10:15])
        gain_out[:, own] = shared[j][4:5, :]
    dt_out[...] = dt[:, 0 : dt_out.shape[1]].astype(BF)
    per = ways // GROUPS
    for g in range(GROUPS):
        cut = slice(g * N, (g + 1) * N)
        b_sum, c_sum, w_sum = 0.0, 0.0, 0.0
        for j in range(g * per, (g + 1) * per):
            b_sum = b_sum + received[j, :, 256:384].astype(F32)
            c_sum = c_sum + received[j, :, 384:512].astype(F32)
            w_sum = w_sum + shared[j]
        b_out[:, cut] = b_sum.astype(BF)
        c_out[:, cut] = c_sum.astype(BF)
        conv_b_out[:, cut] = w_sum[0:KT, 0:128]
        conv_c_out[:, cut] = w_sum[0:KT, 128:256]


def per_device(
    x_in, b_in, c_in, dt_in, gate_in, out_grad, conv_x, conv_b, conv_c, a_log, dt_bias, d_skip, norm_gain
):
    ways = lax.axis_size("head")
    blocks = lax.axis_size("ctx")
    head_at = lax.axis_index("head")
    where = jnp.stack([head_at, (head_at * GROUPS) // ways]).astype(jnp.int32)
    head = jnp.concatenate([a_log, dt_bias, d_skip])
    gain = norm_gain.reshape(1, -1)

    def ctx_swap(value):
        return lax.all_to_all(value, "ctx", 0, 0, tiled=True)

    def head_swap(value):
        return lax.all_to_all(value, "head", 0, 0, tiled=True)

    inputs = (x_in, b_in, c_in, dt_in, gate_in, out_grad)
    sent = call(
        pack_kernel,
        [sds((ways, ROWS, IN_W), BF)],
        "hhhhhh",
        scratch=[pltpu.VMEM(a.shape, a.dtype) for a in inputs] + [pltpu.SemaphoreType.DMA((6,))],
    )(*inputs)[0]
    arrived = head_swap(sent)
    rows = arrived.reshape(T, IN_W)
    halo = lax.ppermute(
        arrived[ways - 1, :, 0:512], "ctx", [(i, i + 1) for i in range(blocks - 1)]
    )
    wide = sds((T, CW), F32)
    slim = sds((T, 128), F32)
    chunk = sds((blocks, T // blocks, 128), F32)
    ext = pltpu.VMEM((ROWS + T, 512), F32)

    xbc, step, cum, send = call(
        enter_kernel,
        [sds((T, 512), BF), slim, slim, sds((blocks, 2 * T // blocks, 128), F32)],
        "vvvvvss",
        scratch=[ext],
    )(rows, halo, conv_x, conv_b, conv_c, head, where)
    received = ctx_swap(send)
    inside, kept = call(
        within_kernel, [wide, sds((HD, T, T), BF)], "vvv", flops=10**8, bytes_accessed=2 * 10**6
    )(xbc, step, cum)
    send, decays = call(scan_kernel, [chunk, chunk], "v")(received)
    carried = ctx_swap(send).reshape(T, 128)
    y, mixed, sums = call(
        mix_kernel, [wide, sds((T, CW), BF), sds((8, T), F32)], "vvvvvvss"
    )(carried, xbc, inside, cum, rows, gain, head, where)
    per = ways // GROUPS
    sums = lax.psum(
        sums, "head", axis_index_groups=[[g * per + i for i in range(per)] for g in range(GROUPS)]
    )
    y_grad, gate_grad, gain_grad, lifted, send = call(
        norm_kernel,
        [sds((T, CW), BF), sds((T, CW), BF), sds((8, CW), F32), wide, chunk],
        "vvvvvvs",
    )(sums, mixed, rows, gain, xbc, cum, where)
    received = ctx_swap(send)
    x_part, b_part, c_grad, out_dots, in_dots, skip_grad, slopes = call(
        back_kernel,
        [wide, slim, slim, slim, slim, sds((8, CW), F32), sds((T, 512), F32)],
        "vvvvvsvvvvvvvv",
        scratch=[ext],
        flops=3 * 10**8,
        bytes_accessed=4 * 10**6,
    )(rows, halo, conv_x, conv_b, conv_c, where, xbc, step, cum, kept, y, y_grad, lifted, carried)
    send = call(scan_back_kernel, [chunk], "vv")(received, decays)[0]
    end_grad = ctx_swap(send).reshape(T, 128)
    pre, dt_grad, rim, send = call(
        leave_kernel,
        [sds((T, 512), F32), slim, sds((8, 512), F32), sds((blocks, 24, 128), F32)],
        "vvvs" + "v" * 13,
        scratch=[ext],
    )(
        end_grad, rows, halo, head, xbc, step, cum, y_grad, x_part, b_part, c_grad, out_dots,
        in_dots, carried, gain_grad, skip_grad, slopes,
    )
    following = lax.ppermute(rim, "ctx", [(i + 1, i) for i in range(blocks - 1)])
    received = ctx_swap(send)
    four = sds((HD,), F32)
    send, conv_x_grad, alog_grad, bias_grad, skip_sum = call(
        finish_kernel,
        [sds((ways, ROWS, OUT_W), BF), sds((KT, CW), F32), four, four, four],
        "vvsvvvvvv",
        "vvsss",
        scratch=[pltpu.VMEM((T + 8, 512), F32)],
    )(received, following, where, conv_x, conv_b, conv_c, pre, dt_grad, gate_grad)
    received = head_swap(send)
    x_grad, b_grad, c_grad, dt_out, gate_out, conv_b_grad, conv_c_grad, gain_sum = call(
        unpack_kernel,
        [
            sds(x_in.shape, BF),
            sds(b_in.shape, BF),
            sds(c_in.shape, BF),
            sds(dt_in.shape, BF),
            sds(gate_in.shape, BF),
            sds(conv_b.shape, F32),
            sds(conv_c.shape, F32),
            sds((1, norm_gain.shape[0]), F32),
        ],
        "v",
    )(received)
    return (
        x_grad,
        b_grad,
        c_grad,
        dt_out,
        gate_out,
        conv_x_grad,
        conv_b_grad,
        conv_c_grad,
        alog_grad,
        bias_grad,
        skip_sum,
        gain_sum.reshape(-1),
    )


def solution(mesh):
    tokens = P(("ctx", "head"), None)
    return jax.shard_map(
        per_device,
        mesh=mesh,
        in_specs=(tokens,) * 6 + (P(None, "head"), P(), P(), P("head"), P("head"), P("head"), P()),
        out_specs=(tokens,) * 5
        + (P(None, "head"), P(), P(), P("head"), P("head"), P("head"), P()),
        check_vma=False,
    )
```

```python
import functools

import jax
import jax.numpy as jnp
from jax import lax
from jax.experimental import pallas as pl
from jax.experimental.pallas import tpu as pltpu
from jax.sharding import PartitionSpec as P

BF, F32 = jnp.bfloat16, jnp.float32
GROUPS = 8
N = 128
PS = 64
HD = 4
CW = 256
T = 256
KT = 4
ROWS = 16
IN_W = 1152
OUT_W = 1152
VMEM_LIMIT = 8 * 1024 * 1024
PACK_LIMIT = 60 * 1024 * 1024


def dot(a, b, ca, cb):
    return lax.dot_general(
        a, b, (((ca,), (cb,)), ((), ())), preferred_element_type=F32
    )


def pieces(a, count):
    out = []
    for _ in range(count - 1):
        head = a.astype(BF)
        out.append(head)
        a = a - head.astype(F32)
    return out + [a.astype(BF)]


def dot_parts(a, b, ca, cb, count):
    total = None
    for piece in pieces(a, count):
        term = dot(piece, b, ca, cb)
        total = term if total is None else total + term
    return total


def dot_right(a, b, ca, cb):
    high, low = pieces(b, 2)
    return dot(a, high, ca, cb) + dot(a, low, ca, cb)


def dot_both(a, b, ca, cb):
    a_high, a_low = pieces(a, 2)
    b_high, b_low = pieces(b, 2)
    return dot(a_high, b_high, ca, cb) + (dot(a_high, b_low, ca, cb) + dot(a_low, b_high, ca, cb))


def iota(shape, axis):
    return lax.broadcasted_iota(jnp.int32, shape, axis)


def spread(cols):
    low = iota((cols.shape[0], 128), 1) < PS
    halves = []
    for pair in range(HD // 2):
        first = jnp.broadcast_to(cols[:, 2 * pair : 2 * pair + 1], (cols.shape[0], 128))
        second = jnp.broadcast_to(cols[:, 2 * pair + 1 : 2 * pair + 2], (cols.shape[0], 128))
        halves.append(jnp.where(low, first, second))
    return jnp.concatenate(halves, axis=1)


def head_sums(wide):
    pick = (iota((CW, 128), 0) // PS == iota((CW, 128), 1)).astype(BF)
    return dot_parts(wide, pick, 1, 0, 3)


def scalar_row(ref, first, width, per):
    lane = iota((1, width), 1) // per
    row = jnp.zeros((1, width), F32)
    for e in range(HD):
        row = jnp.where(lane == e, ref[first + e], row)
    return row


def softplus(v):
    return jnp.maximum(v, 0.0) + jnp.log1p(jnp.exp(-jnp.abs(v)))


def rates(dt_cols, bias_row, alog_row):
    live = iota((T, 128), 1) < HD
    shifted = dt_cols + bias_row
    step = jnp.where(live, softplus(shifted), 0.0)
    logd = -jnp.exp(alog_row) * step
    tril = (iota((T, T), 0) >= iota((T, T), 1)).astype(BF)
    cum = sum(dot(tril, piece, 1, 0) for piece in pieces(logd, 3))
    return shifted, step, logd, cum


def taps(ext_ref, weight, lo, hi):
    total = None
    for k in range(KT):
        term = weight[k : k + 1, :] * ext_ref[ROWS - KT + 1 + k : ROWS - KT + 1 + k + T, lo:hi]
        total = term if total is None else total + term
    return total


def gap_decay(cum, cum_t, e):
    causal = iota((T, T), 0) >= iota((T, T), 1)
    gap = jnp.where(causal, cum[:, e : e + 1] - cum_t[e : e + 1, :], 0.0)
    return jnp.where(causal, jnp.exp(gap), 0.0)


def silu_slope(pre):
    gate = jax.nn.sigmoid(pre)
    return pre * gate, gate * (1.0 + pre * (1.0 - gate))


def three_rows(row, count):
    at = iota((count, row.shape[1]), 0)
    high, middle, low = pieces(row, 3)
    return jnp.where(
        at == 0,
        high.astype(F32),
        jnp.where(at == 1, middle.astype(F32), jnp.where(at == 2, low.astype(F32), 0.0)),
    ).astype(BF)


def enter_math(ext, dt_cols, wx, wb, bias_row, alog_row):
    def act(weight, lo, hi):
        pre = taps(ext, weight, lo, hi)
        return (pre * jax.nn.sigmoid(pre)).astype(BF)

    x_act, b_act = act(wx, 0, 256), act(wb, 256, 384)
    shifted, step, logd, cum = rates(dt_cols, bias_row, alog_row)
    final = cum[T - 1 : T, :]
    to_end = jnp.exp(final - cum) * step
    wide_end = spread(to_end)
    late = iota((T, CW), 0) >= KT - 1
    weighted = jnp.where(late, x_act.astype(F32) * wide_end, 0.0)
    fresh = dot_parts(weighted, b_act, 0, 0, 2)
    return step, cum, fresh, wide_end[0:8], spread(jnp.broadcast_to(final, (8, 128)))


def within_math(x_act, b_act, c_act, step, cum, cum_t):
    scores = dot(c_act, b_act, 1, 1)
    stepped = x_act.astype(F32) * spread(step)
    outs, kept = [], []
    for e in range(HD):
        mix = (scores * gap_decay(cum, cum_t, e)).astype(BF)
        kept.append(mix)
        part = stepped[:, e * PS : (e + 1) * PS]
        high, low = pieces(part, 2)
        both = dot(mix, jnp.concatenate([high, low], axis=1), 1, 0)
        outs.append(both[:, :PS] + both[:, PS:])
    return jnp.concatenate(outs, axis=1), kept


def mix_math(x_act, c_act, inside, carried, cum, skip_row, gate, out_grad, gain):
    grown = spread(jnp.exp(cum))
    y = inside + grown * dot_right(c_act, carried, 1, 1)
    mixed = (y + skip_row * x_act.astype(F32)).astype(BF)
    gate_act = gate * jax.nn.sigmoid(gate)
    v = mixed.astype(F32) * gate_act
    squares = jnp.sum(v * v, axis=1, keepdims=True)
    along = jnp.sum(out_grad * gain * v, axis=1, keepdims=True)
    return y, mixed, squares, along


def norm_math(mixed, gate, out_grad, gain, squares, along, c_act, cum):
    gate_act, gate_slope = silu_slope(gate)
    mixed = mixed.astype(F32)
    v = mixed * gate_act
    inv = lax.rsqrt(squares * (1.0 / (2 * CW)) + 1e-05)
    normed = v * inv
    v_grad = inv * (out_grad * gain - normed * (along * inv * (1.0 / (2 * CW))))
    y_grad = (v_grad * gate_act).astype(BF)
    gate_grad = (v_grad * mixed * gate_slope).astype(BF)
    gain_grad = jnp.sum(out_grad * normed, axis=0, keepdims=True)
    grown = spread(jnp.exp(cum))
    lifted = y_grad.astype(F32) * grown
    start_grad = dot_parts(lifted, c_act, 0, 0, 2)
    return y_grad, gate_grad, gain_grad, start_grad


def within_back_math(x_act, b_act, c_act, step, cum, cum_t, kept, y, y_grad, carried):
    lifted = y_grad.astype(F32) * spread(jnp.exp(cum))
    score_grad = jnp.zeros((T, T), F32)
    x_parts = []
    step_t = step.T
    for e in range(HD):
        cut = slice(e * PS, (e + 1) * PS)
        x_parts.append(dot(kept[e], y_grad[:, cut], 0, 0))
        mix_grad = dot(y_grad[:, cut], x_act[:, cut], 1, 1)
        score_grad = score_grad + mix_grad * (gap_decay(cum, cum_t, e) * step_t[e : e + 1, :])
    x_in = jnp.concatenate(x_parts, axis=1)
    score_grad = score_grad.astype(BF)
    c_grad = dot(score_grad, b_act, 1, 0) + dot_both(lifted, carried, 1, 0)
    b_in = dot(score_grad, c_act, 0, 0)
    dy = y_grad.astype(F32)
    x32 = x_act.astype(F32)
    out_dots = head_sums(dy * y)
    in_dots = head_sums(x32 * x_in)
    skip_grad = jnp.sum(dy * x32, axis=0, keepdims=True)
    return x_in, b_in, c_grad, out_dots, in_dots, skip_grad


def leave_math(x_act, b_act, step, cum, shifted, logd, alog_row, skip_row, y_grad, x_in, b_in, out_dots, in_dots, carried, end_grad):
    final = cum[T - 1 : T, :]
    tail = jnp.exp(final - cum)
    x32 = x_act.astype(F32)
    end_b = end_grad.astype(BF)
    x_state = spread(tail) * dot(b_act, end_b, 1, 1)
    state_dots = head_sums(x32 * x_state)
    wide_step = spread(step)
    x_grad = wide_step * (x_in + x_state) + skip_row * y_grad.astype(F32)
    weighted = (x32 * spread(tail * step)).astype(BF)
    b_grad = b_in + dot(weighted, end_b, 1, 0)
    pull = step * state_dots
    cum_grad = out_dots - step * in_dots - pull
    kept_dots = jnp.sum(carried * end_grad, axis=1, keepdims=True)
    lane = iota((1, 128), 1)
    over = jnp.zeros((1, 128), F32)
    for e in range(HD):
        over = jnp.where(lane == e, jnp.sum(kept_dots[e * PS : (e + 1) * PS, :], axis=0, keepdims=True), over)
    final_grad = jnp.sum(pull, axis=0, keepdims=True) + jnp.exp(final) * over
    triu = (iota((T, T), 0) <= iota((T, T), 1)).astype(BF)
    log_grad = sum(dot(triu, piece, 1, 0) for piece in pieces(cum_grad, 3)) + final_grad
    step_grad = in_dots + state_dots - jnp.exp(alog_row) * log_grad
    alog_grad = jnp.sum(log_grad * logd, axis=0, keepdims=True)
    live = iota((T, 128), 1) < HD
    dt_grad = jnp.where(live, step_grad * jax.nn.sigmoid(shifted), 0.0)
    bias_grad = jnp.sum(dt_grad, axis=0, keepdims=True)
    return x_grad, b_grad, dt_grad, alog_grad, bias_grad


def conv_slopes(ext, wx, wb, wc):
    def slope(weight, lo, hi):
        return silu_slope(taps(ext, weight, lo, hi))[1]

    return jnp.concatenate([slope(wx, 0, 256), slope(wb, 256, 384), slope(wc, 384, 512)], axis=1)


def weight_grads(ext, pre_grad):
    return [
        jnp.sum(pre_grad * ext[ROWS - KT + 1 + k : ROWS - KT + 1 + k + T], axis=0, keepdims=True)
        for k in range(KT)
    ]


def conv_back(pre_ext, weight, lo, hi):
    total = None
    for k in range(KT):
        term = weight[k : k + 1, :] * pre_ext[KT - 1 - k : KT - 1 - k + T, lo:hi]
        total = term if total is None else total + term
    return total


def call(kernel, out_shape, in_specs, out_specs=None, scratch=(), flops=0, bytes_accessed=0, limit=VMEM_LIMIT):
    place = {
        "v": pl.BlockSpec(memory_space=pltpu.VMEM),
        "s": pl.BlockSpec(memory_space=pltpu.SMEM),
        "h": pl.BlockSpec(memory_space=pltpu.HBM),
    }
    return pl.pallas_call(
        kernel,
        out_shape=out_shape,
        in_specs=[place[c] for c in in_specs],
        out_specs=[place[c] for c in (out_specs or "v" * len(out_shape))],
        scratch_shapes=list(scratch),
        compiler_params=pltpu.CompilerParams(vmem_limit_bytes=limit),
        cost_estimate=pl.CostEstimate(
            flops=flops, bytes_accessed=bytes_accessed, transcendentals=0
        ),
    )


def sds(shape, dtype):
    return jax.ShapeDtypeStruct(shape, dtype)


def pack_kernel(x_at, b_at, c_at, dt_at, gate_at, grad_at, out, x, b, c, dt, gate, out_grad, sems):
    moves = [
        pltpu.make_async_copy(source, target, sems.at[i])
        for i, (source, target) in enumerate(
            [(x_at, x), (b_at, b), (c_at, c), (dt_at, dt), (gate_at, gate), (grad_at, out_grad)]
        )
    ]
    for move in moves:
        move.start()
    for move in moves:
        move.wait()
    ways = out.shape[0]
    per = GROUPS * N // ways
    wide_dt = jnp.concatenate(
        [dt[...].astype(F32), jnp.zeros((ROWS, 128 - dt.shape[1]), F32)], axis=1
    )
    lane = iota((ROWS, 128), 1)
    for j in range(ways):
        g = (j * per) // N
        own = slice(j * CW, (j + 1) * CW)
        shared = slice(g * N, (g + 1) * N)
        out[j, :, 0:256] = x[:, own]
        out[j, :, 256:384] = b[:, shared]
        out[j, :, 384:512] = c[:, shared]
        out[j, :, 512:768] = gate[:, own]
        out[j, :, 768:1024] = out_grad[:, own]
        turned = pltpu.roll(wide_dt, (128 - HD * j) % 128, 1)
        out[j, :, 1024:1152] = jnp.where(lane < HD, turned, 0.0).astype(BF)


def group_lanes(ref, where):
    return ref[:, pl.ds(pl.multiple_of(where[1] * N, N), N)]


def gain_lanes(ref, where):
    return ref[:, pl.ds(pl.multiple_of(where[0] * CW, CW), CW)]


def head_column(row):
    return jnp.concatenate(
        [jnp.broadcast_to(row[:, e : e + 1], (PS, 128)) for e in range(HD)], axis=0
    )


def enter_kernel(rows, wx, wb, head, where, step_out, cum_out, send, ext):
    ext[0:ROWS] = jnp.zeros((ROWS, 384), F32)
    ext[ROWS : ROWS + T] = rows[:, 0:384].astype(F32)
    step, cum, fresh, first_end, final = enter_math(
        ext,
        rows[:, 1024:1152].astype(F32),
        wx[...],
        group_lanes(wb, where),
        scalar_row(head, HD, 128, 1),
        scalar_row(head, 0, 128, 1),
    )
    step_out[...] = step
    cum_out[...] = cum
    count = send.shape[0]
    first = ext[ROWS : ROWS + 8]
    last = pltpu.roll(ext[ROWS + T - 8 : ROWS + T], 6, 0)
    rim = jnp.where(iota((8, 384), 0) < 3, first, last)
    ends = jnp.where(iota((8, CW), 0) < 3, first_end, final)
    columns = jnp.concatenate([rim[:, 0:CW], ends, jnp.zeros((112, CW), F32)], axis=0).T
    send[:, 0:8] = fresh.reshape(count, 8, 128)
    send[:, 8:16] = columns.reshape(count, 8, 128)
    for i in range(count):
        send[i, 16:24] = rim[:, 256:384]


def within_kernel(rows, halo, wx, wb, wc, where, step, cum, xbc, slopes, inside, kept, ext):
    ext[0:ROWS] = halo[...].astype(F32)
    ext[ROWS : ROWS + T] = rows[:, 0:512].astype(F32)
    acts = []
    for weight, lo, hi in (
        (wx[...], 0, 256),
        (group_lanes(wb, where), 256, 384),
        (group_lanes(wc, where), 384, 512),
    ):
        value, slope = silu_slope(taps(ext, weight, lo, hi))
        acts.append(value.astype(BF))
        xbc[:, lo:hi] = acts[-1]
        slopes[:, lo:hi] = slope
    step, cum = step[...], cum[...]
    out, mixes = within_math(*acts, step, cum, cum.T)
    inside[...] = out
    for e in range(HD):
        kept[e] = mixes[e]


def scan_kernel(received, wx, wb, where, send, decays, columns):
    count = received.shape[0]
    columns[...] = jnp.concatenate([wx[...], jnp.zeros((128 - KT, CW), F32)], axis=0).T
    mine = columns[pl.ds(pl.multiple_of(where[2] * 8, 8), 8), :]
    taps_b = group_lanes(wb, where)
    lane, row = iota((8, 128), 1), iota((8, 128), 0)
    state = jnp.zeros((8, 128), F32)
    x_last, b_last = state, state
    for i in range(count):
        x_rim, b_rim = received[i, 8:16], received[i, 16:24]
        x_seen = jnp.where(lane < 3, pltpu.roll(x_last, 125, 1), pltpu.roll(x_rim, 3, 1))
        b_seen = jnp.where(row < 3, pltpu.roll(b_last, 5, 0), pltpu.roll(b_rim, 3, 0))
        x_pre = mine[:, 0:1] * x_seen
        b_pre = taps_b[0:1] * b_seen
        for k in range(1, KT):
            x_pre = x_pre + mine[:, k : k + 1] * pltpu.roll(x_seen, 128 - k, 1)
            b_pre = b_pre + taps_b[k : k + 1] * pltpu.roll(b_seen, 8 - k, 0)
        x_act = (x_pre * jax.nn.sigmoid(x_pre)).astype(BF).astype(F32) * pltpu.roll(x_rim, 120, 1)
        b_act = (b_pre * jax.nn.sigmoid(b_pre)).astype(BF).astype(F32)
        fresh = received[i, 0:8]
        for t in range(KT - 1):
            fresh = fresh + x_act[:, t : t + 1] * b_act[t : t + 1, :]
        decay = jnp.exp(jnp.broadcast_to(x_rim[:, 11:12], (8, 128)))
        send[i] = state
        decays[i] = decay
        state = decay * state + fresh
        x_last, b_last = x_rim, b_rim


def scan_back_kernel(received, decays, send):
    state = jnp.zeros((8, 128), F32)
    for i in reversed(range(received.shape[0])):
        send[i] = state
        state = decays[i] * state + received[i]


def pair_rows(squares, along):
    lane = iota((T, 128), 1)
    both = jnp.where(lane == 0, squares, jnp.where(lane == 1, along, 0.0))
    return both.T[0:8, :]


def mix_kernel(carried, xbc, inside, cum, rows, gain, head, where, y_out, mixed_out, message):
    y, mixed, squares, along = mix_math(
        xbc[:, 0:256],
        xbc[:, 384:512],
        inside[...],
        carried[...],
        cum[...],
        scalar_row(head, 2 * HD, CW, PS),
        rows[:, 512:768].astype(F32),
        rows[:, 768:1024].astype(F32),
        gain_lanes(gain, where),
    )
    y_out[...] = y
    mixed_out[...] = mixed
    message[...] = pair_rows(squares, along)


def norm_kernel(message, mixed, rows, gain, xbc, cum, where, y_grad_out, gate_out, gain_out, send):
    sums = jnp.concatenate([message[...], jnp.zeros((120, T), F32)], axis=0).T
    y_grad, gate_grad, gain_grad, start_grad = norm_math(
        mixed[...],
        rows[:, 512:768].astype(F32),
        rows[:, 768:1024].astype(F32),
        gain_lanes(gain, where),
        sums[:, 0:1],
        sums[:, 1:2],
        xbc[:, 384:512],
        cum[...],
    )
    y_grad_out[...] = y_grad
    gate_out[...] = gate_grad
    gain_out[...] = jnp.broadcast_to(gain_grad, (8, CW))
    send[...] = start_grad.reshape(send.shape)


def back_kernel(xbc, step, cum, kept, y, y_grad, carried, middle, dots):
    cum = cum[...]
    x_in, b_in, c_grad, out_dots, in_dots, skip_grad = within_back_math(
        xbc[:, 0:256],
        xbc[:, 256:384],
        xbc[:, 384:512],
        step[...],
        cum,
        cum.T,
        [kept[e] for e in range(HD)],
        y[...],
        y_grad[...],
        carried[...],
    )
    middle[:, 0:256] = x_in
    middle[:, 256:384] = b_in
    middle[:, 384:512] = c_grad
    dots[0:T] = out_dots + pltpu.roll(in_dots, 64, 1)
    dots[T : T + 8] = head_sums(jnp.broadcast_to(skip_grad, (8, CW)))


def leave_kernel(
    end_grad, rows, halo, head, xbc, step, cum, y_grad, middle, dots, carried, gain_grad, slopes,
    pre_out, dt_out, send, ext,
):
    ext[0:ROWS] = halo[...].astype(F32)
    ext[ROWS : ROWS + T] = rows[:, 0:512].astype(F32)
    alog_row = scalar_row(head, 0, 128, 1)
    step = step[...]
    both = dots[0:T]
    live = iota((T, 128), 1) < HD
    x_grad, b_grad, dt_grad, alog_grad, bias_grad = leave_math(
        xbc[:, 0:256],
        xbc[:, 256:384],
        step,
        cum[...],
        rows[:, 1024:1152].astype(F32) + scalar_row(head, HD, 128, 1),
        -jnp.exp(alog_row) * step,
        alog_row,
        scalar_row(head, 2 * HD, CW, PS),
        y_grad[...],
        middle[:, 0:256],
        middle[:, 256:384],
        jnp.where(live, both, 0.0),
        jnp.where(live, pltpu.roll(both, 64, 1), 0.0),
        carried[...],
        end_grad[...],
    )
    dt_out[...] = dt_grad
    pre = jnp.concatenate([x_grad, b_grad, middle[:, 384:512]], axis=1) * slopes[...]
    pre_out[...] = pre
    weights = jnp.concatenate(weight_grads(ext, pre), axis=0)
    sums = jnp.concatenate([alog_grad, bias_grad, dots[T : T + 1], jnp.zeros((5, 128), F32)], axis=0)
    line = sums[0:1] + pltpu.roll(sums, 32, 1)[1:2] + pltpu.roll(sums, 64, 1)[2:3]
    block = jnp.concatenate(
        [weights[:, i * 128 : (i + 1) * 128] for i in range(4)]
        + [gain_grad[0:1, 0:128], gain_grad[0:1, 128:256], line]
        + [pre[0:3, i * 128 : (i + 1) * 128] for i in range(4)]
        + [jnp.zeros((1, 128), F32)],
        axis=0,
    )
    for i in range(send.shape[0]):
        send[i] = block


def finish_kernel(received, where, wx, wb, wc, pre, dt_grad, gate_grad, send, conv_x_out, alog_out, bias_out, skip_out, ext):
    count = received.shape[0]
    total = received[0, 0:24]
    for i in range(1, count):
        total = total + received[i, 0:24]
    after = where[2] + 1
    next_block = received[jnp.minimum(after, count - 1)]
    following = jnp.concatenate(
        [next_block[19 + 3 * i : 22 + 3 * i] for i in range(4)], axis=1
    )
    ext[0:T] = pre[...]
    ext[T : T + 3] = jnp.where(after < count, following, 0.0)
    x_grad = conv_back(ext, wx[...], 0, 256).astype(BF)
    b_grad = conv_back(ext, group_lanes(wb, where), 256, 384).astype(BF)
    c_grad = conv_back(ext, group_lanes(wc, where), 384, 512).astype(BF)
    conv_x_out[...] = jnp.concatenate([total[0:4], total[4:8]], axis=1)
    for e in range(HD):
        alog_out[e] = jnp.sum(total[18:19, e : e + 1])
        bias_out[e] = jnp.sum(total[18:19, 32 + e : 33 + e])
        skip_out[e] = jnp.sum(total[18:19, 64 + e : 65 + e])
    shared = jnp.concatenate(
        [
            jnp.concatenate([total[8:12], total[12:16]], axis=1),
            jnp.concatenate([total[16:17], total[17:18]], axis=1),
        ],
        axis=0,
    )
    high = shared.astype(BF).astype(F32)
    middle = (shared - high).astype(BF).astype(F32)
    low = shared - high - middle
    shared = jnp.concatenate([high, middle, low, jnp.zeros((1, 256), F32)], axis=0).astype(BF)
    dt_low = dt_grad[...].astype(BF)
    for j in range(send.shape[0]):
        cut = slice(j * ROWS, (j + 1) * ROWS)
        send[j, :, 0:256] = x_grad[cut]
        send[j, :, 256:384] = b_grad[cut]
        send[j, :, 384:512] = c_grad[cut]
        send[j, :, 512:768] = gate_grad[cut, :]
        send[j, :, 768:896] = dt_low[cut]
        send[j, :, 896:1152] = shared


def unpack_kernel(received, x_out, b_out, c_out, dt_out, gate_out, conv_b_out, conv_c_out, gain_out):
    ways = received.shape[0]
    lane = iota((ROWS, 128), 1)
    dt = jnp.zeros((ROWS, 128), F32)
    shared = []
    for j in range(ways):
        own = slice(j * CW, (j + 1) * CW)
        x_out[:, own] = received[j, :, 0:256]
        gate_out[:, own] = received[j, :, 512:768]
        turned = pltpu.roll(received[j, :, 768:896].astype(F32), HD * j, 1)
        dt = jnp.where(lane // HD == j, turned, dt)
        three = received[j, :, 896:1152].astype(F32)
        shared.append(three[0:5] + three[5:10] + three[10:15])
        gain_out[:, own] = shared[j][4:5, :]
    dt_out[...] = dt[:, 0 : dt_out.shape[1]].astype(BF)
    per = ways // GROUPS
    for g in range(GROUPS):
        cut = slice(g * N, (g + 1) * N)
        b_sum, c_sum, w_sum = 0.0, 0.0, 0.0
        for j in range(g * per, (g + 1) * per):
            b_sum = b_sum + received[j, :, 256:384].astype(F32)
            c_sum = c_sum + received[j, :, 384:512].astype(F32)
            w_sum = w_sum + shared[j]
        b_out[:, cut] = b_sum.astype(BF)
        c_out[:, cut] = c_sum.astype(BF)
        conv_b_out[:, cut] = w_sum[0:KT, 0:128]
        conv_c_out[:, cut] = w_sum[0:KT, 128:256]


def per_device(
    x_in, b_in, c_in, dt_in, gate_in, out_grad, conv_x, conv_b, conv_c, a_log, dt_bias, d_skip, norm_gain
):
    ways = lax.axis_size("head")
    blocks = lax.axis_size("ctx")
    head_at = lax.axis_index("head")
    where = jnp.stack([head_at, (head_at * GROUPS) // ways, lax.axis_index("ctx")]).astype(jnp.int32)
    head = jnp.concatenate([a_log, dt_bias, d_skip])
    gain = norm_gain.reshape(1, -1)

    def ctx_swap(value):
        return lax.all_to_all(value, "ctx", 0, 0, tiled=True)

    def head_swap(value):
        return lax.all_to_all(value, "head", 0, 0, tiled=True)

    inputs = (x_in, b_in, c_in, dt_in, gate_in, out_grad)
    sent = call(
        pack_kernel,
        [sds((ways, ROWS, IN_W), BF)],
        "hhhhhh",
        scratch=[pltpu.VMEM(a.shape, a.dtype) for a in inputs] + [pltpu.SemaphoreType.DMA((6,))],
        limit=PACK_LIMIT,
    )(*inputs)[0]
    arrived = head_swap(sent)
    rows = arrived.reshape(T, IN_W)
    halo = lax.ppermute(
        arrived[ways - 1, :, 0:512], "ctx", [(i, i + 1) for i in range(blocks - 1)]
    )
    wide = sds((T, CW), F32)
    slim = sds((T, 128), F32)
    chunk = sds((blocks, T // blocks, 128), F32)
    ext = pltpu.VMEM((ROWS + T, 512), F32)

    step, cum, send = call(
        enter_kernel,
        [slim, slim, sds((blocks, 24, 128), F32)],
        "vvvss",
        scratch=[pltpu.VMEM((ROWS + T, 384), F32)],
    )(rows, conv_x, conv_b, head, where)
    received = ctx_swap(send)
    xbc, slopes, inside, kept = call(
        within_kernel,
        [sds((T, 512), BF), sds((T, 512), F32), wide, sds((HD, T, T), BF)],
        "vvvvvsvv",
        scratch=[ext],
        flops=10**8,
        bytes_accessed=3 * 10**6,
    )(rows, halo, conv_x, conv_b, conv_c, where, step, cum)
    send, decays = call(
        scan_kernel, [chunk, chunk], "vvvs", scratch=[pltpu.VMEM((CW, 128), F32)]
    )(received, conv_x, conv_b, where)
    carried = ctx_swap(send).reshape(T, 128)
    y, mixed, sums = call(
        mix_kernel, [wide, sds((T, CW), BF), sds((8, T), F32)], "vvvvvvss"
    )(carried, xbc, inside, cum, rows, gain, head, where)
    per = ways // GROUPS
    sums = lax.psum(
        sums, "head", axis_index_groups=[[g * per + i for i in range(per)] for g in range(GROUPS)]
    )
    y_grad, gate_grad, gain_grad, send = call(
        norm_kernel,
        [sds((T, CW), BF), sds((T, CW), BF), sds((8, CW), F32), chunk],
        "vvvvvvs",
    )(sums, mixed, rows, gain, xbc, cum, where)
    received = ctx_swap(send)
    middle, dots = call(
        back_kernel,
        [sds((T, 512), F32), sds((T + 8, 128), F32)],
        "vvvvvvv",
        flops=3 * 10**8,
        bytes_accessed=4 * 10**6,
    )(xbc, step, cum, kept, y, y_grad, carried)
    send = call(scan_back_kernel, [chunk], "vv")(received, decays)[0]
    end_grad = ctx_swap(send).reshape(T, 128)
    pre, dt_grad, send = call(
        leave_kernel,
        [sds((T, 512), F32), slim, sds((blocks, 32, 128), F32)],
        "vvvs" + "v" * 9,
        scratch=[ext],
    )(
        end_grad, rows, halo, head, xbc, step, cum, y_grad, middle, dots, carried, gain_grad, slopes,
    )
    received = ctx_swap(send)
    four = sds((HD,), F32)
    send, conv_x_grad, alog_grad, bias_grad, skip_sum = call(
        finish_kernel,
        [sds((ways, ROWS, OUT_W), BF), sds((KT, CW), F32), four, four, four],
        "vsvvvvvv",
        "vvsss",
        scratch=[pltpu.VMEM((T + 8, 512), F32)],
    )(received, where, conv_x, conv_b, conv_c, pre, dt_grad, gate_grad)
    received = head_swap(send)
    x_grad, b_grad, c_grad, dt_out, gate_out, conv_b_grad, conv_c_grad, gain_sum = call(
        unpack_kernel,
        [
            sds(x_in.shape, BF),
            sds(b_in.shape, BF),
            sds(c_in.shape, BF),
            sds(dt_in.shape, BF),
            sds(gate_in.shape, BF),
            sds(conv_b.shape, F32),
            sds(conv_c.shape, F32),
            sds((1, norm_gain.shape[0]), F32),
        ],
        "v",
    )(received)
    return (
        x_grad,
        b_grad,
        c_grad,
        dt_out,
        gate_out,
        conv_x_grad,
        conv_b_grad,
        conv_c_grad,
        alog_grad,
        bias_grad,
        skip_sum,
        gain_sum.reshape(-1),
    )


def solution(mesh):
    tokens = P(("ctx", "head"), None)
    return jax.shard_map(
        per_device,
        mesh=mesh,
        in_specs=(tokens,) * 6 + (P(None, "head"), P(), P(), P("head"), P("head"), P("head"), P()),
        out_specs=(tokens,) * 5
        + (P(None, "head"), P(), P(), P("head"), P("head"), P("head"), P()),
        check_vma=False,
    )
```

```python
import functools

import jax
import jax.numpy as jnp
from jax import lax
from jax.experimental import pallas as pl
from jax.experimental.pallas import tpu as pltpu
from jax.sharding import PartitionSpec as P

BF, F32 = jnp.bfloat16, jnp.float32
GROUPS = 8
N = 128
PS = 64
HD = 4
CW = 256
T = 256
KT = 4
ROWS = 16
IN_W = 1152
OUT_W = 1152
VMEM_LIMIT = 8 * 1024 * 1024
PACK_LIMIT = 60 * 1024 * 1024


def dot(a, b, ca, cb):
    return lax.dot_general(
        a, b, (((ca,), (cb,)), ((), ())), preferred_element_type=F32
    )


def pieces(a, count):
    out = []
    for _ in range(count - 1):
        head = a.astype(BF)
        out.append(head)
        a = a - head.astype(F32)
    return out + [a.astype(BF)]


def dot_parts(a, b, ca, cb, count):
    total = None
    for piece in pieces(a, count):
        term = dot(piece, b, ca, cb)
        total = term if total is None else total + term
    return total


def dot_right(a, b, ca, cb):
    high, low = pieces(b, 2)
    return dot(a, high, ca, cb) + dot(a, low, ca, cb)


def dot_both(a, b, ca, cb):
    a_high, a_low = pieces(a, 2)
    b_high, b_low = pieces(b, 2)
    return dot(a_high, b_high, ca, cb) + (dot(a_high, b_low, ca, cb) + dot(a_low, b_high, ca, cb))


def iota(shape, axis):
    return lax.broadcasted_iota(jnp.int32, shape, axis)


def spread(cols):
    low = iota((cols.shape[0], 128), 1) < PS
    halves = []
    for pair in range(HD // 2):
        first = jnp.broadcast_to(cols[:, 2 * pair : 2 * pair + 1], (cols.shape[0], 128))
        second = jnp.broadcast_to(cols[:, 2 * pair + 1 : 2 * pair + 2], (cols.shape[0], 128))
        halves.append(jnp.where(low, first, second))
    return jnp.concatenate(halves, axis=1)


def head_sums(wide):
    pick = (iota((CW, 128), 0) // PS == iota((CW, 128), 1)).astype(BF)
    return dot_parts(wide, pick, 1, 0, 3)


def scalar_row(ref, first, width, per):
    lane = iota((1, width), 1) // per
    row = jnp.zeros((1, width), F32)
    for e in range(HD):
        row = jnp.where(lane == e, ref[first + e], row)
    return row


def softplus(v):
    return jnp.maximum(v, 0.0) + jnp.log1p(jnp.exp(-jnp.abs(v)))


def rates(dt_cols, bias_row, alog_row):
    live = iota((T, 128), 1) < HD
    shifted = dt_cols + bias_row
    step = jnp.where(live, softplus(shifted), 0.0)
    logd = -jnp.exp(alog_row) * step
    tril = (iota((T, T), 0) >= iota((T, T), 1)).astype(BF)
    cum = sum(dot(tril, piece, 1, 0) for piece in pieces(logd, 3))
    return shifted, step, logd, cum


def taps(ext_ref, weight, lo, hi):
    total = None
    for k in range(KT):
        term = weight[k : k + 1, :] * ext_ref[ROWS - KT + 1 + k : ROWS - KT + 1 + k + T, lo:hi]
        total = term if total is None else total + term
    return total


def gap_decay(cum, cum_t, e):
    causal = iota((T, T), 0) >= iota((T, T), 1)
    gap = jnp.where(causal, cum[:, e : e + 1] - cum_t[e : e + 1, :], 0.0)
    return jnp.where(causal, jnp.exp(gap), 0.0)


def silu_slope(pre):
    gate = jax.nn.sigmoid(pre)
    return pre * gate, gate * (1.0 + pre * (1.0 - gate))


def three_rows(row, count):
    at = iota((count, row.shape[1]), 0)
    high, middle, low = pieces(row, 3)
    return jnp.where(
        at == 0,
        high.astype(F32),
        jnp.where(at == 1, middle.astype(F32), jnp.where(at == 2, low.astype(F32), 0.0)),
    ).astype(BF)


def enter_math(ext, dt_cols, wx, wb, bias_row, alog_row):
    def act(weight, lo, hi):
        pre = taps(ext, weight, lo, hi)
        return (pre * jax.nn.sigmoid(pre)).astype(BF)

    x_act, b_act = act(wx, 0, 256), act(wb, 256, 384)
    shifted, step, logd, cum = rates(dt_cols, bias_row, alog_row)
    final = cum[T - 1 : T, :]
    to_end = jnp.exp(final - cum) * step
    wide_end = spread(to_end)
    late = iota((T, CW), 0) >= KT - 1
    weighted = jnp.where(late, x_act.astype(F32) * wide_end, 0.0)
    fresh = dot_parts(weighted, b_act, 0, 0, 2)
    return step, cum, fresh, wide_end[0:8], spread(jnp.broadcast_to(final, (8, 128)))


def within_math(x_act, b_act, c_act, step, cum, cum_t):
    scores = dot(c_act, b_act, 1, 1)
    stepped = x_act.astype(F32) * spread(step)
    outs, kept = [], []
    for e in range(HD):
        mix = (scores * gap_decay(cum, cum_t, e)).astype(BF)
        kept.append(mix)
        part = stepped[:, e * PS : (e + 1) * PS]
        high, low = pieces(part, 2)
        both = dot(mix, jnp.concatenate([high, low], axis=1), 1, 0)
        outs.append(both[:, :PS] + both[:, PS:])
    return jnp.concatenate(outs, axis=1), kept


def mix_math(x_act, c_act, inside, carried, cum, skip_row, gate, out_grad, gain):
    grown = spread(jnp.exp(cum))
    y = inside + grown * dot_right(c_act, carried, 1, 1)
    mixed = (y + skip_row * x_act.astype(F32)).astype(BF)
    gate_act = gate * jax.nn.sigmoid(gate)
    v = mixed.astype(F32) * gate_act
    squares = jnp.sum(v * v, axis=1, keepdims=True)
    along = jnp.sum(out_grad * gain * v, axis=1, keepdims=True)
    return y, mixed, squares, along


def norm_math(mixed, gate, out_grad, gain, squares, along, c_act, cum):
    gate_act, gate_slope = silu_slope(gate)
    mixed = mixed.astype(F32)
    v = mixed * gate_act
    inv = lax.rsqrt(squares * (1.0 / (2 * CW)) + 1e-05)
    normed = v * inv
    v_grad = inv * (out_grad * gain - normed * (along * inv * (1.0 / (2 * CW))))
    y_grad = (v_grad * gate_act).astype(BF)
    gate_grad = (v_grad * mixed * gate_slope).astype(BF)
    gain_grad = jnp.sum(out_grad * normed, axis=0, keepdims=True)
    grown = spread(jnp.exp(cum))
    lifted = y_grad.astype(F32) * grown
    start_grad = dot_parts(lifted, c_act, 0, 0, 2)
    return y_grad, gate_grad, gain_grad, start_grad


def within_back_math(x_act, b_act, c_act, step, cum, cum_t, kept, y, y_grad, carried):
    lifted = y_grad.astype(F32) * spread(jnp.exp(cum))
    score_grad = jnp.zeros((T, T), F32)
    x_parts = []
    step_t = step.T
    for e in range(HD):
        cut = slice(e * PS, (e + 1) * PS)
        x_parts.append(dot(kept[e], y_grad[:, cut], 0, 0))
        mix_grad = dot(y_grad[:, cut], x_act[:, cut], 1, 1)
        score_grad = score_grad + mix_grad * (gap_decay(cum, cum_t, e) * step_t[e : e + 1, :])
    x_in = jnp.concatenate(x_parts, axis=1)
    score_grad = score_grad.astype(BF)
    c_grad = dot(score_grad, b_act, 1, 0) + dot_both(lifted, carried, 1, 0)
    b_in = dot(score_grad, c_act, 0, 0)
    dy = y_grad.astype(F32)
    x32 = x_act.astype(F32)
    out_dots = head_sums(dy * y)
    in_dots = head_sums(x32 * x_in)
    skip_grad = jnp.sum(dy * x32, axis=0, keepdims=True)
    return x_in, b_in, c_grad, out_dots, in_dots, skip_grad


def leave_math(x_act, b_act, step, cum, shifted, logd, alog_row, skip_row, y_grad, x_in, b_in, out_dots, in_dots, carried, end_grad):
    final = cum[T - 1 : T, :]
    tail = jnp.exp(final - cum)
    x32 = x_act.astype(F32)
    end_b = end_grad.astype(BF)
    x_state = spread(tail) * dot(b_act, end_b, 1, 1)
    state_dots = head_sums(x32 * x_state)
    wide_step = spread(step)
    x_grad = wide_step * (x_in + x_state) + skip_row * y_grad.astype(F32)
    weighted = (x32 * spread(tail * step)).astype(BF)
    b_grad = b_in + dot(weighted, end_b, 1, 0)
    pull = step * state_dots
    cum_grad = out_dots - step * in_dots - pull
    kept_dots = jnp.sum(carried * end_grad, axis=1, keepdims=True)
    lane = iota((1, 128), 1)
    over = jnp.zeros((1, 128), F32)
    for e in range(HD):
        over = jnp.where(lane == e, jnp.sum(kept_dots[e * PS : (e + 1) * PS, :], axis=0, keepdims=True), over)
    final_grad = jnp.sum(pull, axis=0, keepdims=True) + jnp.exp(final) * over
    triu = (iota((T, T), 0) <= iota((T, T), 1)).astype(BF)
    log_grad = sum(dot(triu, piece, 1, 0) for piece in pieces(cum_grad, 3)) + final_grad
    step_grad = in_dots + state_dots - jnp.exp(alog_row) * log_grad
    alog_grad = jnp.sum(log_grad * logd, axis=0, keepdims=True)
    live = iota((T, 128), 1) < HD
    dt_grad = jnp.where(live, step_grad * jax.nn.sigmoid(shifted), 0.0)
    bias_grad = jnp.sum(dt_grad, axis=0, keepdims=True)
    return x_grad, b_grad, dt_grad, alog_grad, bias_grad


def conv_slopes(ext, wx, wb, wc):
    def slope(weight, lo, hi):
        return silu_slope(taps(ext, weight, lo, hi))[1]

    return jnp.concatenate([slope(wx, 0, 256), slope(wb, 256, 384), slope(wc, 384, 512)], axis=1)


def weight_grads(ext, pre_grad):
    return [
        jnp.sum(pre_grad * ext[ROWS - KT + 1 + k : ROWS - KT + 1 + k + T], axis=0, keepdims=True)
        for k in range(KT)
    ]


def conv_back(pre_ext, weight, lo, hi):
    total = None
    for k in range(KT):
        term = weight[k : k + 1, :] * pre_ext[KT - 1 - k : KT - 1 - k + T, lo:hi]
        total = term if total is None else total + term
    return total


def call(kernel, out_shape, in_specs, out_specs=None, scratch=(), flops=0, bytes_accessed=0, limit=VMEM_LIMIT):
    place = {
        "v": pl.BlockSpec(memory_space=pltpu.VMEM),
        "s": pl.BlockSpec(memory_space=pltpu.SMEM),
        "h": pl.BlockSpec(memory_space=pltpu.HBM),
    }
    return pl.pallas_call(
        kernel,
        out_shape=out_shape,
        in_specs=[place[c] for c in in_specs],
        out_specs=[place[c] for c in (out_specs or "v" * len(out_shape))],
        scratch_shapes=list(scratch),
        compiler_params=pltpu.CompilerParams(vmem_limit_bytes=limit),
        cost_estimate=pl.CostEstimate(
            flops=flops, bytes_accessed=bytes_accessed, transcendentals=0
        ),
    )


def sds(shape, dtype):
    return jax.ShapeDtypeStruct(shape, dtype)


def pack_kernel(x_at, b_at, c_at, dt_at, gate_at, grad_at, out, x, b, c, dt, gate, out_grad, sems):
    moves = [
        pltpu.make_async_copy(source, target, sems.at[i])
        for i, (source, target) in enumerate(
            [(x_at, x), (b_at, b), (c_at, c), (dt_at, dt), (gate_at, gate), (grad_at, out_grad)]
        )
    ]
    for move in moves:
        move.start()
    ways = out.shape[0]
    per = GROUPS * N // ways
    for move, ref, lo in ((moves[0], x, 0), (moves[4], gate, 512), (moves[5], out_grad, 768)):
        move.wait()
        for j in range(ways):
            out[j, :, lo : lo + CW] = ref[:, j * CW : (j + 1) * CW]
    for move, ref, lo in ((moves[1], b, 256), (moves[2], c, 384)):
        move.wait()
        for j in range(ways):
            g = (j * per) // N
            out[j, :, lo : lo + N] = ref[:, g * N : (g + 1) * N]
    moves[3].wait()
    wide_dt = jnp.concatenate(
        [dt[...].astype(F32), jnp.zeros((ROWS, 128 - dt.shape[1]), F32)], axis=1
    )
    lane = iota((ROWS, 128), 1)
    for j in range(ways):
        turned = pltpu.roll(wide_dt, (128 - HD * j) % 128, 1)
        out[j, :, 1024:1152] = jnp.where(lane < HD, turned, 0.0).astype(BF)


def group_lanes(ref, where):
    return ref[:, pl.ds(pl.multiple_of(where[1] * N, N), N)]


def gain_lanes(ref, where):
    return ref[:, pl.ds(pl.multiple_of(where[0] * CW, CW), CW)]


def head_column(row):
    return jnp.concatenate(
        [jnp.broadcast_to(row[:, e : e + 1], (PS, 128)) for e in range(HD)], axis=0
    )


def enter_kernel(rows, wx, wb, head, where, step_out, cum_out, send, ext):
    ext[0:ROWS] = jnp.zeros((ROWS, 384), F32)
    ext[ROWS : ROWS + T] = rows[:, 0:384].astype(F32)
    step, cum, fresh, first_end, final = enter_math(
        ext,
        rows[:, 1024:1152].astype(F32),
        wx[...],
        group_lanes(wb, where),
        scalar_row(head, HD, 128, 1),
        scalar_row(head, 0, 128, 1),
    )
    step_out[...] = step
    cum_out[...] = cum
    count = send.shape[0]
    first = ext[ROWS : ROWS + 8]
    last = pltpu.roll(ext[ROWS + T - 8 : ROWS + T], 6, 0)
    rim = jnp.where(iota((8, 384), 0) < 3, first, last)
    ends = jnp.where(iota((8, CW), 0) < 3, first_end, final)
    columns = jnp.concatenate([rim[:, 0:CW], ends, jnp.zeros((112, CW), F32)], axis=0).T
    send[:, 0:8] = fresh.reshape(count, 8, 128)
    send[:, 8:16] = columns.reshape(count, 8, 128)
    for i in range(count):
        send[i, 16:24] = rim[:, 256:384]


def within_kernel(rows, halo, wx, wb, wc, where, step, cum, xbc, slopes, inside, kept, order, ext):
    ext[0:ROWS] = halo[...].astype(F32)
    ext[ROWS : ROWS + T] = rows[:, 0:512].astype(F32)
    acts = []
    for weight, lo, hi in (
        (wx[...], 0, 256),
        (group_lanes(wb, where), 256, 384),
        (group_lanes(wc, where), 384, 512),
    ):
        value, slope = silu_slope(taps(ext, weight, lo, hi))
        acts.append(value.astype(BF))
        xbc[:, lo:hi] = acts[-1]
        slopes[:, lo:hi] = slope
    step, cum = step[...], cum[...]
    out, mixes = within_math(*acts, step, cum, cum.T)
    inside[...] = out
    order[...] = out[0:8, 0:128]
    for e in range(HD):
        kept[e] = mixes[e]


def scan_kernel(received, wx, wb, where, order, send, decays, columns, fresh, grown):
    del order
    count = received.shape[0]
    columns[...] = jnp.concatenate([wx[...], jnp.zeros((128 - KT, CW), F32)], axis=0).T
    mine = columns[pl.ds(pl.multiple_of(where[2] * 8, 8), 8), :]
    taps_b = group_lanes(wb, where)
    shape = (count, 8, 128)
    lane, row = iota(shape, 2), iota(shape, 1)
    x_rim, b_rim = received[:, 8:16], received[:, 16:24]
    blank = jnp.zeros((1, 8, 128), F32)
    x_last = jnp.concatenate([blank, x_rim[:-1]], axis=0)
    b_last = jnp.concatenate([blank, b_rim[:-1]], axis=0)
    x_seen = jnp.where(lane < 3, pltpu.roll(x_last, 125, 2), pltpu.roll(x_rim, 3, 2))
    b_seen = jnp.where(row < 3, pltpu.roll(b_last, 5, 1), pltpu.roll(b_rim, 3, 1))
    x_pre = mine[None, :, 0:1] * x_seen
    b_pre = taps_b[None, 0:1] * b_seen
    for k in range(1, KT):
        x_pre = x_pre + mine[None, :, k : k + 1] * pltpu.roll(x_seen, 128 - k, 2)
        b_pre = b_pre + taps_b[None, k : k + 1] * pltpu.roll(b_seen, 8 - k, 1)
    x_act = (x_pre * jax.nn.sigmoid(x_pre)).astype(BF).astype(F32) * pltpu.roll(x_rim, 120, 2)
    b_act = (b_pre * jax.nn.sigmoid(b_pre)).astype(BF).astype(F32)
    total = received[:, 0:8]
    for t in range(KT - 1):
        total = total + x_act[:, :, t : t + 1] * b_act[:, t : t + 1, :]
    fresh[...] = total
    grown[...] = jnp.exp(jnp.broadcast_to(x_rim[:, :, 11:12], shape))
    decays[...] = grown[...]
    state = jnp.zeros((8, 128), F32)
    for i in range(count):
        send[i] = state
        state = grown[i] * state + fresh[i]


def scan_back_kernel(received, decays, send):
    state = jnp.zeros((8, 128), F32)
    for i in reversed(range(received.shape[0])):
        send[i] = state
        state = decays[i] * state + received[i]


def pair_rows(squares, along):
    lane = iota((T, 128), 1)
    both = jnp.where(lane == 0, squares, jnp.where(lane == 1, along, 0.0))
    return both.T[0:8, :]


def mix_kernel(carried, xbc, inside, cum, rows, gain, head, where, y_out, mixed_out, message):
    y, mixed, squares, along = mix_math(
        xbc[:, 0:256],
        xbc[:, 384:512],
        inside[...],
        carried[...],
        cum[...],
        scalar_row(head, 2 * HD, CW, PS),
        rows[:, 512:768].astype(F32),
        rows[:, 768:1024].astype(F32),
        gain_lanes(gain, where),
    )
    y_out[...] = y
    mixed_out[...] = mixed
    message[...] = pair_rows(squares, along)


def norm_kernel(message, mixed, rows, gain, xbc, cum, where, y_grad_out, gate_out, gain_out, send):
    sums = jnp.concatenate([message[...], jnp.zeros((120, T), F32)], axis=0).T
    y_grad, gate_grad, gain_grad, start_grad = norm_math(
        mixed[...],
        rows[:, 512:768].astype(F32),
        rows[:, 768:1024].astype(F32),
        gain_lanes(gain, where),
        sums[:, 0:1],
        sums[:, 1:2],
        xbc[:, 384:512],
        cum[...],
    )
    y_grad_out[...] = y_grad
    gate_out[...] = gate_grad
    gain_out[...] = jnp.broadcast_to(gain_grad, (8, CW))
    send[...] = start_grad.reshape(send.shape)


def back_kernel(xbc, step, cum, kept, y, y_grad, carried, middle, dots):
    cum = cum[...]
    x_in, b_in, c_grad, out_dots, in_dots, skip_grad = within_back_math(
        xbc[:, 0:256],
        xbc[:, 256:384],
        xbc[:, 384:512],
        step[...],
        cum,
        cum.T,
        [kept[e] for e in range(HD)],
        y[...],
        y_grad[...],
        carried[...],
    )
    middle[:, 0:256] = x_in
    middle[:, 256:384] = b_in
    middle[:, 384:512] = c_grad
    dots[0:T] = out_dots + pltpu.roll(in_dots, 64, 1)
    dots[T : T + 8] = head_sums(jnp.broadcast_to(skip_grad, (8, CW)))


def leave_kernel(
    end_grad, rows, halo, head, xbc, step, cum, y_grad, middle, dots, carried, gain_grad, slopes,
    pre_out, dt_out, send, ext,
):
    ext[0:ROWS] = halo[...].astype(F32)
    ext[ROWS : ROWS + T] = rows[:, 0:512].astype(F32)
    alog_row = scalar_row(head, 0, 128, 1)
    step = step[...]
    both = dots[0:T]
    live = iota((T, 128), 1) < HD
    x_grad, b_grad, dt_grad, alog_grad, bias_grad = leave_math(
        xbc[:, 0:256],
        xbc[:, 256:384],
        step,
        cum[...],
        rows[:, 1024:1152].astype(F32) + scalar_row(head, HD, 128, 1),
        -jnp.exp(alog_row) * step,
        alog_row,
        scalar_row(head, 2 * HD, CW, PS),
        y_grad[...],
        middle[:, 0:256],
        middle[:, 256:384],
        jnp.where(live, both, 0.0),
        jnp.where(live, pltpu.roll(both, 64, 1), 0.0),
        carried[...],
        end_grad[...],
    )
    dt_out[...] = dt_grad
    pre = jnp.concatenate([x_grad, b_grad, middle[:, 384:512]], axis=1) * slopes[...]
    pre_out[...] = pre
    weights = jnp.concatenate(weight_grads(ext, pre), axis=0)
    sums = jnp.concatenate([alog_grad, bias_grad, dots[T : T + 1], jnp.zeros((5, 128), F32)], axis=0)
    line = sums[0:1] + pltpu.roll(sums, 32, 1)[1:2] + pltpu.roll(sums, 64, 1)[2:3]
    coarse = line.astype(BF).astype(F32)
    block = jnp.concatenate(
        [weights[:, i * 128 : (i + 1) * 128] for i in range(4)]
        + [gain_grad[0:1, 0:128], gain_grad[0:1, 128:256], coarse, line - coarse]
        + [pre[0:3, i * 128 : (i + 1) * 128] for i in range(4)],
        axis=0,
    ).astype(BF)
    for i in range(send.shape[0]):
        send[i] = block


def finish_kernel(received, where, wx, wb, wc, pre, dt_grad, gate_grad, send, conv_x_out, alog_out, bias_out, skip_out, ext):
    count = received.shape[0]
    total = received[0].astype(F32)
    for i in range(1, count):
        total = total + received[i].astype(F32)
    line = total[18:19] + total[19:20]
    after = where[2] + 1
    next_block = received[jnp.minimum(after, count - 1)].astype(F32)
    following = jnp.concatenate(
        [next_block[20 + 3 * i : 23 + 3 * i] for i in range(4)], axis=1
    )
    ext[0:T] = pre[...]
    ext[T : T + 3] = jnp.where(after < count, following, 0.0)
    x_grad = conv_back(ext, wx[...], 0, 256).astype(BF)
    b_grad = conv_back(ext, group_lanes(wb, where), 256, 384).astype(BF)
    c_grad = conv_back(ext, group_lanes(wc, where), 384, 512).astype(BF)
    conv_x_out[...] = jnp.concatenate([total[0:4], total[4:8]], axis=1)
    for e in range(HD):
        alog_out[e] = jnp.sum(line[:, e : e + 1])
        bias_out[e] = jnp.sum(line[:, 32 + e : 33 + e])
        skip_out[e] = jnp.sum(line[:, 64 + e : 65 + e])
    shared = jnp.concatenate(
        [
            jnp.concatenate([total[8:12], total[12:16]], axis=1),
            jnp.concatenate([total[16:17], total[17:18]], axis=1),
        ],
        axis=0,
    )
    high = shared.astype(BF).astype(F32)
    middle = (shared - high).astype(BF).astype(F32)
    low = shared - high - middle
    shared = jnp.concatenate([high, middle, low, jnp.zeros((1, 256), F32)], axis=0).astype(BF)
    dt_low = dt_grad[...].astype(BF)
    for j in range(send.shape[0]):
        cut = slice(j * ROWS, (j + 1) * ROWS)
        send[j, :, 0:256] = x_grad[cut]
        send[j, :, 256:384] = b_grad[cut]
        send[j, :, 384:512] = c_grad[cut]
        send[j, :, 512:768] = gate_grad[cut, :]
        send[j, :, 768:896] = dt_low[cut]
        send[j, :, 896:1152] = shared


def unpack_kernel(received, x_out, b_out, c_out, dt_out, gate_out, conv_b_out, conv_c_out, gain_out):
    ways = received.shape[0]
    lane = iota((ROWS, 128), 1)
    dt = jnp.zeros((ROWS, 128), F32)
    shared = []
    for j in range(ways):
        own = slice(j * CW, (j + 1) * CW)
        x_out[:, own] = received[j, :, 0:256]
        gate_out[:, own] = received[j, :, 512:768]
        turned = pltpu.roll(received[j, :, 768:896].astype(F32), HD * j, 1)
        dt = jnp.where(lane // HD == j, turned, dt)
        three = received[j, :, 896:1152].astype(F32)
        shared.append(three[0:5] + three[5:10] + three[10:15])
        gain_out[:, own] = shared[j][4:5, :]
    dt_out[...] = dt[:, 0 : dt_out.shape[1]].astype(BF)
    per = ways // GROUPS
    for g in range(GROUPS):
        cut = slice(g * N, (g + 1) * N)
        b_sum, c_sum, w_sum = 0.0, 0.0, 0.0
        for j in range(g * per, (g + 1) * per):
            b_sum = b_sum + received[j, :, 256:384].astype(F32)
            c_sum = c_sum + received[j, :, 384:512].astype(F32)
            w_sum = w_sum + shared[j]
        b_out[:, cut] = b_sum.astype(BF)
        c_out[:, cut] = c_sum.astype(BF)
        conv_b_out[:, cut] = w_sum[0:KT, 0:128]
        conv_c_out[:, cut] = w_sum[0:KT, 128:256]


def per_device(
    x_in, b_in, c_in, dt_in, gate_in, out_grad, conv_x, conv_b, conv_c, a_log, dt_bias, d_skip, norm_gain
):
    ways = lax.axis_size("head")
    blocks = lax.axis_size("ctx")
    head_at = lax.axis_index("head")
    where = jnp.stack([head_at, (head_at * GROUPS) // ways, lax.axis_index("ctx")]).astype(jnp.int32)
    head = jnp.concatenate([a_log, dt_bias, d_skip])
    gain = norm_gain.reshape(1, -1)

    def ctx_swap(value):
        return lax.all_to_all(value, "ctx", 0, 0, tiled=True)

    def head_swap(value):
        return lax.all_to_all(value, "head", 0, 0, tiled=True)

    inputs = (x_in, b_in, c_in, dt_in, gate_in, out_grad)
    sent = call(
        pack_kernel,
        [sds((ways, ROWS, IN_W), BF)],
        "hhhhhh",
        scratch=[pltpu.VMEM(a.shape, a.dtype) for a in inputs] + [pltpu.SemaphoreType.DMA((6,))],
        limit=PACK_LIMIT,
    )(*inputs)[0]
    arrived = head_swap(sent)
    rows = arrived.reshape(T, IN_W)
    halo = lax.ppermute(
        arrived[ways - 1, :, 0:512], "ctx", [(i, i + 1) for i in range(blocks - 1)]
    )
    wide = sds((T, CW), F32)
    slim = sds((T, 128), F32)
    chunk = sds((blocks, T // blocks, 128), F32)
    ext = pltpu.VMEM((ROWS + T, 512), F32)

    step, cum, send = call(
        enter_kernel,
        [slim, slim, sds((blocks, 24, 128), F32)],
        "vvvss",
        scratch=[pltpu.VMEM((ROWS + T, 384), F32)],
    )(rows, conv_x, conv_b, head, where)
    received = ctx_swap(send)
    xbc, slopes, inside, kept, order = call(
        within_kernel,
        [sds((T, 512), BF), sds((T, 512), F32), wide, sds((HD, T, T), BF), sds((8, 128), F32)],
        "vvvvvsvv",
        scratch=[ext],
        flops=10**8,
        bytes_accessed=3 * 10**6,
    )(rows, halo, conv_x, conv_b, conv_c, where, step, cum)
    send, decays = call(
        scan_kernel,
        [chunk, chunk],
        "vvvsv",
        scratch=[pltpu.VMEM((CW, 128), F32)] + [pltpu.VMEM((blocks, 8, 128), F32)] * 2,
    )(received, conv_x, conv_b, where, order)
    carried = ctx_swap(send).reshape(T, 128)
    y, mixed, sums = call(
        mix_kernel, [wide, sds((T, CW), BF), sds((8, T), F32)], "vvvvvvss"
    )(carried, xbc, inside, cum, rows, gain, head, where)
    per = ways // GROUPS
    sums = lax.psum(
        sums, "head", axis_index_groups=[[g * per + i for i in range(per)] for g in range(GROUPS)]
    )
    y_grad, gate_grad, gain_grad, send = call(
        norm_kernel,
        [sds((T, CW), BF), sds((T, CW), BF), sds((8, CW), F32), chunk],
        "vvvvvvs",
    )(sums, mixed, rows, gain, xbc, cum, where)
    received = ctx_swap(send)
    middle, dots = call(
        back_kernel,
        [sds((T, 512), F32), sds((T + 8, 128), F32)],
        "vvvvvvv",
        flops=3 * 10**8,
        bytes_accessed=4 * 10**6,
    )(xbc, step, cum, kept, y, y_grad, carried)
    send = call(scan_back_kernel, [chunk], "vv")(received, decays)[0]
    end_grad = ctx_swap(send).reshape(T, 128)
    pre, dt_grad, send = call(
        leave_kernel,
        [sds((T, 512), F32), slim, sds((blocks, 32, 128), BF)],
        "vvvs" + "v" * 9,
        scratch=[ext],
    )(
        end_grad, rows, halo, head, xbc, step, cum, y_grad, middle, dots, carried, gain_grad, slopes,
    )
    received = ctx_swap(send)
    four = sds((HD,), F32)
    send, conv_x_grad, alog_grad, bias_grad, skip_sum = call(
        finish_kernel,
        [sds((ways, ROWS, OUT_W), BF), sds((KT, CW), F32), four, four, four],
        "vsvvvvvv",
        "vvsss",
        scratch=[pltpu.VMEM((T + 8, 512), F32)],
    )(received, where, conv_x, conv_b, conv_c, pre, dt_grad, gate_grad)
    received = head_swap(send)
    x_grad, b_grad, c_grad, dt_out, gate_out, conv_b_grad, conv_c_grad, gain_sum = call(
        unpack_kernel,
        [
            sds(x_in.shape, BF),
            sds(b_in.shape, BF),
            sds(c_in.shape, BF),
            sds(dt_in.shape, BF),
            sds(gate_in.shape, BF),
            sds(conv_b.shape, F32),
            sds(conv_c.shape, F32),
            sds((1, norm_gain.shape[0]), F32),
        ],
        "v",
    )(received)
    return (
        x_grad,
        b_grad,
        c_grad,
        dt_out,
        gate_out,
        conv_x_grad,
        conv_b_grad,
        conv_c_grad,
        alog_grad,
        bias_grad,
        skip_sum,
        gain_sum.reshape(-1),
    )


def solution(mesh):
    tokens = P(("ctx", "head"), None)
    return jax.shard_map(
        per_device,
        mesh=mesh,
        in_specs=(tokens,) * 6 + (P(None, "head"), P(), P(), P("head"), P("head"), P("head"), P()),
        out_specs=(tokens,) * 5
        + (P(None, "head"), P(), P(), P("head"), P("head"), P("head"), P()),
        check_vma=False,
    )
```

```python
import functools

import jax
import jax.numpy as jnp
from jax import lax
from jax.experimental import pallas as pl
from jax.experimental.pallas import tpu as pltpu
from jax.sharding import PartitionSpec as P

BF, F32 = jnp.bfloat16, jnp.float32
GROUPS = 8
N = 128
PS = 64
HD = 4
CW = 256
T = 256
KT = 4
ROWS = 16
IN_W = 1152
OUT_W = 896
BASE = 21
VMEM_LIMIT = 8 * 1024 * 1024
PACK_LIMIT = 60 * 1024 * 1024


def dot(a, b, ca, cb):
    return lax.dot_general(
        a, b, (((ca,), (cb,)), ((), ())), preferred_element_type=F32
    )


def pieces(a, count):
    out = []
    for _ in range(count - 1):
        head = a.astype(BF)
        out.append(head)
        a = a - head.astype(F32)
    return out + [a.astype(BF)]


def dot_parts(a, b, ca, cb, count):
    total = None
    for piece in pieces(a, count):
        term = dot(piece, b, ca, cb)
        total = term if total is None else total + term
    return total


def dot_right(a, b, ca, cb):
    high, low = pieces(b, 2)
    return dot(a, high, ca, cb) + dot(a, low, ca, cb)


def dot_both(a, b, ca, cb):
    a_high, a_low = pieces(a, 2)
    b_high, b_low = pieces(b, 2)
    return dot(a_high, b_high, ca, cb) + (dot(a_high, b_low, ca, cb) + dot(a_low, b_high, ca, cb))


def iota(shape, axis):
    return lax.broadcasted_iota(jnp.int32, shape, axis)


def spread(cols):
    low = iota((cols.shape[0], 128), 1) < PS
    halves = []
    for pair in range(HD // 2):
        first = jnp.broadcast_to(cols[:, 2 * pair : 2 * pair + 1], (cols.shape[0], 128))
        second = jnp.broadcast_to(cols[:, 2 * pair + 1 : 2 * pair + 2], (cols.shape[0], 128))
        halves.append(jnp.where(low, first, second))
    return jnp.concatenate(halves, axis=1)


def head_sums(wide):
    pick = (iota((CW, 128), 0) // PS == iota((CW, 128), 1)).astype(BF)
    return dot_parts(wide, pick, 1, 0, 3)


def scalar_row(ref, first, width, per):
    lane = iota((1, width), 1) // per
    row = jnp.zeros((1, width), F32)
    for e in range(HD):
        row = jnp.where(lane == e, ref[first + e], row)
    return row


def softplus(v):
    return jnp.maximum(v, 0.0) + jnp.log1p(jnp.exp(-jnp.abs(v)))


def rates(dt_cols, bias_row, alog_row):
    live = iota((T, 128), 1) < HD
    shifted = dt_cols + bias_row
    step = jnp.where(live, softplus(shifted), 0.0)
    logd = -jnp.exp(alog_row) * step
    tril = (iota((T, T), 0) >= iota((T, T), 1)).astype(BF)
    cum = sum(dot(tril, piece, 1, 0) for piece in pieces(logd, 3))
    return shifted, step, logd, cum


def taps(ext_ref, weight, lo, hi):
    total = None
    for k in range(KT):
        term = weight[k : k + 1, :] * ext_ref[ROWS - KT + 1 + k : ROWS - KT + 1 + k + T, lo:hi]
        total = term if total is None else total + term
    return total


def gap_decay(cum, cum_t, e):
    causal = iota((T, T), 0) >= iota((T, T), 1)
    gap = jnp.where(causal, cum[:, e : e + 1] - cum_t[e : e + 1, :], 0.0)
    return jnp.where(causal, jnp.exp(gap), 0.0)


def silu_slope(pre):
    gate = jax.nn.sigmoid(pre)
    return pre * gate, gate * (1.0 + pre * (1.0 - gate))


def enter_math(ext, dt_cols, wx, wb, bias_row, alog_row):
    def act(weight, lo, hi):
        pre = taps(ext, weight, lo, hi)
        return (pre * jax.nn.sigmoid(pre)).astype(BF)

    x_act, b_act = act(wx, 0, 256), act(wb, 256, 384)
    shifted, step, logd, cum = rates(dt_cols, bias_row, alog_row)
    final = cum[T - 1 : T, :]
    to_end = jnp.exp(final - cum) * step
    wide_end = spread(to_end)
    late = iota((T, CW), 0) >= KT - 1
    weighted = jnp.where(late, x_act.astype(F32) * wide_end, 0.0)
    fresh = dot_parts(weighted, b_act, 0, 0, 2)
    return step, cum, fresh, wide_end[0:8], spread(jnp.broadcast_to(final, (8, 128)))


def within_math(x_act, b_act, c_act, step, cum, cum_t):
    scores = dot(c_act, b_act, 1, 1)
    stepped = x_act.astype(F32) * spread(step)
    outs = []
    for e in range(HD):
        mix = (scores * gap_decay(cum, cum_t, e)).astype(BF)
        part = stepped[:, e * PS : (e + 1) * PS]
        high, low = pieces(part, 2)
        both = dot(mix, jnp.concatenate([high, low], axis=1), 1, 0)
        outs.append(both[:, :PS] + both[:, PS:])
    return jnp.concatenate(outs, axis=1)


def rim_rows(columns):
    x_rim = columns.T[0:8]
    lane = iota((8, 128), 1)
    both = jnp.zeros((8, 128), F32)
    for i in range(T // 8):
        part = pltpu.roll(columns[8 * i : 8 * i + 8], (4 * i + 4 - BASE) % 128, 1)
        both = jnp.where(lane // 4 == i, part, both)
    return jnp.concatenate([x_rim, both, pltpu.roll(both, 5, 0)], axis=1)


def spread_eight(cols):
    lane = iota(cols.shape, 1)
    out = jnp.zeros(cols.shape, F32)
    for e in range(HD):
        out = jnp.where(lane // 8 == e, jnp.broadcast_to(cols[:, e : e + 1], cols.shape), out)
    return out


def early_math(x_first, b_first, c_act, step, cum):
    lane, row = iota((T, 128), 1), iota((T, 128), 0)
    b_rows = jnp.concatenate([b_first] * HD + [jnp.zeros((128 - 8 * HD, 128), F32)], axis=0)
    scores = dot(c_act, b_rows.astype(BF), 1, 1)
    at_first = spread_eight(cum[0:8])
    at_first = jnp.sum(
        jnp.where(iota((8, 128), 0) == iota((8, 128), 1) % 8, at_first, 0.0), axis=0, keepdims=True
    )
    use = (lane % 8 < KT - 1) & (lane < 8 * HD) & (row >= lane % 8)
    gap = jnp.where(use, spread_eight(cum) - at_first, 0.0)
    mix = jnp.where(use, scores * jnp.exp(gap), 0.0).astype(BF)
    stepped = x_first * spread(step[0:8])
    blocks = jnp.concatenate([stepped] * HD + [jnp.zeros((128 - 8 * HD, CW), F32)], axis=0)
    blocks = jnp.where(iota((128, CW), 0) // 8 == iota((128, CW), 1) // PS, blocks, 0.0)
    return dot_right(mix, blocks, 1, 0)


def norm_math(mixed, gate, out_grad, gain, squares, along, c_act, cum):
    gate_act, gate_slope = silu_slope(gate)
    mixed = mixed.astype(F32)
    v = mixed * gate_act
    inv = lax.rsqrt(squares * (1.0 / (2 * CW)) + 1e-05)
    normed = v * inv
    v_grad = inv * (out_grad * gain - normed * (along * inv * (1.0 / (2 * CW))))
    y_grad = (v_grad * gate_act).astype(BF)
    gate_grad = (v_grad * mixed * gate_slope).astype(BF)
    gain_grad = jnp.sum(out_grad * normed, axis=0, keepdims=True)
    grown = spread(jnp.exp(cum))
    lifted = y_grad.astype(F32) * grown
    start_grad = dot_parts(lifted, c_act, 0, 0, 2)
    return y_grad, gate_grad, gain_grad, start_grad


def within_back_math(x_act, b_act, c_act, step, cum, cum_t, y, y_grad, carried):
    lifted = y_grad.astype(F32) * spread(jnp.exp(cum))
    scores = dot(c_act, b_act, 1, 1)
    score_grad = jnp.zeros((T, T), F32)
    x_parts = []
    step_t = step.T
    for e in range(HD):
        cut = slice(e * PS, (e + 1) * PS)
        decay = gap_decay(cum, cum_t, e)
        x_parts.append(dot((scores * decay).astype(BF), y_grad[:, cut], 0, 0))
        mix_grad = dot(y_grad[:, cut], x_act[:, cut], 1, 1)
        score_grad = score_grad + mix_grad * (decay * step_t[e : e + 1, :])
    x_in = jnp.concatenate(x_parts, axis=1)
    score_grad = score_grad.astype(BF)
    c_grad = dot(score_grad, b_act, 1, 0) + dot_both(lifted, carried, 1, 0)
    b_in = dot(score_grad, c_act, 0, 0)
    dy = y_grad.astype(F32)
    x32 = x_act.astype(F32)
    out_dots = head_sums(dy * y)
    in_dots = head_sums(x32 * x_in)
    skip_grad = jnp.sum(dy * x32, axis=0, keepdims=True)
    return x_in, b_in, c_grad, out_dots, in_dots, skip_grad


def leave_math(x_act, b_act, step, cum, shifted, logd, alog_row, skip_row, y_grad, x_in, b_in, out_dots, in_dots, carried, end_grad):
    final = cum[T - 1 : T, :]
    tail = jnp.exp(final - cum)
    x32 = x_act.astype(F32)
    end_b = end_grad.astype(BF)
    x_state = spread(tail) * dot(b_act, end_b, 1, 1)
    state_dots = head_sums(x32 * x_state)
    wide_step = spread(step)
    x_grad = wide_step * (x_in + x_state) + skip_row * y_grad.astype(F32)
    weighted = (x32 * spread(tail * step)).astype(BF)
    b_grad = b_in + dot(weighted, end_b, 1, 0)
    pull = step * state_dots
    cum_grad = out_dots - step * in_dots - pull
    kept_dots = jnp.sum(carried * end_grad, axis=1, keepdims=True)
    lane = iota((1, 128), 1)
    over = jnp.zeros((1, 128), F32)
    for e in range(HD):
        over = jnp.where(lane == e, jnp.sum(kept_dots[e * PS : (e + 1) * PS, :], axis=0, keepdims=True), over)
    final_grad = jnp.sum(pull, axis=0, keepdims=True) + jnp.exp(final) * over
    triu = (iota((T, T), 0) <= iota((T, T), 1)).astype(BF)
    log_grad = sum(dot(triu, piece, 1, 0) for piece in pieces(cum_grad, 3)) + final_grad
    step_grad = in_dots + state_dots - jnp.exp(alog_row) * log_grad
    alog_grad = jnp.sum(log_grad * logd, axis=0, keepdims=True)
    live = iota((T, 128), 1) < HD
    dt_grad = jnp.where(live, step_grad * jax.nn.sigmoid(shifted), 0.0)
    bias_grad = jnp.sum(dt_grad, axis=0, keepdims=True)
    return x_grad, b_grad, dt_grad, alog_grad, bias_grad


def weight_grads(ext, pre_grad):
    return [
        jnp.sum(pre_grad * ext[ROWS - KT + 1 + k : ROWS - KT + 1 + k + T], axis=0, keepdims=True)
        for k in range(KT)
    ]


def conv_back(pre_ext, weight, lo, hi):
    total = None
    for k in range(KT):
        term = weight[k : k + 1, :] * pre_ext[KT - 1 - k : KT - 1 - k + T, lo:hi]
        total = term if total is None else total + term
    return total


def call(kernel, out_shape, in_specs, out_specs=None, scratch=(), flops=0, bytes_accessed=0, limit=VMEM_LIMIT):
    place = {
        "v": pl.BlockSpec(memory_space=pltpu.VMEM),
        "s": pl.BlockSpec(memory_space=pltpu.SMEM),
        "h": pl.BlockSpec(memory_space=pltpu.HBM),
    }
    return pl.pallas_call(
        kernel,
        out_shape=out_shape,
        in_specs=[place[c] for c in in_specs],
        out_specs=[place[c] for c in (out_specs or "v" * len(out_shape))],
        scratch_shapes=list(scratch),
        compiler_params=pltpu.CompilerParams(vmem_limit_bytes=limit),
        cost_estimate=pl.CostEstimate(
            flops=flops, bytes_accessed=bytes_accessed, transcendentals=0
        ),
    )


def sds(shape, dtype):
    return jax.ShapeDtypeStruct(shape, dtype)


def pack_kernel(x_at, b_at, c_at, dt_at, gate_at, grad_at, out, x, b, c, dt, gate, out_grad, sems):
    moves = [
        pltpu.make_async_copy(source, target, sems.at[i])
        for i, (source, target) in enumerate(
            [(x_at, x), (b_at, b), (c_at, c), (dt_at, dt), (gate_at, gate), (grad_at, out_grad)]
        )
    ]
    for move in moves:
        move.start()
    ways = out.shape[0]
    per = GROUPS * N // ways
    for move, ref, lo in ((moves[0], x, 0), (moves[4], gate, 512), (moves[5], out_grad, 768)):
        move.wait()
        for j in range(ways):
            out[j, :, lo : lo + CW] = ref[:, j * CW : (j + 1) * CW]
    for move, ref, lo in ((moves[1], b, 256), (moves[2], c, 384)):
        move.wait()
        for j in range(ways):
            g = (j * per) // N
            out[j, :, lo : lo + N] = ref[:, g * N : (g + 1) * N]
    moves[3].wait()
    wide_dt = jnp.concatenate(
        [dt[...].astype(F32), jnp.zeros((ROWS, 128 - dt.shape[1]), F32)], axis=1
    )
    lane = iota((ROWS, 128), 1)
    for j in range(ways):
        turned = pltpu.roll(wide_dt, (128 - HD * j) % 128, 1)
        out[j, :, 1024:1152] = jnp.where(lane < HD, turned, 0.0).astype(BF)


def group_lanes(ref, where):
    return ref[:, pl.ds(pl.multiple_of(where[1] * N, N), N)]


def gain_lanes(ref, where):
    return ref[:, pl.ds(pl.multiple_of(where[0] * CW, CW), CW)]


def head_column(row):
    return jnp.concatenate(
        [jnp.broadcast_to(row[:, e : e + 1], (PS, 128)) for e in range(HD)], axis=0
    )


def enter_kernel(rows, wx, wb, head, where, step_out, cum_out, send, ext):
    ext[0:ROWS] = jnp.zeros((ROWS, 384), F32)
    ext[ROWS : ROWS + T] = rows[:, 0:384].astype(F32)
    step, cum, fresh, first_end, final = enter_math(
        ext,
        rows[:, 1024:1152].astype(F32),
        wx[...],
        group_lanes(wb, where),
        scalar_row(head, HD, 128, 1),
        scalar_row(head, 0, 128, 1),
    )
    step_out[...] = step
    cum_out[...] = cum
    count = send.shape[0]
    lane, row = iota((8, 128), 1), iota((8, 128), 0)
    first = ext[ROWS : ROWS + 8]
    end = rows[T - ROWS : T, 256:512].astype(F32)[8:16]
    last = pltpu.roll(ext[ROWS + T - 8 : ROWS + T], 6, 0)
    rim = jnp.where(iota((8, 384), 0) < 3, first, last)
    end_high = first_end.astype(BF).astype(F32)
    final_parts = [piece.astype(F32) for piece in pieces(final, 3)]
    wide_row = iota((8, CW), 0)
    ends = jnp.where(wide_row < 3, end_high, pltpu.roll(first_end - end_high, 3, 0))
    ends = jnp.where(wide_row == 6, final_parts[0], jnp.where(wide_row == 7, final_parts[1], ends))
    columns = jnp.concatenate(
        [rim[:, 0:CW], ends, final_parts[2], jnp.zeros((104, CW), F32)], axis=0
    ).T
    both = jnp.where(row < 3, pltpu.roll(end, 3, 0)[:, 0:128], pltpu.roll(end, 6, 0)[:, 128:256])
    b_rim = rim[:, 256:384]
    b_part = b_rim
    for t in range(3):
        moved = pltpu.roll(b_rim, BASE * (t + 1), 1)
        there = lane // BASE == t + 1
        b_part = jnp.where((row == 6) & there, moved[t : t + 1], b_part)
        b_part = jnp.where((row == 7) & there, moved[t + 3 : t + 4], b_part)
    tiles = []
    for i in range(count):
        part = pltpu.roll(both, (BASE - 4 - 4 * i) % 128, 1)
        tile = jnp.where(lane < BASE - 4, columns[8 * i : 8 * i + 8], part)
        tiles.append(jnp.where(lane < BASE, tile, b_part)[None])
    high = fresh.astype(BF).astype(F32)
    shape = (count, 8, 128)
    send[...] = jnp.concatenate(
        [high.reshape(shape), (fresh - high).reshape(shape), jnp.concatenate(tiles, axis=0)], axis=1
    ).astype(BF)


def conv_rows(ext, wx, wb, wc, where):
    for weight, lo, hi in (
        (wx[...], 0, 256),
        (group_lanes(wb, where), 256, 384),
        (group_lanes(wc, where), 384, 512),
    ):
        yield lo, hi, taps(ext, weight, lo, hi)


def within_kernel(rows, wx, wb, wc, where, step, cum, after, xbc, inside, ext):
    del after
    ext[0:ROWS] = jnp.zeros((ROWS, 512), F32)
    ext[ROWS : ROWS + T] = rows[:, 0:512].astype(F32)
    acts = []
    for lo, hi, pre in conv_rows(ext, wx, wb, wc, where):
        late = iota((T, hi - lo), 0) >= KT - 1
        acts.append(jnp.where(late, pre * jax.nn.sigmoid(pre), 0.0).astype(BF))
        xbc[:, lo:hi] = acts[-1]
    step, cum = step[...], cum[...]
    inside[...] = within_math(*acts, step, cum, cum.T)


def scan_kernel(received, wx, wb, where, send, decays, columns, fresh, states):
    count = received.shape[0]
    columns[...] = jnp.concatenate([wx[...], jnp.zeros((128 - KT, CW), F32)], axis=0).T
    mine = columns[pl.ds(pl.multiple_of(where[2] * 8, 8), 8), :]
    taps_b = group_lanes(wb, where)
    shape = (count, 8, 128)
    lane, row = iota(shape, 2), iota(shape, 1)
    message = received[...].astype(F32)
    x_rim = message[:, 16:24]
    low = x_rim
    for t in range(3):
        moved = pltpu.roll(x_rim, 128 - BASE * (t + 1), 2)
        low = jnp.where(row == t, moved[:, 6:7], jnp.where(row == t + 3, moved[:, 7:8], low))
    b_rim = jnp.where(lane < BASE, low, x_rim)
    blank = jnp.zeros((1, 8, 128), F32)
    x_last = jnp.concatenate([blank, x_rim[:-1]], axis=0)
    b_last = jnp.concatenate([blank, b_rim[:-1]], axis=0)
    x_seen = jnp.where(lane < 3, pltpu.roll(x_last, 125, 2), pltpu.roll(x_rim, 3, 2))
    b_seen = jnp.where(row < 3, pltpu.roll(b_last, 5, 1), pltpu.roll(b_rim, 3, 1))
    x_pre = mine[None, :, 0:1] * x_seen
    b_pre = taps_b[None, 0:1] * b_seen
    for k in range(1, KT):
        x_pre = x_pre + mine[None, :, k : k + 1] * pltpu.roll(x_seen, 128 - k, 2)
        b_pre = b_pre + taps_b[None, k : k + 1] * pltpu.roll(b_seen, 8 - k, 1)
    to_end = pltpu.roll(x_rim, 120, 2) + pltpu.roll(x_rim, 117, 2)
    x_act = (x_pre * jax.nn.sigmoid(x_pre)).astype(BF).astype(F32) * to_end
    b_act = (b_pre * jax.nn.sigmoid(b_pre)).astype(BF).astype(F32)
    total = message[:, 0:8] + message[:, 8:16]
    for t in range(KT - 1):
        total = total + x_act[:, :, t : t + 1] * b_act[:, t : t + 1, :]
    fresh[...] = total
    final = x_rim[:, :, 14:15] + x_rim[:, :, 15:16] + x_rim[:, :, 16:17]
    decays[...] = jnp.exp(jnp.broadcast_to(final, shape))
    state = jnp.zeros((8, 128), F32)
    for i in range(count):
        states[i] = state
        state = decays[i] * state + fresh[i]
    state = states[...]
    high = state.astype(BF).astype(F32)
    back = jnp.where(lane < 3, x_seen, x_last)
    send[...] = jnp.concatenate([high, state - high, back], axis=1).astype(BF)


def scan_back_kernel(received, decays, send, states):
    message = received[...].astype(F32)
    state = jnp.zeros((8, 128), F32)
    for i in reversed(range(received.shape[0])):
        states[i] = state
        state = decays[i] * state + message[i]
    send[...] = states[...].astype(BF)


def pair_rows(squares, along):
    lane = iota((T, 128), 1)
    both = jnp.where(lane == 0, squares, jnp.where(lane == 1, along, 0.0))
    return both.T[0:8, :]


def mix_kernel(
    received, xbc_late, inside, step, cum, rows, wx, wb, wc, gain, head, where,
    y_out, mixed_out, message, xbc, carried_out, rim_out,
):
    arrived = received[...].astype(F32)
    carried = (arrived[:, 0:8] + arrived[:, 8:16]).reshape(T, 128)
    carried_out[...] = carried
    rim = rim_rows(arrived[:, 16:24].reshape(T, 128))
    rim_out[...] = rim
    raw = rows[0:ROWS, 0:512].astype(F32)[0:8]
    seen = jnp.where(iota((8, 512), 0) < 3, rim, pltpu.roll(raw, 3, 0))
    weights = jnp.concatenate([wx[...], group_lanes(wb, where), group_lanes(wc, where)], axis=1)
    pre = weights[0:1] * seen
    for k in range(1, KT):
        pre = pre + weights[k : k + 1] * pltpu.roll(seen, 8 - k, 0)
    first = jnp.where(iota((8, 512), 0) < 3, pre * jax.nn.sigmoid(pre), 0.0).astype(BF).astype(F32)
    late = xbc_late[...]
    whole = jnp.concatenate([(late[0:ROWS].astype(F32) + jnp.concatenate([first, jnp.zeros((8, 512), F32)], axis=0)).astype(BF), late[ROWS:T]], axis=0)
    xbc[...] = whole
    x_act, c_act = whole[:, 0:256], whole[:, 384:512]
    cum = cum[...]
    early = early_math(first[:, 0:256], first[:, 256:384], c_act, step[...], cum)
    grown = spread(jnp.exp(cum))
    y = inside[...] + early + grown * dot_right(c_act, carried, 1, 1)
    mixed = (y + scalar_row(head, 2 * HD, CW, PS) * x_act.astype(F32)).astype(BF)
    gate = rows[:, 512:768].astype(F32)
    v = mixed.astype(F32) * (gate * jax.nn.sigmoid(gate))
    scaled = rows[:, 768:1024].astype(F32) * gain_lanes(gain, where)
    y_out[...] = y
    mixed_out[...] = mixed
    message[...] = pair_rows(
        jnp.sum(v * v, axis=1, keepdims=True), jnp.sum(scaled * v, axis=1, keepdims=True)
    )


def norm_kernel(message, mixed, rows, gain, xbc, cum, where, y_grad_out, gate_out, gain_out, send):
    sums = jnp.concatenate([message[...], jnp.zeros((120, T), F32)], axis=0).T
    y_grad, gate_grad, gain_grad, start_grad = norm_math(
        mixed[...],
        rows[:, 512:768].astype(F32),
        rows[:, 768:1024].astype(F32),
        gain_lanes(gain, where),
        sums[:, 0:1],
        sums[:, 1:2],
        xbc[:, 384:512],
        cum[...],
    )
    y_grad_out[...] = y_grad
    gate_out[...] = gate_grad
    gain_out[...] = jnp.broadcast_to(gain_grad, (8, CW))
    send[...] = start_grad.reshape(send.shape).astype(BF)


def place_rim(ext, rim):
    ext[0:8] = jnp.zeros((8, ext.shape[1]), F32)
    ext[8:ROWS] = pltpu.roll(rim, 5, 0)


def back_kernel(
    rows, rim, wx, wb, wc, where, xbc, step, cum, y, y_grad, carried, middle, dots, slopes, ext
):
    place_rim(ext, rim[...])
    ext[ROWS : ROWS + T] = rows[:, 0:512].astype(F32)
    for lo, hi, pre in conv_rows(ext, wx, wb, wc, where):
        slopes[:, lo:hi] = silu_slope(pre)[1]
    cum = cum[...]
    x_in, b_in, c_grad, out_dots, in_dots, skip_grad = within_back_math(
        xbc[:, 0:256],
        xbc[:, 256:384],
        xbc[:, 384:512],
        step[...],
        cum,
        cum.T,
        y[...],
        y_grad[...],
        carried[...],
    )
    middle[:, 0:256] = x_in
    middle[:, 256:384] = b_in
    middle[:, 384:512] = c_grad
    dots[0:T] = out_dots + pltpu.roll(in_dots, 64, 1)
    dots[T : T + 8] = head_sums(jnp.broadcast_to(skip_grad, (8, CW)))


def leave_kernel(
    end_grad, rows, rim, head, xbc, step, cum, y_grad, middle, dots, carried, gain_grad, slopes,
    pre_out, dt_out, send, ext,
):
    place_rim(ext, rim[...])
    ext[ROWS : ROWS + T] = rows[:, 0:512].astype(F32)
    alog_row = scalar_row(head, 0, 128, 1)
    step = step[...]
    both = dots[0:T]
    live = iota((T, 128), 1) < HD
    x_grad, b_grad, dt_grad, alog_grad, bias_grad = leave_math(
        xbc[:, 0:256],
        xbc[:, 256:384],
        step,
        cum[...],
        rows[:, 1024:1152].astype(F32) + scalar_row(head, HD, 128, 1),
        -jnp.exp(alog_row) * step,
        alog_row,
        scalar_row(head, 2 * HD, CW, PS),
        y_grad[...],
        middle[:, 0:256],
        middle[:, 256:384],
        jnp.where(live, both, 0.0),
        jnp.where(live, pltpu.roll(both, 64, 1), 0.0),
        carried[...],
        end_grad[...].astype(F32),
    )
    dt_out[...] = dt_grad
    pre = jnp.concatenate([x_grad, b_grad, middle[:, 384:512]], axis=1) * slopes[...]
    pre_out[...] = pre
    weights = jnp.concatenate(weight_grads(ext, pre), axis=0)
    sums = jnp.concatenate([alog_grad, bias_grad, dots[T : T + 1], jnp.zeros((5, 128), F32)], axis=0)
    line = sums[0:1] + pltpu.roll(sums, 32, 1)[1:2] + pltpu.roll(sums, 64, 1)[2:3]
    coarse = line.astype(BF).astype(F32)
    block = jnp.concatenate(
        [weights[:, i * 128 : (i + 1) * 128] for i in range(4)]
        + [gain_grad[0:1, 0:128], gain_grad[0:1, 128:256], coarse, line - coarse]
        + [pre[0:3, i * 128 : (i + 1) * 128] for i in range(4)],
        axis=0,
    ).astype(BF)
    for i in range(send.shape[0]):
        send[i] = block


def finish_kernel(received, where, wx, wb, wc, pre, dt_grad, gate_grad, send, conv_x_out, alog_out, bias_out, skip_out, ext):
    count = received.shape[0]
    total = received[0].astype(F32)
    for i in range(1, count):
        total = total + received[i].astype(F32)
    line = total[18:19] + total[19:20]
    after = where[2] + 1
    next_block = received[jnp.minimum(after, count - 1)].astype(F32)
    following = jnp.concatenate(
        [next_block[20 + 3 * i : 23 + 3 * i] for i in range(4)], axis=1
    )
    ext[0:T] = pre[...]
    ext[T : T + 3] = jnp.where(after < count, following, 0.0)
    x_grad = conv_back(ext, wx[...], 0, 256).astype(BF)
    b_grad = conv_back(ext, group_lanes(wb, where), 256, 384).astype(BF)
    c_grad = conv_back(ext, group_lanes(wc, where), 384, 512).astype(BF)
    conv_x_out[...] = jnp.concatenate([total[0:4], total[4:8]], axis=1)
    for e in range(HD):
        alog_out[e] = jnp.sum(line[:, e : e + 1])
        bias_out[e] = jnp.sum(line[:, 32 + e : 33 + e])
        skip_out[e] = jnp.sum(line[:, 64 + e : 65 + e])
    dt_low = dt_grad[...].astype(BF)
    lane, row = iota((128, 128), 1), iota((128, 128), 0)
    apart = dot(dt_low, ((lane // ROWS == row) & (row < HD)).astype(BF), 1, 0)
    apart = jnp.where(iota((T, 128), 0) % ROWS == iota((T, 128), 1) % ROWS, apart, 0.0).astype(BF)
    ways = send.shape[0]
    joined = dot((iota((ways, T), 1) // ROWS == iota((ways, T), 0)).astype(BF), apart, 1, 0)
    shared = jnp.concatenate([total[8:18], jnp.zeros((6, 128), F32)], axis=0)
    row = iota((ROWS, 128), 0)
    for j in range(ways):
        cut = slice(j * ROWS, (j + 1) * ROWS)
        send[j, :, 0:256] = x_grad[cut]
        send[j, :, 256:384] = b_grad[cut]
        send[j, :, 384:512] = c_grad[cut]
        send[j, :, 512:768] = gate_grad[cut, :]
        send[j, :, 768:896] = jnp.where(row == 10, joined[j : j + 1], shared).astype(BF)


def unpack_kernel(received, x_out, b_out, c_out, dt_out, gate_out, conv_b_out, conv_c_out, gain_out):
    ways = received.shape[0]
    shared, lines = [], []
    for j in range(ways):
        own = slice(j * CW, (j + 1) * CW)
        x_out[:, own] = received[j, :, 0:256]
        gate_out[:, own] = received[j, :, 512:768]
        shared.append(received[j, :, 768:896].astype(F32))
        lines.append(shared[j][10:11])
        gain_out[:, own] = jnp.concatenate([shared[j][8:9], shared[j][9:10]], axis=1)
    lines = jnp.concatenate(lines, axis=0)
    heads = dt_out.shape[1]
    dt = jnp.zeros((ROWS, heads), F32)
    for e in range(HD):
        place = (iota((ways, heads), 1) == HD * iota((ways, heads), 0) + e).astype(BF)
        dt = dt + dot(lines[:, e * ROWS : (e + 1) * ROWS].astype(BF), place, 0, 0)
    dt_out[...] = dt.astype(BF)
    per = ways // GROUPS
    for g in range(GROUPS):
        cut = slice(g * N, (g + 1) * N)
        b_sum, c_sum, w_sum = 0.0, 0.0, 0.0
        for j in range(g * per, (g + 1) * per):
            b_sum = b_sum + received[j, :, 256:384].astype(F32)
            c_sum = c_sum + received[j, :, 384:512].astype(F32)
            w_sum = w_sum + shared[j]
        b_out[:, cut] = b_sum.astype(BF)
        c_out[:, cut] = c_sum.astype(BF)
        conv_b_out[:, cut] = w_sum[0:KT]
        conv_c_out[:, cut] = w_sum[KT : 2 * KT]


def per_device(
    x_in, b_in, c_in, dt_in, gate_in, out_grad, conv_x, conv_b, conv_c, a_log, dt_bias, d_skip, norm_gain
):
    ways = lax.axis_size("head")
    blocks = lax.axis_size("ctx")
    head_at = lax.axis_index("head")
    where = jnp.stack([head_at, (head_at * GROUPS) // ways, lax.axis_index("ctx")]).astype(jnp.int32)
    head = jnp.concatenate([a_log, dt_bias, d_skip])
    gain = norm_gain.reshape(1, -1)

    def ctx_swap(value):
        return lax.all_to_all(value, "ctx", 0, 0, tiled=True)

    def head_swap(value):
        return lax.all_to_all(value, "head", 0, 0, tiled=True)

    inputs = (x_in, b_in, c_in, dt_in, gate_in, out_grad)
    sent = call(
        pack_kernel,
        [sds((ways, ROWS, IN_W), BF)],
        "hhhhhh",
        scratch=[pltpu.VMEM(a.shape, a.dtype) for a in inputs] + [pltpu.SemaphoreType.DMA((6,))],
        limit=PACK_LIMIT,
    )(*inputs)[0]
    arrived = head_swap(sent)
    rows = arrived.reshape(T, IN_W)
    wide = sds((T, CW), F32)
    slim = sds((T, 128), F32)
    chunk = sds((blocks, T // blocks, 128), F32)
    half_chunk = sds((blocks, T // blocks, 128), BF)
    ext = pltpu.VMEM((ROWS + T, 512), F32)

    step, cum, send = call(
        enter_kernel,
        [slim, slim, sds((blocks, 24, 128), BF)],
        "vvvss",
        scratch=[pltpu.VMEM((ROWS + T, 384), F32)],
    )(rows, conv_x, conv_b, head, where)
    received = ctx_swap(send)
    send, decays = call(
        scan_kernel,
        [sds((blocks, 24, 128), BF), chunk],
        "vvvs",
        scratch=[pltpu.VMEM((CW, 128), F32)] + [pltpu.VMEM((blocks, 8, 128), F32)] * 2,
    )(received, conv_x, conv_b, where)
    received = ctx_swap(send)
    xbc, inside = call(
        within_kernel,
        [sds((T, 512), BF), wide],
        "vvvvsvvv",
        scratch=[ext],
        flops=10**8,
        bytes_accessed=3 * 10**6,
    )(rows, conv_x, conv_b, conv_c, where, step, cum, decays)
    y, mixed, sums, xbc, carried, rim = call(
        mix_kernel,
        [wide, sds((T, CW), BF), sds((8, T), F32), sds((T, 512), BF), slim, sds((8, 512), F32)],
        "vvvvvvvvvvss",
    )(received, xbc, inside, step, cum, rows, conv_x, conv_b, conv_c, gain, head, where)
    per = ways // GROUPS
    sums = lax.psum(
        sums, "head", axis_index_groups=[[g * per + i for i in range(per)] for g in range(GROUPS)]
    )
    y_grad, gate_grad, gain_grad, send = call(
        norm_kernel,
        [sds((T, CW), BF), sds((T, CW), BF), sds((8, CW), F32), half_chunk],
        "vvvvvvs",
    )(sums, mixed, rows, gain, xbc, cum, where)
    received = ctx_swap(send)
    middle, dots, slopes = call(
        back_kernel,
        [sds((T, 512), F32), sds((T + 8, 128), F32), sds((T, 512), F32)],
        "vvvvvsvvvvvv",
        scratch=[ext],
        flops=3 * 10**8,
        bytes_accessed=4 * 10**6,
    )(rows, rim, conv_x, conv_b, conv_c, where, xbc, step, cum, y, y_grad, carried)
    send = call(
        scan_back_kernel, [half_chunk], "vv", scratch=[pltpu.VMEM((blocks, 8, 128), F32)]
    )(received, decays)[0]
    end_grad = ctx_swap(send).reshape(T, 128)
    pre, dt_grad, send = call(
        leave_kernel,
        [sds((T, 512), F32), slim, sds((blocks, 32, 128), BF)],
        "vvvs" + "v" * 9,
        scratch=[ext],
    )(
        end_grad, rows, rim, head, xbc, step, cum, y_grad, middle, dots, carried, gain_grad, slopes,
    )
    received = ctx_swap(send)
    four = sds((HD,), F32)
    send, conv_x_grad, alog_grad, bias_grad, skip_sum = call(
        finish_kernel,
        [sds((ways, ROWS, OUT_W), BF), sds((KT, CW), F32), four, four, four],
        "vsvvvvvv",
        "vvsss",
        scratch=[pltpu.VMEM((T + 8, 512), F32)],
    )(received, where, conv_x, conv_b, conv_c, pre, dt_grad, gate_grad)
    received = head_swap(send)
    x_grad, b_grad, c_grad, dt_out, gate_out, conv_b_grad, conv_c_grad, gain_sum = call(
        unpack_kernel,
        [
            sds(x_in.shape, BF),
            sds(b_in.shape, BF),
            sds(c_in.shape, BF),
            sds(dt_in.shape, BF),
            sds(gate_in.shape, BF),
            sds(conv_b.shape, F32),
            sds(conv_c.shape, F32),
            sds((1, norm_gain.shape[0]), F32),
        ],
        "v",
    )(received)
    return (
        x_grad,
        b_grad,
        c_grad,
        dt_out,
        gate_out,
        conv_x_grad,
        conv_b_grad,
        conv_c_grad,
        alog_grad,
        bias_grad,
        skip_sum,
        gain_sum.reshape(-1),
    )


def solution(mesh):
    tokens = P(("ctx", "head"), None)
    return jax.shard_map(
        per_device,
        mesh=mesh,
        in_specs=(tokens,) * 6 + (P(None, "head"), P(), P(), P("head"), P("head"), P("head"), P()),
        out_specs=(tokens,) * 5
        + (P(None, "head"), P(), P(), P("head"), P("head"), P("head"), P()),
        check_vma=False,
    )
```

```python
import functools

import jax
import jax.numpy as jnp
from jax import lax
from jax.experimental import pallas as pl
from jax.experimental.pallas import tpu as pltpu
from jax.sharding import PartitionSpec as P

BF, F32 = jnp.bfloat16, jnp.float32
GROUPS = 8
N = 128
PS = 64
HD = 4
CW = 256
T = 256
KT = 4
ROWS = 16
IN_W = 1152
OUT_W = 896
BASE = 21
VMEM_LIMIT = 8 * 1024 * 1024
PACK_LIMIT = 60 * 1024 * 1024


def dot(a, b, ca, cb):
    return lax.dot_general(
        a, b, (((ca,), (cb,)), ((), ())), preferred_element_type=F32
    )


def pieces(a, count):
    out = []
    for _ in range(count - 1):
        head = a.astype(BF)
        out.append(head)
        a = a - head.astype(F32)
    return out + [a.astype(BF)]


def dot_parts(a, b, ca, cb, count):
    total = None
    for piece in pieces(a, count):
        term = dot(piece, b, ca, cb)
        total = term if total is None else total + term
    return total


def dot_right(a, b, ca, cb):
    high, low = pieces(b, 2)
    return dot(a, high, ca, cb) + dot(a, low, ca, cb)


def dot_both(a, b, ca, cb):
    a_high, a_low = pieces(a, 2)
    b_high, b_low = pieces(b, 2)
    return dot(a_high, b_high, ca, cb) + (dot(a_high, b_low, ca, cb) + dot(a_low, b_high, ca, cb))


def iota(shape, axis):
    return lax.broadcasted_iota(jnp.int32, shape, axis)


def spread(cols):
    low = iota((cols.shape[0], 128), 1) < PS
    halves = []
    for pair in range(HD // 2):
        first = jnp.broadcast_to(cols[:, 2 * pair : 2 * pair + 1], (cols.shape[0], 128))
        second = jnp.broadcast_to(cols[:, 2 * pair + 1 : 2 * pair + 2], (cols.shape[0], 128))
        halves.append(jnp.where(low, first, second))
    return jnp.concatenate(halves, axis=1)


def head_sums(wide, count=3):
    pick = (iota((CW, 128), 0) // PS == iota((CW, 128), 1)).astype(BF)
    return dot_parts(wide, pick, 1, 0, count)


def scalar_row(ref, first, width, per):
    lane = iota((1, width), 1) // per
    row = jnp.zeros((1, width), F32)
    for e in range(HD):
        row = jnp.where(lane == e, ref[first + e], row)
    return row


def softplus(v):
    return jnp.maximum(v, 0.0) + jnp.log1p(jnp.exp(-jnp.abs(v)))


def rates(dt_cols, bias_row, alog_row):
    live = iota((T, 128), 1) < HD
    shifted = dt_cols + bias_row
    step = jnp.where(live, softplus(shifted), 0.0)
    logd = -jnp.exp(alog_row) * step
    tril = (iota((T, T), 0) >= iota((T, T), 1)).astype(BF)
    cum = sum(dot(tril, piece, 1, 0) for piece in pieces(logd, 3))
    return shifted, step, logd, cum


def taps(ext_ref, weight, lo, hi):
    total = None
    for k in range(KT):
        term = weight[k : k + 1, :] * ext_ref[ROWS - KT + 1 + k : ROWS - KT + 1 + k + T, lo:hi]
        total = term if total is None else total + term
    return total


def gap_decay(cum, cum_t, e):
    causal = iota((T, T), 0) >= iota((T, T), 1)
    gap = jnp.where(causal, cum[:, e : e + 1] - cum_t[e : e + 1, :], 0.0)
    return jnp.where(causal, jnp.exp(gap), 0.0)


def silu_slope(pre):
    gate = jax.nn.sigmoid(pre)
    return pre * gate, gate * (1.0 + pre * (1.0 - gate))


def enter_math(ext, dt_cols, wx, wb, bias_row, alog_row):
    def act(weight, lo, hi):
        pre = taps(ext, weight, lo, hi)
        return (pre * jax.nn.sigmoid(pre)).astype(BF)

    x_act, b_act = act(wx, 0, 256), act(wb, 256, 384)
    shifted, step, logd, cum = rates(dt_cols, bias_row, alog_row)
    final = cum[T - 1 : T, :]
    to_end = jnp.exp(final - cum) * step
    wide_end = spread(to_end)
    late = iota((T, CW), 0) >= KT - 1
    weighted = jnp.where(late, x_act.astype(F32) * wide_end, 0.0)
    fresh = dot_parts(weighted, b_act, 0, 0, 2)
    return step, cum, fresh, wide_end[0:8], spread(jnp.broadcast_to(final, (8, 128)))


def within_math(x_act, b_act, c_act, step, cum, cum_t):
    scores = dot(c_act, b_act, 1, 1)
    stepped = x_act.astype(F32) * spread(step)
    outs = []
    for e in range(HD):
        mix = (scores * gap_decay(cum, cum_t, e)).astype(BF)
        part = stepped[:, e * PS : (e + 1) * PS]
        high, low = pieces(part, 2)
        both = dot(mix, jnp.concatenate([high, low], axis=1), 1, 0)
        outs.append(both[:, :PS] + both[:, PS:])
    return jnp.concatenate(outs, axis=1)


def rim_rows(columns):
    x_rim = columns.T[0:8]
    lane = iota((8, 128), 1)
    both = jnp.zeros((8, 128), F32)
    for i in range(T // 8):
        part = pltpu.roll(columns[8 * i : 8 * i + 8], (4 * i + 4 - BASE) % 128, 1)
        both = jnp.where(lane // 4 == i, part, both)
    return jnp.concatenate([x_rim, both, pltpu.roll(both, 5, 0)], axis=1)


def spread_eight(cols):
    lane = iota(cols.shape, 1)
    out = jnp.zeros(cols.shape, F32)
    for e in range(HD):
        out = jnp.where(lane // 8 == e, jnp.broadcast_to(cols[:, e : e + 1], cols.shape), out)
    return out


def early_math(x_first, b_first, c_act, step, cum):
    lane, row = iota((T, 128), 1), iota((T, 128), 0)
    b_rows = jnp.concatenate([b_first] * HD + [jnp.zeros((128 - 8 * HD, 128), F32)], axis=0)
    scores = dot(c_act, b_rows.astype(BF), 1, 1)
    at_first = spread_eight(cum[0:8])
    at_first = jnp.sum(
        jnp.where(iota((8, 128), 0) == iota((8, 128), 1) % 8, at_first, 0.0), axis=0, keepdims=True
    )
    use = (lane % 8 < KT - 1) & (lane < 8 * HD) & (row >= lane % 8)
    gap = jnp.where(use, spread_eight(cum) - at_first, 0.0)
    mix = jnp.where(use, scores * jnp.exp(gap), 0.0).astype(BF)
    stepped = x_first * spread(step[0:8])
    blocks = jnp.concatenate([stepped] * HD + [jnp.zeros((128 - 8 * HD, CW), F32)], axis=0)
    blocks = jnp.where(iota((128, CW), 0) // 8 == iota((128, CW), 1) // PS, blocks, 0.0)
    return dot_right(mix, blocks, 1, 0)


def norm_math(mixed, gate, out_grad, gain, squares, along, c_act, cum):
    gate_act, gate_slope = silu_slope(gate)
    mixed = mixed.astype(F32)
    v = mixed * gate_act
    inv = lax.rsqrt(squares * (1.0 / (2 * CW)) + 1e-05)
    normed = v * inv
    v_grad = inv * (out_grad * gain - normed * (along * inv * (1.0 / (2 * CW))))
    y_grad = (v_grad * gate_act).astype(BF)
    gate_grad = (v_grad * mixed * gate_slope).astype(BF)
    gain_grad = jnp.sum(out_grad * normed, axis=0, keepdims=True)
    grown = spread(jnp.exp(cum))
    lifted = y_grad.astype(F32) * grown
    start_grad = dot(lifted.astype(BF), c_act, 0, 0)
    return y_grad, gate_grad, gain_grad, start_grad


def within_back_math(x_act, b_act, c_act, step, cum, cum_t, y, y_grad, carried):
    lifted = y_grad.astype(F32) * spread(jnp.exp(cum))
    scores = dot(c_act, b_act, 1, 1)
    score_grad = jnp.zeros((T, T), F32)
    x_parts = []
    step_t = step.T
    for e in range(HD):
        cut = slice(e * PS, (e + 1) * PS)
        decay = gap_decay(cum, cum_t, e)
        x_parts.append(dot((scores * decay).astype(BF), y_grad[:, cut], 0, 0))
        mix_grad = dot(y_grad[:, cut], x_act[:, cut], 1, 1)
        score_grad = score_grad + mix_grad * (decay * step_t[e : e + 1, :])
    x_in = jnp.concatenate(x_parts, axis=1)
    score_grad = score_grad.astype(BF)
    c_grad = dot(score_grad, b_act, 1, 0) + dot_both(lifted, carried, 1, 0)
    b_in = dot(score_grad, c_act, 0, 0)
    dy = y_grad.astype(F32)
    x32 = x_act.astype(F32)
    out_dots = head_sums(dy * y)
    in_dots = head_sums(x32 * x_in)
    skip_grad = jnp.sum(dy * x32, axis=0, keepdims=True)
    return x_in, b_in, c_grad, out_dots, in_dots, skip_grad


def leave_math(x_act, b_act, step, cum, shifted, logd, alog_row, skip_row, y_grad, x_in, b_in, out_dots, in_dots, carried, end_grad):
    final = cum[T - 1 : T, :]
    tail = jnp.exp(final - cum)
    x32 = x_act.astype(F32)
    end_b = end_grad.astype(BF)
    x_state = spread(tail) * dot(b_act, end_b, 1, 1)
    state_dots = head_sums(x32 * x_state, 2)
    wide_step = spread(step)
    x_grad = wide_step * (x_in + x_state) + skip_row * y_grad.astype(F32)
    weighted = (x32 * spread(tail * step)).astype(BF)
    b_grad = b_in + dot(weighted, end_b, 1, 0)
    pull = step * state_dots
    cum_grad = out_dots - step * in_dots - pull
    kept_dots = jnp.sum(carried * end_grad, axis=1, keepdims=True)
    lane = iota((1, 128), 1)
    over = jnp.zeros((1, 128), F32)
    for e in range(HD):
        over = jnp.where(lane == e, jnp.sum(kept_dots[e * PS : (e + 1) * PS, :], axis=0, keepdims=True), over)
    final_grad = jnp.sum(pull, axis=0, keepdims=True) + jnp.exp(final) * over
    triu = (iota((T, T), 0) <= iota((T, T), 1)).astype(BF)
    log_grad = sum(dot(triu, piece, 1, 0) for piece in pieces(cum_grad, 2)) + final_grad
    step_grad = in_dots + state_dots - jnp.exp(alog_row) * log_grad
    alog_grad = jnp.sum(log_grad * logd, axis=0, keepdims=True)
    live = iota((T, 128), 1) < HD
    dt_grad = jnp.where(live, step_grad * jax.nn.sigmoid(shifted), 0.0)
    bias_grad = jnp.sum(dt_grad, axis=0, keepdims=True)
    return x_grad, b_grad, dt_grad, alog_grad, bias_grad


def weight_grads(ext, pre_grad):
    return [
        jnp.sum(pre_grad * ext[ROWS - KT + 1 + k : ROWS - KT + 1 + k + T], axis=0, keepdims=True)
        for k in range(KT)
    ]


def conv_back(pre_ext, weight, lo, hi):
    total = None
    for k in range(KT):
        term = weight[k : k + 1, :] * pre_ext[KT - 1 - k : KT - 1 - k + T, lo:hi]
        total = term if total is None else total + term
    return total


def call(kernel, out_shape, in_specs, out_specs=None, scratch=(), flops=0, bytes_accessed=0, limit=VMEM_LIMIT):
    place = {
        "v": pl.BlockSpec(memory_space=pltpu.VMEM),
        "s": pl.BlockSpec(memory_space=pltpu.SMEM),
        "h": pl.BlockSpec(memory_space=pltpu.HBM),
    }
    return pl.pallas_call(
        kernel,
        out_shape=out_shape,
        in_specs=[place[c] for c in in_specs],
        out_specs=[place[c] for c in (out_specs or "v" * len(out_shape))],
        scratch_shapes=list(scratch),
        compiler_params=pltpu.CompilerParams(vmem_limit_bytes=limit),
        cost_estimate=pl.CostEstimate(
            flops=flops, bytes_accessed=bytes_accessed, transcendentals=0
        ),
    )


def sds(shape, dtype):
    return jax.ShapeDtypeStruct(shape, dtype)


def pack_kernel(
    x_at, b_at, c_at, dt_at, gate_at, grad_at, out_at, x, b, c, dt, gate, out_grad, out, sems, out_sems
):
    moves = [
        pltpu.make_async_copy(source, target, sems.at[i])
        for i, (source, target) in enumerate(
            [(dt_at, dt), (x_at, x), (gate_at, gate), (grad_at, out_grad), (b_at, b), (c_at, c)]
        )
    ]
    for move in moves:
        move.start()
    ways = out.shape[0]
    per = GROUPS * N // ways
    leaving = []

    def leave(lo, hi):
        leaving.append(
            pltpu.make_async_copy(
                out.at[:, :, lo:hi], out_at.at[:, :, lo:hi], out_sems.at[len(leaving)]
            )
        )
        leaving[-1].start()

    moves[0].wait()
    wide_dt = jnp.concatenate(
        [dt[...].astype(F32), jnp.zeros((ROWS, 128 - dt.shape[1]), F32)], axis=1
    )
    lane = iota((ROWS, 128), 1)
    for j in range(ways):
        turned = pltpu.roll(wide_dt, (128 - HD * j) % 128, 1)
        out[j, :, 1024:1152] = jnp.where(lane < HD, turned, 0.0).astype(BF)
    for i, (ref, lo) in enumerate([(x, 0), (gate, 512), (out_grad, 768)]):
        moves[i + 1].wait()
        for j in range(ways):
            out[j, :, lo : lo + CW] = ref[:, j * CW : (j + 1) * CW]
        leave(lo, IN_W if lo == 768 else lo + CW)
    for i, (ref, lo) in enumerate([(b, 256), (c, 384)]):
        moves[i + 4].wait()
        for j in range(ways):
            g = (j * per) // N
            out[j, :, lo : lo + N] = ref[:, g * N : (g + 1) * N]
    leave(256, 512)
    for move in leaving:
        move.wait()


def group_lanes(ref, where):
    return ref[:, pl.ds(pl.multiple_of(where[1] * N, N), N)]


def gain_lanes(ref, where):
    return ref[:, pl.ds(pl.multiple_of(where[0] * CW, CW), CW)]


def head_column(row):
    return jnp.concatenate(
        [jnp.broadcast_to(row[:, e : e + 1], (PS, 128)) for e in range(HD)], axis=0
    )


def enter_kernel(rows, wx, wb, head, where, step_out, cum_out, send, ext):
    ext[0:ROWS] = jnp.zeros((ROWS, 384), F32)
    ext[ROWS : ROWS + T] = rows[:, 0:384].astype(F32)
    step, cum, fresh, first_end, final = enter_math(
        ext,
        rows[:, 1024:1152].astype(F32),
        wx[...],
        group_lanes(wb, where),
        scalar_row(head, HD, 128, 1),
        scalar_row(head, 0, 128, 1),
    )
    step_out[...] = step
    cum_out[...] = cum
    count = send.shape[0]
    lane, row = iota((8, 128), 1), iota((8, 128), 0)
    first = ext[ROWS : ROWS + 8]
    end = rows[T - ROWS : T, 256:512].astype(F32)[8:16]
    last = pltpu.roll(ext[ROWS + T - 8 : ROWS + T], 6, 0)
    rim = jnp.where(iota((8, 384), 0) < 3, first, last)
    end_high = first_end.astype(BF).astype(F32)
    final_parts = [piece.astype(F32) for piece in pieces(final, 3)]
    wide_row = iota((8, CW), 0)
    ends = jnp.where(wide_row < 3, end_high, pltpu.roll(first_end - end_high, 3, 0))
    ends = jnp.where(wide_row == 6, final_parts[0], jnp.where(wide_row == 7, final_parts[1], ends))
    columns = jnp.concatenate(
        [rim[:, 0:CW], ends, final_parts[2], jnp.zeros((104, CW), F32)], axis=0
    ).T
    both = jnp.where(row < 3, pltpu.roll(end, 3, 0)[:, 0:128], pltpu.roll(end, 6, 0)[:, 128:256])
    b_rim = rim[:, 256:384]
    b_part = b_rim
    for t in range(3):
        moved = pltpu.roll(b_rim, BASE * (t + 1), 1)
        there = lane // BASE == t + 1
        b_part = jnp.where((row == 6) & there, moved[t : t + 1], b_part)
        b_part = jnp.where((row == 7) & there, moved[t + 3 : t + 4], b_part)
    tiles = []
    for i in range(count):
        part = pltpu.roll(both, (BASE - 4 - 4 * i) % 128, 1)
        tile = jnp.where(lane < BASE - 4, columns[8 * i : 8 * i + 8], part)
        tiles.append(jnp.where(lane < BASE, tile, b_part)[None])
    high = fresh.astype(BF).astype(F32)
    shape = (count, 8, 128)
    send[...] = jnp.concatenate(
        [high.reshape(shape), (fresh - high).reshape(shape), jnp.concatenate(tiles, axis=0)], axis=1
    ).astype(BF)


def conv_rows(ext, wx, wb, wc, where):
    for weight, lo, hi in (
        (wx[...], 0, 256),
        (group_lanes(wb, where), 256, 384),
        (group_lanes(wc, where), 384, 512),
    ):
        yield lo, hi, taps(ext, weight, lo, hi)


def within_kernel(rows, wx, wb, wc, where, step, cum, after, xbc, inside, ext):
    del after
    ext[0:ROWS] = jnp.zeros((ROWS, 512), F32)
    ext[ROWS : ROWS + T] = rows[:, 0:512].astype(F32)
    acts = []
    for lo, hi, pre in conv_rows(ext, wx, wb, wc, where):
        late = iota((T, hi - lo), 0) >= KT - 1
        acts.append(jnp.where(late, pre * jax.nn.sigmoid(pre), 0.0).astype(BF))
        xbc[:, lo:hi] = acts[-1]
    step, cum = step[...], cum[...]
    inside[...] = within_math(*acts, step, cum, cum.T)


def scan_kernel(received, wx, wb, where, send, decays, columns, fresh, states):
    count = received.shape[0]
    columns[...] = jnp.concatenate([wx[...], jnp.zeros((128 - KT, CW), F32)], axis=0).T
    mine = columns[pl.ds(pl.multiple_of(where[2] * 8, 8), 8), :]
    taps_b = group_lanes(wb, where)
    shape = (count, 8, 128)
    lane, row = iota(shape, 2), iota(shape, 1)
    message = received[...].astype(F32)
    x_rim = message[:, 16:24]
    low = x_rim
    for t in range(3):
        moved = pltpu.roll(x_rim, 128 - BASE * (t + 1), 2)
        low = jnp.where(row == t, moved[:, 6:7], jnp.where(row == t + 3, moved[:, 7:8], low))
    b_rim = jnp.where(lane < BASE, low, x_rim)
    blank = jnp.zeros((1, 8, 128), F32)
    x_last = jnp.concatenate([blank, x_rim[:-1]], axis=0)
    b_last = jnp.concatenate([blank, b_rim[:-1]], axis=0)
    x_seen = jnp.where(lane < 3, pltpu.roll(x_last, 125, 2), pltpu.roll(x_rim, 3, 2))
    b_seen = jnp.where(row < 3, pltpu.roll(b_last, 5, 1), pltpu.roll(b_rim, 3, 1))
    x_pre = mine[None, :, 0:1] * x_seen
    b_pre = taps_b[None, 0:1] * b_seen
    for k in range(1, KT):
        x_pre = x_pre + mine[None, :, k : k + 1] * pltpu.roll(x_seen, 128 - k, 2)
        b_pre = b_pre + taps_b[None, k : k + 1] * pltpu.roll(b_seen, 8 - k, 1)
    to_end = pltpu.roll(x_rim, 120, 2) + pltpu.roll(x_rim, 117, 2)
    x_act = (x_pre * jax.nn.sigmoid(x_pre)).astype(BF).astype(F32) * to_end
    b_act = (b_pre * jax.nn.sigmoid(b_pre)).astype(BF).astype(F32)
    total = message[:, 0:8] + message[:, 8:16]
    for t in range(KT - 1):
        total = total + x_act[:, :, t : t + 1] * b_act[:, t : t + 1, :]
    fresh[...] = total
    final = x_rim[:, :, 14:15] + x_rim[:, :, 15:16] + x_rim[:, :, 16:17]
    decays[...] = jnp.exp(jnp.broadcast_to(final, shape))
    state = jnp.zeros((8, 128), F32)
    for i in range(count):
        states[i] = state
        state = decays[i] * state + fresh[i]
    state = states[...]
    high = state.astype(BF).astype(F32)
    back = jnp.where(lane < 3, x_seen, x_last)
    send[...] = jnp.concatenate([high, state - high, back], axis=1).astype(BF)


def scan_back_kernel(received, decays, send, states):
    message = received[...].astype(F32)
    state = jnp.zeros((8, 128), F32)
    for i in reversed(range(received.shape[0])):
        states[i] = state
        state = decays[i] * state + message[i]
    send[...] = states[...].astype(BF)


def pair_rows(squares, along):
    lane = iota((T, 128), 1)
    both = jnp.where(lane == 0, squares, jnp.where(lane == 1, along, 0.0))
    return both.T[0:8, :]


def mix_kernel(
    received, xbc_late, inside, step, cum, rows, wx, wb, wc, gain, head, where,
    y_out, mixed_out, message, xbc, carried_out, rim_out,
):
    arrived = received[...].astype(F32)
    carried = (arrived[:, 0:8] + arrived[:, 8:16]).reshape(T, 128)
    carried_out[...] = carried
    rim = rim_rows(arrived[:, 16:24].reshape(T, 128))
    rim_out[...] = rim
    raw = rows[0:ROWS, 0:512].astype(F32)[0:8]
    seen = jnp.where(iota((8, 512), 0) < 3, rim, pltpu.roll(raw, 3, 0))
    weights = jnp.concatenate([wx[...], group_lanes(wb, where), group_lanes(wc, where)], axis=1)
    pre = weights[0:1] * seen
    for k in range(1, KT):
        pre = pre + weights[k : k + 1] * pltpu.roll(seen, 8 - k, 0)
    first = jnp.where(iota((8, 512), 0) < 3, pre * jax.nn.sigmoid(pre), 0.0).astype(BF).astype(F32)
    late = xbc_late[...]
    whole = jnp.concatenate([(late[0:ROWS].astype(F32) + jnp.concatenate([first, jnp.zeros((8, 512), F32)], axis=0)).astype(BF), late[ROWS:T]], axis=0)
    xbc[...] = whole
    x_act, c_act = whole[:, 0:256], whole[:, 384:512]
    cum = cum[...]
    early = early_math(first[:, 0:256], first[:, 256:384], c_act, step[...], cum)
    grown = spread(jnp.exp(cum))
    y = inside[...] + early + grown * dot_right(c_act, carried, 1, 1)
    mixed = (y + scalar_row(head, 2 * HD, CW, PS) * x_act.astype(F32)).astype(BF)
    gate = rows[:, 512:768].astype(F32)
    v = mixed.astype(F32) * (gate * jax.nn.sigmoid(gate))
    scaled = rows[:, 768:1024].astype(F32) * gain_lanes(gain, where)
    y_out[...] = y
    mixed_out[...] = mixed
    message[...] = pair_rows(
        jnp.sum(v * v, axis=1, keepdims=True), jnp.sum(scaled * v, axis=1, keepdims=True)
    )


def norm_kernel(message, mixed, rows, gain, xbc, cum, where, y_grad_out, gate_out, gain_out, send):
    sums = jnp.concatenate([message[...], jnp.zeros((120, T), F32)], axis=0).T
    y_grad, gate_grad, gain_grad, start_grad = norm_math(
        mixed[...],
        rows[:, 512:768].astype(F32),
        rows[:, 768:1024].astype(F32),
        gain_lanes(gain, where),
        sums[:, 0:1],
        sums[:, 1:2],
        xbc[:, 384:512],
        cum[...],
    )
    y_grad_out[...] = y_grad
    gate_out[...] = gate_grad
    gain_out[...] = jnp.broadcast_to(gain_grad, (8, CW))
    send[...] = start_grad.reshape(send.shape).astype(BF)


def place_rim(ext, rim):
    ext[0:8] = jnp.zeros((8, ext.shape[1]), F32)
    ext[8:ROWS] = pltpu.roll(rim, 5, 0)


def back_kernel(
    rows, rim, wx, wb, wc, where, xbc, step, cum, y, y_grad, carried, middle, dots, slopes, ext
):
    place_rim(ext, rim[...])
    ext[ROWS : ROWS + T] = rows[:, 0:512].astype(F32)
    for lo, hi, pre in conv_rows(ext, wx, wb, wc, where):
        slopes[:, lo:hi] = silu_slope(pre)[1]
    cum = cum[...]
    x_in, b_in, c_grad, out_dots, in_dots, skip_grad = within_back_math(
        xbc[:, 0:256],
        xbc[:, 256:384],
        xbc[:, 384:512],
        step[...],
        cum,
        cum.T,
        y[...],
        y_grad[...],
        carried[...],
    )
    middle[:, 0:256] = x_in
    middle[:, 256:384] = b_in
    middle[:, 384:512] = c_grad
    dots[0:T] = out_dots + pltpu.roll(in_dots, 64, 1)
    dots[T : T + 8] = head_sums(jnp.broadcast_to(skip_grad, (8, CW)))


def leave_kernel(
    end_grad, rows, rim, head, xbc, step, cum, y_grad, middle, dots, carried, gain_grad, slopes,
    pre_out, dt_out, send, ext,
):
    place_rim(ext, rim[...])
    ext[ROWS : ROWS + T] = rows[:, 0:512].astype(F32)
    alog_row = scalar_row(head, 0, 128, 1)
    step = step[...]
    both = dots[0:T]
    live = iota((T, 128), 1) < HD
    x_grad, b_grad, dt_grad, alog_grad, bias_grad = leave_math(
        xbc[:, 0:256],
        xbc[:, 256:384],
        step,
        cum[...],
        rows[:, 1024:1152].astype(F32) + scalar_row(head, HD, 128, 1),
        -jnp.exp(alog_row) * step,
        alog_row,
        scalar_row(head, 2 * HD, CW, PS),
        y_grad[...],
        middle[:, 0:256],
        middle[:, 256:384],
        jnp.where(live, both, 0.0),
        jnp.where(live, pltpu.roll(both, 64, 1), 0.0),
        carried[...],
        end_grad[...].astype(F32),
    )
    dt_out[...] = dt_grad
    pre = jnp.concatenate([x_grad, b_grad, middle[:, 384:512]], axis=1) * slopes[...]
    pre_out[...] = pre
    weights = jnp.concatenate(weight_grads(ext, pre), axis=0)
    sums = jnp.concatenate([alog_grad, bias_grad, dots[T : T + 1], jnp.zeros((5, 128), F32)], axis=0)
    line = sums[0:1] + pltpu.roll(sums, 32, 1)[1:2] + pltpu.roll(sums, 64, 1)[2:3]
    coarse = line.astype(BF).astype(F32)
    block = jnp.concatenate(
        [weights[:, i * 128 : (i + 1) * 128] for i in range(4)]
        + [gain_grad[0:1, 0:128], gain_grad[0:1, 128:256], coarse, line - coarse]
        + [pre[0:3, i * 128 : (i + 1) * 128] for i in range(4)],
        axis=0,
    ).astype(BF)
    for i in range(send.shape[0]):
        send[i] = block


def finish_kernel(received, where, wx, wb, wc, pre, dt_grad, gate_grad, send, total_out, ext):
    count = received.shape[0]
    total = received[0].astype(F32)
    for i in range(1, count):
        total = total + received[i].astype(F32)
    total_out[...] = total
    after = where[2] + 1
    next_block = received[jnp.minimum(after, count - 1)].astype(F32)
    following = jnp.concatenate(
        [next_block[20 + 3 * i : 23 + 3 * i] for i in range(4)], axis=1
    )
    ext[0:T] = pre[...]
    ext[T : T + 3] = jnp.where(after < count, following, 0.0)
    x_grad = conv_back(ext, wx[...], 0, 256).astype(BF)
    b_grad = conv_back(ext, group_lanes(wb, where), 256, 384).astype(BF)
    c_grad = conv_back(ext, group_lanes(wc, where), 384, 512).astype(BF)
    dt_low = dt_grad[...].astype(BF)
    lane, row = iota((128, 128), 1), iota((128, 128), 0)
    apart = dot(dt_low, ((lane // ROWS == row) & (row < HD)).astype(BF), 1, 0)
    apart = jnp.where(iota((T, 128), 0) % ROWS == iota((T, 128), 1) % ROWS, apart, 0.0).astype(BF)
    ways = send.shape[0]
    joined = dot((iota((ways, T), 1) // ROWS == iota((ways, T), 0)).astype(BF), apart, 1, 0)
    shared = jnp.concatenate([total[8:18], jnp.zeros((6, 128), F32)], axis=0)
    row = iota((ROWS, 128), 0)
    for j in range(ways):
        cut = slice(j * ROWS, (j + 1) * ROWS)
        send[j, :, 0:256] = x_grad[cut]
        send[j, :, 256:384] = b_grad[cut]
        send[j, :, 384:512] = c_grad[cut]
        send[j, :, 512:768] = gate_grad[cut, :]
        send[j, :, 768:896] = jnp.where(row == 10, joined[j : j + 1], shared).astype(BF)


def unpack_kernel(
    received, total, x_out, b_out, c_out, dt_out, gate_out, conv_x_out, conv_b_out, conv_c_out,
    alog_out, bias_out, skip_out, gain_out,
):
    line = total[18:19] + total[19:20]
    conv_x_out[...] = jnp.concatenate([total[0:4], total[4:8]], axis=1)
    for e in range(HD):
        alog_out[e] = jnp.sum(line[:, e : e + 1])
        bias_out[e] = jnp.sum(line[:, 32 + e : 33 + e])
        skip_out[e] = jnp.sum(line[:, 64 + e : 65 + e])
    ways = received.shape[0]
    shared, lines = [], []
    for j in range(ways):
        own = slice(j * CW, (j + 1) * CW)
        x_out[:, own] = received[j, :, 0:256]
        gate_out[:, own] = received[j, :, 512:768]
        shared.append(received[j, :, 768:896].astype(F32))
        lines.append(shared[j][10:11])
        gain_out[:, own] = jnp.concatenate([shared[j][8:9], shared[j][9:10]], axis=1)
    lines = jnp.concatenate(lines, axis=0)
    heads = dt_out.shape[1]
    dt = jnp.zeros((ROWS, heads), F32)
    for e in range(HD):
        place = (iota((ways, heads), 1) == HD * iota((ways, heads), 0) + e).astype(BF)
        dt = dt + dot(lines[:, e * ROWS : (e + 1) * ROWS].astype(BF), place, 0, 0)
    dt_out[...] = dt.astype(BF)
    per = ways // GROUPS
    for g in range(GROUPS):
        cut = slice(g * N, (g + 1) * N)
        b_sum, c_sum, w_sum = 0.0, 0.0, 0.0
        for j in range(g * per, (g + 1) * per):
            b_sum = b_sum + received[j, :, 256:384].astype(F32)
            c_sum = c_sum + received[j, :, 384:512].astype(F32)
            w_sum = w_sum + shared[j]
        b_out[:, cut] = b_sum.astype(BF)
        c_out[:, cut] = c_sum.astype(BF)
        conv_b_out[:, cut] = w_sum[0:KT]
        conv_c_out[:, cut] = w_sum[KT : 2 * KT]


def per_device(
    x_in, b_in, c_in, dt_in, gate_in, out_grad, conv_x, conv_b, conv_c, a_log, dt_bias, d_skip, norm_gain
):
    ways = lax.axis_size("head")
    blocks = lax.axis_size("ctx")
    head_at = lax.axis_index("head")
    where = jnp.stack([head_at, (head_at * GROUPS) // ways, lax.axis_index("ctx")]).astype(jnp.int32)
    head = jnp.concatenate([a_log, dt_bias, d_skip])
    gain = norm_gain.reshape(1, -1)

    def ctx_swap(value):
        return lax.all_to_all(value, "ctx", 0, 0, tiled=True)

    def head_swap(value):
        return lax.all_to_all(value, "head", 0, 0, tiled=True)

    inputs = (x_in, b_in, c_in, dt_in, gate_in, out_grad)
    sent = call(
        pack_kernel,
        [sds((ways, ROWS, IN_W), BF)],
        "hhhhhh",
        "h",
        scratch=[pltpu.VMEM(a.shape, a.dtype) for a in (x_in, b_in, c_in, dt_in, gate_in, out_grad)]
        + [pltpu.VMEM((ways, ROWS, IN_W), BF)]
        + [pltpu.SemaphoreType.DMA((6,)), pltpu.SemaphoreType.DMA((4,))],
        limit=PACK_LIMIT,
    )(*inputs)[0]
    arrived = head_swap(sent)
    rows = arrived.reshape(T, IN_W)
    wide = sds((T, CW), F32)
    slim = sds((T, 128), F32)
    chunk = sds((blocks, T // blocks, 128), F32)
    half_chunk = sds((blocks, T // blocks, 128), BF)
    ext = pltpu.VMEM((ROWS + T, 512), F32)

    step, cum, send = call(
        enter_kernel,
        [slim, slim, sds((blocks, 24, 128), BF)],
        "vvvss",
        scratch=[pltpu.VMEM((ROWS + T, 384), F32)],
    )(rows, conv_x, conv_b, head, where)
    received = ctx_swap(send)
    send, decays = call(
        scan_kernel,
        [sds((blocks, 24, 128), BF), chunk],
        "vvvs",
        scratch=[pltpu.VMEM((CW, 128), F32)] + [pltpu.VMEM((blocks, 8, 128), F32)] * 2,
    )(received, conv_x, conv_b, where)
    received = ctx_swap(send)
    xbc, inside = call(
        within_kernel,
        [sds((T, 512), BF), wide],
        "vvvvsvvv",
        scratch=[ext],
        flops=10**8,
        bytes_accessed=3 * 10**6,
    )(rows, conv_x, conv_b, conv_c, where, step, cum, decays)
    y, mixed, sums, xbc, carried, rim = call(
        mix_kernel,
        [wide, sds((T, CW), BF), sds((8, T), F32), sds((T, 512), BF), slim, sds((8, 512), F32)],
        "vvvvvvvvvvss",
    )(received, xbc, inside, step, cum, rows, conv_x, conv_b, conv_c, gain, head, where)
    per = ways // GROUPS
    sums = lax.psum(
        sums, "head", axis_index_groups=[[g * per + i for i in range(per)] for g in range(GROUPS)]
    )
    y_grad, gate_grad, gain_grad, send = call(
        norm_kernel,
        [sds((T, CW), BF), sds((T, CW), BF), sds((8, CW), F32), half_chunk],
        "vvvvvvs",
    )(sums, mixed, rows, gain, xbc, cum, where)
    received = ctx_swap(send)
    middle, dots, slopes = call(
        back_kernel,
        [sds((T, 512), F32), sds((T + 8, 128), F32), sds((T, 512), F32)],
        "vvvvvsvvvvvv",
        scratch=[ext],
        flops=3 * 10**8,
        bytes_accessed=4 * 10**6,
    )(rows, rim, conv_x, conv_b, conv_c, where, xbc, step, cum, y, y_grad, carried)
    send = call(
        scan_back_kernel, [half_chunk], "vv", scratch=[pltpu.VMEM((blocks, 8, 128), F32)]
    )(received, decays)[0]
    end_grad = ctx_swap(send).reshape(T, 128)
    pre, dt_grad, send = call(
        leave_kernel,
        [sds((T, 512), F32), slim, sds((blocks, 32, 128), BF)],
        "vvvs" + "v" * 9,
        scratch=[ext],
    )(
        end_grad, rows, rim, head, xbc, step, cum, y_grad, middle, dots, carried, gain_grad, slopes,
    )
    received = ctx_swap(send)
    send, total = call(
        finish_kernel,
        [sds((ways, ROWS, OUT_W), BF), sds((32, 128), F32)],
        "vsvvvvvv",
        scratch=[pltpu.VMEM((T + 8, 512), F32)],
    )(received, where, conv_x, conv_b, conv_c, pre, dt_grad, gate_grad)
    received = head_swap(send)
    four = sds((HD,), F32)
    *grads, gain_sum = call(
        unpack_kernel,
        [
            sds(x_in.shape, BF),
            sds(b_in.shape, BF),
            sds(c_in.shape, BF),
            sds(dt_in.shape, BF),
            sds(gate_in.shape, BF),
            sds(conv_x.shape, F32),
            sds(conv_b.shape, F32),
            sds(conv_c.shape, F32),
            four,
            four,
            four,
            sds((1, norm_gain.shape[0]), F32),
        ],
        "vv",
        "vvvvvvvvsssv",
    )(received, total)
    return (*grads, gain_sum.reshape(-1))


def solution(mesh):
    tokens = P(("ctx", "head"), None)
    return jax.shard_map(
        per_device,
        mesh=mesh,
        in_specs=(tokens,) * 6 + (P(None, "head"), P(), P(), P("head"), P("head"), P("head"), P()),
        out_specs=(tokens,) * 5
        + (P(None, "head"), P(), P(), P("head"), P("head"), P("head"), P()),
        check_vma=False,
    )
```
